128 devices in a mesh: vtx: 32 (over z, x, core), feat: 4 (over y).
Axes of the slice: x: 4, y: 4, z: 4, core: 2. Of those that a mesh axis runs over, the one named last changes fastest.
Arguments:
- features: bfloat16 [131072, 768], P('vtx', 'feat'), may hold values from -6 to 6
- w_self: bfloat16 [768, 256], P('feat'), may hold values from -0.21875 to 0.21875
- w_neigh: bfloat16 [768, 256], P('feat'), may hold values from -0.21875 to 0.21875
- bias_terms: float32 [256], P('feat'), may hold values from -3 to 3
- block_vals: bfloat16 [10240, 128, 128], P('vtx'), may hold values from 0 to 1
- block_rows: int32 [10240], P('vtx'), may hold values from 0 to 31, as said below
- block_cols: int32 [10240], P('vtx'), may hold values from 0 to 63, as said below
- block_count: int32 [32], P('vtx'), may hold values from 1 to 320, as said below
- recv_lists: int32 [1024], P('vtx'), may hold values from -1 to 31, as said below
- degree: int32 [131072], P('vtx'), may hold values from 8 to 63
- cotangent: bfloat16 [131072, 256], P('vtx', 'feat'), may hold values from -6 to 6
Outputs:
- hidden: bfloat16 [131072, 256], P('vtx', 'feat')
- grad_features: bfloat16 [131072, 768], P('vtx', 'feat')
- grad_self: float32 [768, 256], P('feat')
- grad_neigh: float32 [768, 256], P('feat')
The draws below stay inside these ranges and needn't reach their ends.
Inputs may be any that keep to these rules, and one draw needn't show every extreme that they name: Entry e of a shard's list adds into the shard's own row block block_rows[e]. `block_cols`: an index into the shard's extended list: 16 left slots, its 32 own blocks, 16 right slots. `block_count`: the live entries of a shard's list come first and entries past its count are ignored; some shard has all 320 entries live. `recv_lists`: per shard 2 * 16 slots: distinct blocks of the left neighbour, then distinct blocks of the right neighbour; live slots come first, the others and all slots toward a missing neighbour are -1; some shard has 16 live right slots.
All inputs are finite; a program needn't handle non-finite values.
Results may differ from the reference program's by a relative error of at most 0.0053.
Values may be sent and summed in bfloat16 or wider, within the bound.
A program may use at most 192 MiB of HBM per device.

```python
import jax
import jax.numpy as jnp
from jax import lax

F_IN = 768
HID = 256
BS = 128
NB_DEV = 32
HALO = 16
NNZ = 320
NBLK = 1024
NODES = 131072
SLOTS = 10240


def layout(key):
    shards = NBLK // NB_DEV
    subkeys = jax.random.split(key, 10)
    counts = jax.random.randint(subkeys[0], (shards, 2), 1, HALO + 1)
    forced = jax.random.randint(subkeys[1], (), 1, shards)
    counts = counts.at[forced, 0].set(HALO)
    orders = jax.vmap(lambda subkey: jax.random.permutation(subkey, NB_DEV))(jax.random.split(subkeys[2], shards * 2))
    orders = orders.reshape(shards, 2, NB_DEV)[:, :, :HALO].astype(jnp.int32)
    slot_index = jnp.arange(HALO, dtype=jnp.int32)
    outgoing = jnp.where(slot_index[None, None, :] < counts[:, :, None], orders, -1)
    vacant = jnp.full((1, HALO), -1, jnp.int32)
    from_left = jnp.concatenate([vacant, outgoing[:-1, 1]], axis=0)
    from_right = jnp.concatenate([outgoing[1:, 0], vacant], axis=0)
    nothing = jnp.zeros((1,), jnp.int32)
    left_count = jnp.concatenate([nothing, counts[:-1, 1]])
    right_count = jnp.concatenate([counts[1:, 0], nothing])
    wanted = jnp.concatenate([from_left, from_right], axis=1)
    anchor = jax.random.randint(subkeys[3], (shards, NNZ), 0, 4)
    anchor = jnp.where((anchor == 0) & (left_count[:, None] == 0), 2, anchor)
    anchor = jnp.where((anchor == 1) & (right_count[:, None] == 0), 3, anchor)
    choose = jax.random.randint(subkeys[4], (shards, NNZ), 0, 1 << 20)
    left_slot = choose % jnp.maximum(left_count, 1)[:, None]
    right_slot = choose % jnp.maximum(right_count, 1)[:, None]
    home_pick = jax.random.randint(subkeys[5], (shards, NNZ), 0, NB_DEV)
    columns = jnp.where(anchor == 0, left_slot, jnp.where(anchor == 1, HALO + NB_DEV + right_slot, HALO + home_pick))
    targets = jax.random.randint(subkeys[6], (shards, NNZ), 0, NB_DEV)
    factor_one = jax.random.randint(subkeys[7], (shards,), 1, NNZ + 1)
    factor_two = jax.random.randint(subkeys[8], (shards,), 1, NNZ + 1)
    active = jnp.maximum(factor_one * factor_two // NNZ, 1)
    busiest = jax.random.randint(subkeys[9], (), 0, shards)
    active = active.at[busiest].set(NNZ)
    return (targets.reshape(-1).astype(jnp.int32), columns.reshape(-1).astype(jnp.int32), active.astype(jnp.int32), wanted.reshape(-1).astype(jnp.int32))


def draw_block_rows(key, part):
    return layout(key)[0]


def draw_block_cols(key, part):
    return layout(key)[1]


def draw_block_count(key, part):
    return layout(key)[2]


def draw_recv_lists(key, part):
    return layout(key)[3]


def set_ends(array, stream_key, smallest, largest):
    spot = [jax.random.randint(jax.random.fold_in(stream_key, axis), (), 0, length) for axis, length in enumerate(array.shape)]
    longest = array.shape.index(max(array.shape))
    beside = spot[:longest] + [(spot[longest] + 1) % array.shape[longest]] + spot[longest + 1:]
    return array.at[tuple(spot)].set(smallest).at[tuple(beside)].set(largest)


def level_of(stream_key, dims, cuts, least, high):
    gain, own = 1.0, jax.random.fold_in(stream_key, 6)
    for axis_at, shards_of in cuts:
        steps = jnp.exp(jax.random.uniform(jax.random.fold_in(own, axis_at), (shards_of,), jnp.float32, least / len(cuts), high / len(cuts)))
        gain = gain * jnp.repeat(steps, dims[axis_at] // shards_of).reshape([-1 if axis == axis_at else 1 for axis in range(len(dims))])
    return gain


def bell_draw(key, extent, scale, reach, cuts=(), held_as=jnp.bfloat16):
    result = scale * jax.random.normal(key, extent, jnp.float32)
    if cuts:
        result = result * level_of(key, extent, cuts, -0.22, 0.18)
    return jnp.clip(result, -reach, reach).astype(held_as)


def setup_inputs(seed: int = 0) -> dict:
    keys = jax.random.split(jax.random.key(seed), 12)
    return {
        "features": bell_draw(keys[0], (NODES, F_IN), 1.0, 6.0, ((0, 32), (1, 4))),
        "w_self": bell_draw(keys[1], (F_IN, HID), F_IN ** -0.5, 0.21875, ((0, 4),)),
        "w_neigh": bell_draw(keys[2], (F_IN, HID), F_IN ** -0.5, 0.21875, ((0, 4),)),
        "bias_terms": bell_draw(keys[3], (HID,), 0.5, 3.0, ((0, 4),), jnp.float32),
        "block_vals": jnp.clip(1.0 * jax.random.uniform(keys[4], (SLOTS, BS, BS), jnp.float32) ** level_of(keys[4], (SLOTS, BS, BS), ((0, 32),), -0.2, 0.2), 0.0, 1.0).astype(jnp.bfloat16),
        "block_rows": draw_block_rows(jax.random.fold_in(keys[11], 71), 0),
        "block_cols": draw_block_cols(jax.random.fold_in(keys[11], 71), 0),
        "block_count": draw_block_count(jax.random.fold_in(keys[11], 71), 0),
        "recv_lists": draw_recv_lists(jax.random.fold_in(keys[11], 71), 0),
        "degree": set_ends(jax.random.randint(keys[9], (NODES,), 8, 64), jax.random.fold_in(keys[9], 1), 8, 63).astype(jnp.int32),
        "cotangent": bell_draw(keys[10], (NODES, HID), 1.0, 6.0, ((0, 32), (1, 4))),
    }


def select_blocks(source, wanted):
    picked = source[jnp.clip(wanted, 0)]
    return jnp.where((wanted >= 0)[:, None, None], picked, jnp.zeros_like(picked))


def spread_blocks(target, wanted, incoming):
    kept = jnp.where((wanted >= 0)[:, None, None], incoming, jnp.zeros_like(incoming))
    return target.at[jnp.clip(wanted, 0)].add(kept)


def reference(features, w_self, w_neigh, bias_terms, block_vals, block_rows, block_cols, block_count, recv_lists, degree, cotangent):
    shards = NBLK // NB_DEV
    row_total = features.shape[0]
    blocks = features.reshape(shards, NB_DEV, BS, F_IN)
    border = jnp.zeros((1, NB_DEV, BS, F_IN), features.dtype)
    padded = jnp.concatenate([border, blocks, border], axis=0)
    active = jnp.arange(NNZ, dtype=jnp.int32)[None, :] < block_count[:, None]
    matrices = block_vals.reshape(shards, NNZ, BS, BS)
    matrices = jnp.where(active[:, :, None, None], matrices, jnp.zeros_like(matrices))
    targets = block_rows.reshape(shards, NNZ)
    sources = block_cols.reshape(shards, NNZ)
    wanted = recv_lists.reshape(shards, 2 * HALO)
    divisor = degree.astype(jnp.float32)[:, None]
    divisor_blocks = divisor.reshape(shards, NB_DEV * BS, 1)

    def forward_shard(shard):
        nearby = lax.dynamic_slice_in_dim(padded, shard, 3, 0)
        requested = wanted[shard]
        extended = jnp.concatenate([select_blocks(nearby[0], requested[:HALO]), nearby[1], select_blocks(nearby[2], requested[HALO:])], axis=0)
        operand = extended[sources[shard]].astype(jnp.float32)
        products = jnp.einsum("nij,njf->nif", matrices[shard].astype(jnp.float32), operand)
        summed = jnp.zeros((NB_DEV, BS, F_IN), jnp.float32).at[targets[shard]].add(products)
        return (summed.reshape(NB_DEV * BS, F_IN) / divisor_blocks[shard]).astype(jnp.bfloat16)

    neighbour_mean = lax.map(forward_shard, jnp.arange(shards, dtype=jnp.int32)).reshape(row_total, F_IN)
    preact = jnp.dot(features, w_self, preferred_element_type=jnp.float32) + jnp.dot(neighbour_mean, w_neigh, preferred_element_type=jnp.float32) + bias_terms[None, :]
    squash = jax.nn.sigmoid(preact)
    hidden = (preact * squash).astype(jnp.bfloat16)
    slopes = (cotangent.astype(jnp.float32) * squash * (1.0 + preact * (1.0 - squash))).astype(jnp.bfloat16)
    factor = float(NODES) ** -0.5
    grad_self = jnp.dot(features.T, slopes, preferred_element_type=jnp.float32) * factor
    grad_neigh = jnp.dot(neighbour_mean.T, slopes, preferred_element_type=jnp.float32) * factor
    direct = jnp.dot(slopes, w_self.T, preferred_element_type=jnp.float32)
    back_mean = (jnp.dot(slopes, w_neigh.T, preferred_element_type=jnp.float32) / divisor).astype(jnp.bfloat16)
    back_mean = back_mean.reshape(shards, NB_DEV, BS, F_IN)

    def backward_shard(running, shard):
        source = back_mean[shard][targets[shard]].astype(jnp.float32)
        products = jnp.einsum("nji,njf->nif", matrices[shard].astype(jnp.float32), source)
        spread = jnp.zeros((NB_DEV + 2 * HALO, BS, F_IN), jnp.float32).at[sources[shard]].add(products)
        requested = wanted[shard]
        vacant = jnp.zeros((NB_DEV, BS, F_IN), jnp.float32)
        toward_left = spread_blocks(vacant, requested[:HALO], spread[:HALO])
        toward_right = spread_blocks(vacant, requested[HALO:], spread[HALO + NB_DEV:])
        update = jnp.stack([toward_left, spread[HALO:HALO + NB_DEV], toward_right])
        window = lax.dynamic_slice_in_dim(running, shard, 3, 0) + update
        return lax.dynamic_update_slice_in_dim(running, window, shard, 0), None

    start = jnp.zeros((shards + 2, NB_DEV, BS, F_IN), jnp.float32)
    running, unused = lax.scan(backward_shard, start, jnp.arange(shards, dtype=jnp.int32))
    grad_features = (direct + running[1:shards + 1].reshape(row_total, F_IN)).astype(jnp.bfloat16)
    return hidden, grad_features, grad_self, grad_neigh
```

```python
import functools

import jax
import jax.numpy as jnp
from jax import lax
from jax.experimental import pallas as pl
from jax.experimental.pallas import tpu as pltpu
from jax.sharding import PartitionSpec as P

MESH = pl.DeviceIdType.MESH
F32, BF16, I32 = jnp.float32, jnp.bfloat16, jnp.int32
BS = 128
NB = 32
HALO = 16
NNZ = 320
EXT = NB + 2 * HALO
FC = 192
HID = 256
HC = 64
ROWS = NB * BS
NV, NF = 32, 4
ENT = 384
PIECES = 8
PW = ROWS // PIECES
MB = 1 << 20


def vmem():
    return pl.BlockSpec(memory_space=pltpu.VMEM)


def smem():
    return pl.BlockSpec(memory_space=pltpu.SMEM)


def anyspace():
    return pl.BlockSpec(memory_space=pl.ANY)


def greet(peers):
    barrier = pltpu.get_barrier_semaphore()
    for peer in peers:
        pl.semaphore_signal(barrier, inc=1, device_id=peer, device_id_type=MESH)
    pl.semaphore_wait(barrier, len(peers))


def iota(shape, dim):
    return lax.broadcasted_iota(I32, shape, dim).astype(F32)


def as_column(row):
    n = row.shape[1]
    diagonal = iota((n, n), 0) == iota((n, n), 1)
    return jnp.sum(jnp.where(diagonal, row, 0.0), axis=1, keepdims=True)


def pair_schedule(key, other, active):
    far = 1000.0
    sub, lane = iota((ENT, ENT), 0), iota((ENT, ENT), 1)
    key = jnp.where(active, key, far)
    key_col = as_column(key)
    rank = jnp.sum(jnp.where((key_col == key) & (sub < lane), 1.0, 0.0), axis=0, keepdims=True)
    group = iota((EXT, ENT), 0)
    size = jnp.sum(jnp.where(group == key, 1.0, 0.0), axis=1, keepdims=True)
    size = 2.0 * jnp.floor((size + 1.0) * 0.5)
    start = jnp.sum(jnp.where(group < key, size, 0.0), axis=0, keepdims=True)
    slot = jnp.where(active, start + rank, far)
    slot_col = as_column(slot)
    hit = slot_col == lane

    def at_slots(column, default):
        return jnp.sum(jnp.where(hit, column - default, 0.0), axis=0, keepdims=True) + default

    entry = at_slots(sub[:, :1], float(NNZ))
    source = at_slots(as_column(other), 0.0)
    target = at_slots(key_col, float(EXT))
    used = jnp.broadcast_to(jnp.sum(size, axis=0, keepdims=True), (1, ENT))
    return entry, source, target, used


def halo_kernel(table_ref, lists_ref, feat_ref, halo_ref, plan_ref, lists_in, lists_sm, blocks, sent, sm_sem, ls, lr, bs, br):
    me = lax.axis_index("vtx")
    right, left = lax.rem(me + 1, NV), lax.rem(me + NV - 1, NV)
    greet([{"vtx": left}, {"vtx": right}])
    trips = []
    for k, peer in ((0, right), (1, left)):
        trip = pltpu.make_async_remote_copy(
            src_ref=lists_ref, dst_ref=lists_in.at[k], send_sem=ls.at[k], recv_sem=lr.at[k],
            device_id={"vtx": peer}, device_id_type=MESH,
        )
        trip.start()
        trips.append(trip)
    blocks[0] = jnp.zeros((FC, BS), BF16)
    for b in range(NB):
        blocks[1 + b] = feat_ref[:, b * BS : (b + 1) * BS]
    for trip in trips:
        trip.wait()
    local = pltpu.make_async_copy(lists_in, lists_sm, sm_sem)
    local.start()
    local.wait()
    sends = []
    for part in range(4):
        for d in range(2):
            for j in range(4 * part, 4 * part + 4):
                sent[d, j] = blocks[lists_sm[1 - d, 0, j + HALO * d] + 1]
            trip = pltpu.make_async_remote_copy(
                src_ref=sent.at[d, pl.ds(4 * part, 4)], dst_ref=halo_ref.at[d, pl.ds(4 * part, 4)],
                send_sem=bs.at[d, part], recv_sem=br.at[d, part],
                device_id={"vtx": right if d == 0 else left}, device_id_type=MESH,
            )
            trip.start()
            sends.append(trip)
    table = table_ref[...].astype(F32)
    rows, cols, count = table[0:1], table[1:2], table[2:3]
    active = iota((1, ENT), 1) < count
    forward = pair_schedule(rows, cols, active)
    backward = pair_schedule(cols, rows, active)

    def inverse(lists, first):
        ours = as_column(lists)
        sub, lane = iota((BS, BS), 0), iota((BS, BS), 1)
        hit = (ours == lane) & (sub >= first) & (sub < first + HALO)
        return jnp.sum(jnp.where(hit, sub - (first + HALO), 0.0), axis=0, keepdims=True) + float(HALO)

    from_right = inverse(lists_in[1, 0:1].astype(F32), 0)
    from_left = inverse(lists_in[0, 0:1].astype(F32), HALO)
    last = jnp.concatenate([from_right, from_left, jnp.zeros((1, BS), F32)], axis=1)
    used = jnp.where(iota((1, ENT), 1) < 192.0, forward[3], backward[3])
    plan = forward[:3] + backward[:3] + (last, used)
    for k, row in enumerate(plan):
        plan_ref[k : k + 1] = row.astype(I32)
    for trip in sends:
        trip.wait()


def halo_call(table, lists, feat):
    return pl.pallas_call(
        halo_kernel,
        out_shape=(
            jax.ShapeDtypeStruct((2, HALO, FC, BS), BF16),
            jax.ShapeDtypeStruct((8, ENT), I32),
        ),
        in_specs=[vmem()] * 3,
        out_specs=(anyspace(), vmem()),
        scratch_shapes=[
            pltpu.VMEM((2, 8, BS), I32),
            pltpu.SMEM((2, 8, BS), I32),
            pltpu.VMEM((NB + 1, FC, BS), BF16),
            pltpu.VMEM((2, HALO, FC, BS), BF16),
            pltpu.SemaphoreType.DMA,
            pltpu.SemaphoreType.DMA((2,)),
            pltpu.SemaphoreType.DMA((2,)),
            pltpu.SemaphoreType.DMA((2, 4)),
            pltpu.SemaphoreType.DMA((2, 4)),
        ],
        compiler_params=pltpu.CompilerParams(collective_id=0, has_side_effects=True, vmem_limit_bytes=48 * MB),
        name="halo_out",
    )(table, lists, feat)


GROUP = 8


def load_vals(vals_hbm, vals, sems):
    share = NNZ // 8
    loads = [
        pltpu.make_async_copy(vals_hbm.at[pl.ds(k * share, share)], vals.at[pl.ds(k * share, share)], sems.at[k])
        for k in range(8)
    ]
    for load in loads:
        load.start()
    vals[NNZ] = jnp.zeros((BS, BS), BF16)
    return loads


def forward_kernel(plan, vals_hbm, feat_ref, halo_ref, degree_ref, mean_ref, vals, ext, acc, sems):
    loads = load_vals(vals_hbm, vals, sems)
    for j in range(HALO):
        ext[j] = halo_ref[0, j]
        ext[HALO + NB + j] = halo_ref[1, j]
    for b in range(NB):
        ext[HALO + b] = feat_ref[:, b * BS : (b + 1) * BS]
    acc[...] = jnp.zeros_like(acc)
    for load in loads:
        load.wait()

    @pl.loop(0, (plan[7, 0] + 2 * GROUP - 1) // (2 * GROUP))
    def _(step):
        for u in range(GROUP):
            slot = step * (2 * GROUP) + 2 * u
            a = jnp.concatenate([vals[plan[0, slot]], vals[plan[0, slot + 1]]], axis=1)
            x = jnp.concatenate([ext[plan[1, slot]], ext[plan[1, slot + 1]]], axis=1)
            row = jnp.minimum(plan[2, slot], NB)
            acc[row] += lax.dot_general(x, a, (((1,), (1,)), ((), ())), preferred_element_type=F32)

    for b in range(NB):
        divisor = degree_ref[b : b + 1, :].astype(F32)
        mean_ref[:, b * BS : (b + 1) * BS] = (acc[b] / divisor).astype(BF16)


def forward_call(plan, vals, feat, halo, degree):
    return pl.pallas_call(
        forward_kernel,
        out_shape=jax.ShapeDtypeStruct((FC, ROWS), BF16),
        in_specs=[smem(), anyspace(), vmem(), vmem(), vmem()],
        out_specs=vmem(),
        scratch_shapes=[
            pltpu.VMEM((NNZ + 1, BS, BS), BF16),
            pltpu.VMEM((EXT, FC, BS), BF16),
            pltpu.VMEM((NB + 1, FC, BS), F32),
            pltpu.SemaphoreType.DMA((8,)),
        ],
        compiler_params=pltpu.CompilerParams(vmem_limit_bytes=48 * MB),
        name="sparse_forward",
    )(plan, vals, feat, halo, degree)


def dense_kernel(
    feat_ref, mean_ref, cot_ref, ws_ref, wn_ref, wst_ref, wnt_ref, bias_ref, degree_ref,
    hidden_ref, back_ref, direct_ref, grads_ref,
    part, staged, landed, slopes, total, send_sem, recv_sem,
):
    me = lax.axis_index("feat")
    right, left = lax.rem(me + 1, NF), lax.rem(me + NF - 1, NF)
    greet([{"feat": left}, {"feat": right}])

    half = PIECES // 2
    order = [p for k in range(half) for p in (k, half + k)]
    way = {p: (1 if p < half else -1) for p in order}
    peer = {1: right, -1: left}

    def cols(p):
        return slice(p * PW, (p + 1) * PW)

    def chunk(p, back):
        return lax.rem(me - way[p] * back + 2 * NF, NF)

    def reduce_hop(p, s):
        return pltpu.make_async_remote_copy(
            src_ref=staged.at[s, p], dst_ref=landed.at[s, p],
            send_sem=send_sem.at[s, p], recv_sem=recv_sem.at[s, p],
            device_id={"feat": peer[way[p]]}, device_id_type=MESH,
        )

    def gather_hop(p, s):
        owner = chunk(p, s)
        return pltpu.make_async_remote_copy(
            src_ref=slopes.at[p, owner], dst_ref=slopes.at[p, owner],
            send_sem=send_sem.at[3 + s, p], recv_sem=recv_sem.at[3 + s, p],
            device_id={"feat": peer[way[p]]}, device_id_type=MESH,
        )

    hops = {}
    for p in order:
        pre = jnp.dot(wst_ref[...], feat_ref[:, cols(p)], preferred_element_type=F32)
        pre += jnp.dot(wnt_ref[...], mean_ref[:, cols(p)], preferred_element_type=F32)
        part[p] = pre.reshape(NF, HC, PW)
        staged[0, p] = part[p, chunk(p, 1)].astype(BF16)
        hops[0, p] = reduce_hop(p, 0)
        hops[0, p].start()
    for s in range(1, 3):
        for p in order:
            hops[s - 1, p].wait_recv()
            staged[s, p] = (landed[s - 1, p].astype(F32) + part[p, chunk(p, 1 + s)]).astype(BF16)
            hops[s, p] = reduce_hop(p, s)
            hops[s, p].start()
    for p in order:
        hops[2, p].wait_recv()
        pre = landed[2, p].astype(F32) + part[p, me] + bias_ref[...]
        squash = 1.0 / (1.0 + jnp.exp(-pre))
        hidden_ref[:, cols(p)] = (pre * squash).astype(BF16)
        slope = cot_ref[:, cols(p)].astype(F32) * squash * (1.0 + pre * (1.0 - squash))
        slopes[p, me] = slope.astype(BF16)
        hops[3, p] = gather_hop(p, 0)
        hops[3, p].start()
    for s in range(1, 3):
        for p in order:
            hops[2 + s, p].wait_recv()
            hops[3 + s, p] = gather_hop(p, s)
            hops[3 + s, p].start()
    total[...] = jnp.zeros_like(total)
    lanes = (((1,), (1,)), ((), ()))
    for p in order:
        hops[5, p].wait_recv()
        full = slopes[p].reshape(HID, PW)
        direct = jnp.dot(ws_ref[...], full, preferred_element_type=F32)
        back = jnp.dot(wn_ref[...], full, preferred_element_type=F32)
        for k in range(PW // BS):
            b = p * (PW // BS) + k
            part_of = slice(k * BS, (k + 1) * BS)
            direct_ref[b] = direct[:, part_of]
            back_ref[b] = (back[:, part_of] / degree_ref[b : b + 1, :].astype(F32)).astype(BF16)
        total[0] += lax.dot_general(feat_ref[:, cols(p)], full, lanes, preferred_element_type=F32)
        total[1] += lax.dot_general(mean_ref[:, cols(p)], full, lanes, preferred_element_type=F32)
    for k in range(2):
        for c in range(2):
            at = (2 * k + c) * FC
            grads_ref[at : at + FC] = total[k, :, c * BS : (c + 1) * BS]
    for hop in hops.values():
        hop.wait_send()


def dense_call(feat, mean, cot, ws, wn, wst, wnt, bias, degree):
    return pl.pallas_call(
        dense_kernel,
        out_shape=(
            jax.ShapeDtypeStruct((HC, ROWS), BF16),
            jax.ShapeDtypeStruct((NB, FC, BS), BF16),
            jax.ShapeDtypeStruct((NB, FC, BS), F32),
            jax.ShapeDtypeStruct((4 * FC, BS), F32),
        ),
        in_specs=[vmem()] * 9,
        out_specs=(vmem(),) * 4,
        scratch_shapes=[
            pltpu.VMEM((PIECES, NF, HC, PW), F32),
            pltpu.VMEM((3, PIECES, HC, PW), BF16),
            pltpu.VMEM((3, PIECES, HC, PW), BF16),
            pltpu.VMEM((PIECES, NF, HC, PW), BF16),
            pltpu.VMEM((2, FC, HID), F32),
            pltpu.SemaphoreType.DMA((6, PIECES)),
            pltpu.SemaphoreType.DMA((6, PIECES)),
        ],
        compiler_params=pltpu.CompilerParams(collective_id=1, has_side_effects=True, vmem_limit_bytes=48 * MB),
        name="dense_ring",
    )(feat, mean, cot, ws, wn, wst, wnt, bias, degree)


def backward_kernel(plan, vals_hbm, back_ref, direct_ref, home_ref, out_ref, vals, acc, sems):
    loads = load_vals(vals_hbm, vals, sems)
    acc[HALO : HALO + NB] = direct_ref[...]
    acc[:HALO] = jnp.zeros((HALO, FC, BS), F32)
    acc[HALO + NB :] = jnp.zeros((HALO + 1, FC, BS), F32)
    for load in loads:
        load.wait()

    @pl.loop(0, (plan[7, 192] + 2 * GROUP - 1) // (2 * GROUP))
    def _(step):
        for u in range(GROUP):
            slot = step * (2 * GROUP) + 2 * u
            a = jnp.concatenate([vals[plan[3, slot]], vals[plan[3, slot + 1]]], axis=0)
            x = jnp.concatenate([back_ref[plan[4, slot]], back_ref[plan[4, slot + 1]]], axis=1)
            acc[plan[5, slot]] += jnp.dot(x, a, preferred_element_type=F32)

    home_ref[...] = acc[HALO : HALO + NB]
    out_ref[0] = acc[:HALO].astype(BF16)
    out_ref[1] = acc[HALO + NB : EXT].astype(BF16)


def backward_call(plan, vals, back, direct):
    return pl.pallas_call(
        backward_kernel,
        out_shape=(
            jax.ShapeDtypeStruct((NB, FC, BS), F32),
            jax.ShapeDtypeStruct((2, HALO, FC, BS), BF16),
        ),
        in_specs=[smem(), anyspace(), vmem(), vmem()],
        out_specs=(vmem(), vmem()),
        scratch_shapes=[
            pltpu.VMEM((NNZ + 1, BS, BS), BF16),
            pltpu.VMEM((EXT + 1, FC, BS), F32),
            pltpu.SemaphoreType.DMA((8,)),
        ],
        compiler_params=pltpu.CompilerParams(vmem_limit_bytes=48 * MB),
        name="sparse_backward",
    )(plan, vals, back, direct)


SL_A = 4 * FC // 8
SL_B = SL_A // 4


def final_kernel(
    plan, home_ref, out_ref, grads_ref,
    features_ref, self_ref, neigh_ref,
    landed, land_a, sum_a, land_b, sum_b, whole,
    hs, hr, as_, ar, bs, br, cs, cr, ds, dr,
):
    me = lax.axis_index("vtx")
    right, left = lax.rem(me + 1, NV), lax.rem(me + NV - 1, NV)
    core, x, z = lax.rem(me, 2), lax.rem(me // 2, 4), me // 8
    g = 2 * z + core

    def g_peer(k):
        other = lax.rem(g + k, 8)
        return other, {"vtx": ((other // 2) * 4 + x) * 2 + lax.rem(other, 2)}

    def x_peer(k):
        other = lax.rem(x + k, 4)
        return other, {"vtx": (z * 4 + other) * 2 + core}

    greet(
        [{"vtx": left}, {"vtx": right}]
        + [g_peer(k)[1] for k in range(1, 8)]
        + [x_peer(k)[1] for k in range(1, 4)]
    )
    hops = []
    for d, peer in ((0, left), (1, right)):
        for part in range(4):
            hop = pltpu.make_async_remote_copy(
                src_ref=out_ref.at[d, pl.ds(4 * part, 4)], dst_ref=landed.at[d, pl.ds(4 * part, 4)],
                send_sem=hs.at[d, part], recv_sem=hr.at[d, part],
                device_id={"vtx": peer}, device_id_type=MESH,
            )
            hop.start()
            hops.append(hop)

    def exchange(peers, src_of, dst, mine, send, recv):
        trips = []
        for k in range(1, peers + 1):
            other, device = (g_peer if peers == 7 else x_peer)(k)
            trips.append(pltpu.make_async_remote_copy(
                src_ref=src_of(other), dst_ref=dst.at[mine], send_sem=send.at[k - 1], recv_sem=recv.at[k - 1],
                device_id=device, device_id_type=MESH,
            ))
        for trip in trips:
            trip.start()
        return trips

    def rows_a(k):
        return pl.ds(pl.multiple_of(k * SL_A, 8), SL_A)

    def rows_b(k):
        return pl.ds(pl.multiple_of(k * SL_B, 8), SL_B)

    trips = exchange(7, lambda k: grads_ref.at[rows_a(k)], land_a, g, as_, ar)
    for trip in trips:
        trip.wait()
    land_a[g] = grads_ref[rows_a(g)]
    sum_a[...] = jnp.sum(land_a[...], axis=0)
    trips = exchange(3, lambda k: sum_a.at[rows_b(k)], land_b, x, bs, br)
    for trip in trips:
        trip.wait()
    land_b[x] = sum_a[rows_b(x)]
    sum_b[x] = jnp.sum(land_b[...], axis=0) * float(NV * ROWS) ** -0.5
    trips = exchange(3, lambda k: sum_b.at[x], sum_b, x, cs, cr)
    for trip in trips:
        trip.wait()
    whole[g] = sum_b[...].reshape(SL_A, BS)
    trips = exchange(7, lambda k: whole.at[g], whole, g, ds, dr)
    for trip in trips:
        trip.wait()
    every = whole[...].reshape(4 * FC, BS)
    for k, ref in ((0, self_ref), (1, neigh_ref)):
        for c in range(2):
            at = (2 * k + c) * FC
            ref[:, c * BS : (c + 1) * BS] = every[at : at + FC]

    for d in range(2):
        landed[d, HALO] = jnp.zeros((FC, BS), BF16)
    for hop in hops:
        hop.wait()
    for b in range(NB):
        extra = landed[0, plan[6, b]].astype(F32) + landed[1, plan[6, BS + b]].astype(F32)
        features_ref[:, b * BS : (b + 1) * BS] = (home_ref[b] + extra).astype(BF16)


def final_call(plan, home, out, grads):
    dma = pltpu.SemaphoreType.DMA
    return pl.pallas_call(
        final_kernel,
        out_shape=(
            jax.ShapeDtypeStruct((FC, ROWS), BF16),
            jax.ShapeDtypeStruct((FC, HID), F32),
            jax.ShapeDtypeStruct((FC, HID), F32),
        ),
        in_specs=[smem(), vmem(), vmem(), vmem()],
        out_specs=(vmem(), vmem(), vmem()),
        scratch_shapes=[
            pltpu.VMEM((2, HALO + 1, FC, BS), BF16),
            pltpu.VMEM((8, SL_A, BS), F32),
            pltpu.VMEM((SL_A, BS), F32),
            pltpu.VMEM((4, SL_B, BS), F32),
            pltpu.VMEM((4, SL_B, BS), F32),
            pltpu.VMEM((8, SL_A, BS), F32),
            dma((2, 4)), dma((2, 4)), dma((7,)), dma((7,)), dma((3,)), dma((3,)), dma((3,)), dma((3,)), dma((7,)), dma((7,)),
        ],
        compiler_params=pltpu.CompilerParams(collective_id=2, has_side_effects=True, vmem_limit_bytes=48 * MB),
        name="halo_back",
    )(plan, home, out, grads)


def on_device(
    features, w_self, w_neigh, bias_terms, block_vals, block_rows, block_cols, block_count, recv_lists, degree, cotangent
):
    feat, cot = features.T, cotangent.T
    wide = ((0, ENT - NNZ),)
    table = jnp.concatenate(
        [
            jnp.pad(block_rows, wide)[None],
            jnp.pad(block_cols, wide)[None],
            jnp.broadcast_to(block_count, (6, ENT)),
        ],
        axis=0,
    )
    lists = jnp.broadcast_to(jnp.pad(recv_lists, ((0, BS - 2 * HALO),), constant_values=-1)[None], (8, BS))
    degree = degree.reshape(NB, BS)
    halo, plan = halo_call(table, lists, feat)
    mean = forward_call(plan, block_vals, feat, halo, degree)
    hidden, back, direct, grads = dense_call(
        feat, mean, cot, w_self, w_neigh, w_self.T, w_neigh.T, bias_terms.reshape(HC, 1), degree
    )
    home, out = backward_call(plan, block_vals, back, direct)
    grad_features, grad_self, grad_neigh = final_call(plan, home, out, grads)
    return hidden.T, grad_features.T, grad_self, grad_neigh


def solution(mesh):
    placed = (
        P("vtx", "feat"), P("feat", None), P("feat", None), P("feat"), P("vtx", None, None), P("vtx"), P("vtx"), P("vtx"),
        P("vtx"), P("vtx"), P("vtx", "feat"),
    )
    return jax.shard_map(
        on_device,
        mesh=mesh,
        in_specs=placed,
        out_specs=(P("vtx", "feat"), P("vtx", "feat"), P("feat", None), P("feat", None)),
        check_vma=False,
    )
```

```python
import functools

import jax
import jax.numpy as jnp
from jax import lax
from jax.experimental import pallas as pl
from jax.experimental.pallas import tpu as pltpu
from jax.sharding import PartitionSpec as P

MESH = pl.DeviceIdType.MESH
F32, BF16, I32 = jnp.float32, jnp.bfloat16, jnp.int32
BS = 128
NB = 32
HALO = 16
NNZ = 320
EXT = NB + 2 * HALO
FC = 192
HID = 256
HC = 64
ROWS = NB * BS
NV, NF = 32, 4
ENT = 384
PAIRS_F = (NNZ + NB) // 2
PAIRS_B = (NNZ + EXT) // 2
GROUP = 8
PIECES = 8
PW = ROWS // PIECES
MB = 1 << 20


def vmem():
    return pl.BlockSpec(memory_space=pltpu.VMEM)


def smem():
    return pl.BlockSpec(memory_space=pltpu.SMEM)


def anyspace():
    return pl.BlockSpec(memory_space=pl.ANY)


def greet(peers):
    barrier = pltpu.get_barrier_semaphore()
    for peer in peers:
        pl.semaphore_signal(barrier, inc=1, device_id=peer, device_id_type=MESH)
    pl.semaphore_wait(barrier, len(peers))


def iota(shape, dim):
    return lax.broadcasted_iota(I32, shape, dim)


def as_column(row):
    n = row.shape[1]
    diagonal = iota((n, n), 0) == iota((n, n), 1)
    return jnp.sum(jnp.where(diagonal, row, jnp.zeros_like(row)), axis=1, keepdims=True, dtype=row.dtype)


def down(values):
    return jnp.sum(values, axis=0, keepdims=True, dtype=I32)


def pair_schedule(key, other, active, pairs):
    far = 1000
    sub, lane = iota((ENT, ENT), 0), iota((ENT, ENT), 1)
    key = jnp.where(active, key, far)
    key_col = as_column(key)
    rank = down(jnp.where((key_col == key) & (sub < lane), 1, 0))
    group, at = iota((EXT, ENT), 0), iota((EXT, ENT), 1)
    size = jnp.sum(jnp.where(group == key, 1, 0), axis=1, keepdims=True, dtype=I32)
    size = ((size + 1) >> 1) << 1
    start = down(jnp.where(group < key, size, 0))
    slot = jnp.where(active, start + rank, far)
    hit = as_column(slot) == lane

    def at_slots(column, default):
        return down(jnp.where(hit, column - default, 0)) + default

    entry = at_slots(sub[:, :1], NNZ)
    source = at_slots(as_column(other), 0)
    goes_on = jnp.minimum(at_slots(as_column(rank), 1), 1)
    end = down(jnp.where(group <= at, size, 0))
    own = down(jnp.where(group == at, size, 0))
    done = jnp.where(own > 0, (end >> 1) - 1, pairs)
    return [jnp.clip(entry, 0, NNZ), jnp.clip(source, 0, EXT - 1), goes_on, jnp.clip(done, 0, pairs)]


def inverse(lists, first):
    ours = as_column(lists)
    sub, lane = iota((BS, BS), 0), iota((BS, BS), 1)
    hit = (ours == lane) & (sub >= first) & (sub < first + HALO)
    return jnp.clip(down(jnp.where(hit, sub - (first + HALO), 0)) + HALO, 0, HALO)


def load_vals(vals_hbm, vals, sems):
    share = NNZ // 8
    loads = [
        pltpu.make_async_copy(vals_hbm.at[pl.ds(k * share, share)], vals.at[pl.ds(k * share, share)], sems.at[k])
        for k in range(8)
    ]
    for load in loads:
        load.start()
    vals[NNZ] = jnp.zeros((BS, BS), BF16)
    return loads


def sparse_sums(product, goes_on, sums, first, last, carry):
    def step(i, acc):
        for u in range(GROUP):
            t = i * GROUP + u
            acc = acc * goes_on(t).astype(F32) + product(t)
            sums[t] = acc
        return acc

    return lax.fori_loop(first // GROUP, last // GROUP, step, carry)


def gather_kernel(
    rows_ref, cols_ref, count_ref, lists_ref, feat_ref, vals_hbm, degree_ref,
    mean_ref, plan_ref,
    lists_out, lists_in, lists_sm, plan_sm, blocks, sent, halo, vals, sums, sm_sem, ls, lr, bs, br, vs,
):
    me = lax.axis_index("vtx")
    right, left = lax.rem(me + 1, NV), lax.rem(me + NV - 1, NV)
    loads = load_vals(vals_hbm, vals, vs)
    lists_out[...] = jnp.full((8, BS), -1, I32)
    lists_out[0:1, : 2 * HALO] = lists_ref[...]
    greet([{"vtx": left}, {"vtx": right}])
    trips = []
    for k, peer in ((0, right), (1, left)):
        trip = pltpu.make_async_remote_copy(
            src_ref=lists_out, dst_ref=lists_in.at[k], send_sem=ls.at[k], recv_sem=lr.at[k],
            device_id={"vtx": peer}, device_id_type=MESH,
        )
        trip.start()
        trips.append(trip)
    blocks[0] = jnp.zeros((FC, BS), BF16)
    for b in range(NB):
        blocks[1 + b] = feat_ref[:, b * BS : (b + 1) * BS]
    for trip in trips:
        trip.wait()
    local = pltpu.make_async_copy(lists_in, lists_sm, sm_sem)
    local.start()
    local.wait()
    sends = []
    for part in range(4):
        for d in range(2):
            for j in range(4 * part, 4 * part + 4):
                sent[d, j] = blocks[lists_sm[1 - d, 0, j + HALO * d] + 1]
            trip = pltpu.make_async_remote_copy(
                src_ref=sent.at[d, pl.ds(4 * part, 4)], dst_ref=halo.at[pl.ds((HALO + NB) * d + 4 * part, 4)],
                send_sem=bs.at[d, part], recv_sem=br.at[d, part],
                device_id={"vtx": right if d == 0 else left}, device_id_type=MESH,
            )
            trip.start()
            sends.append(trip)

    def wide(ref):
        return jnp.concatenate([ref[...], jnp.zeros((1, ENT - NNZ), I32)], axis=1)

    rows, cols = wide(rows_ref), wide(cols_ref)
    active = iota((1, ENT), 1) < count_ref[0]
    plan = pair_schedule(rows, cols, active, PAIRS_F) + pair_schedule(cols, rows, active, PAIRS_B)
    from_right = inverse(lists_in[1, 0:1], 0)
    from_left = inverse(lists_in[0, 0:1], HALO)
    plan.append(jnp.concatenate([from_right, from_left, jnp.zeros((1, BS), I32)], axis=1))
    for k, row in enumerate(plan):
        plan_ref[k : k + 1] = row
    for k in range(len(plan), 16):
        plan_ref[k : k + 1] = jnp.zeros((1, ENT), I32)
    local = pltpu.make_async_copy(plan_ref, plan_sm, sm_sem)
    local.start()
    local.wait()
    for load in loads:
        load.wait()
    for b in range(NB):
        halo[HALO + b] = blocks[1 + b]
    for trip in sends:
        trip.wait()
    sums[PAIRS_F] = jnp.zeros((FC, BS), F32)

    def product(t):
        a = jnp.concatenate([vals[plan_sm[0, 2 * t]], vals[plan_sm[0, 2 * t + 1]]], axis=1)
        x = jnp.concatenate([halo[plan_sm[1, 2 * t]], halo[plan_sm[1, 2 * t + 1]]], axis=1)
        return lax.dot_general(x, a, (((1,), (1,)), ((), ())), preferred_element_type=F32)

    sparse_sums(product, lambda t: plan_sm[2, 2 * t], sums, 0, PAIRS_F, jnp.zeros((FC, BS), F32))
    for b in range(NB):
        divisor = degree_ref[b : b + 1, :].astype(F32)
        mean_ref[:, b * BS : (b + 1) * BS] = (sums[plan_sm[3, b]] / divisor).astype(BF16)


def gather_call(rows, cols, count, lists, feat, vals, degree):
    dma = pltpu.SemaphoreType.DMA
    return pl.pallas_call(
        gather_kernel,
        out_shape=(jax.ShapeDtypeStruct((FC, ROWS), BF16), jax.ShapeDtypeStruct((16, ENT), I32)),
        in_specs=[vmem(), vmem(), smem(), vmem(), vmem(), anyspace(), vmem()],
        out_specs=(vmem(), vmem()),
        scratch_shapes=[
            pltpu.VMEM((8, BS), I32),
            pltpu.VMEM((2, 8, BS), I32),
            pltpu.SMEM((2, 8, BS), I32),
            pltpu.SMEM((16, ENT), I32),
            pltpu.VMEM((NB + 1, FC, BS), BF16),
            pltpu.VMEM((2, HALO, FC, BS), BF16),
            pltpu.VMEM((EXT, FC, BS), BF16),
            pltpu.VMEM((NNZ + 1, BS, BS), BF16),
            pltpu.VMEM((PAIRS_F + 1, FC, BS), F32),
            dma, dma((2,)), dma((2,)), dma((2, 4)), dma((2, 4)), dma((8,)),
        ],
        compiler_params=pltpu.CompilerParams(collective_id=0, has_side_effects=True, vmem_limit_bytes=48 * MB),
        name="gather_mean",
    )(rows, cols, count, lists, feat, vals, degree)


SL_A = 4 * FC // 8
SL_B = SL_A // 4


def ring_kernel(
    plan, feat_ref, mean_ref, cot_ref, ws_ref, wn_ref, bias_ref, degree_ref, vals_hbm,
    hidden_ref, features_ref, self_ref, neigh_ref,
    wst, wnt, part, staged, landed, slopes, total, vals, sums, back, direct, out, arrived,
    grads, land_a, sum_a, land_b, sum_b, whole,
    send_sem, recv_sem, vs, hs, hr, as_, ar, bs, br, cs, cr, ds, dr,
):
    me = lax.axis_index("feat")
    right, left = lax.rem(me + 1, NF), lax.rem(me + NF - 1, NF)
    v = lax.axis_index("vtx")
    v_right, v_left = lax.rem(v + 1, NV), lax.rem(v + NV - 1, NV)
    core, x, z = lax.rem(v, 2), lax.rem(v // 2, 4), v // 8
    g = 2 * z + core

    def g_peer(k):
        other = lax.rem(g + k, 8)
        return other, {"vtx": ((other // 2) * 4 + x) * 2 + lax.rem(other, 2)}

    def x_peer(k):
        other = lax.rem(x + k, 4)
        return other, {"vtx": (z * 4 + other) * 2 + core}

    loads = load_vals(vals_hbm, vals, vs)
    greet(
        [{"feat": left}, {"feat": right}, {"vtx": v_left}, {"vtx": v_right}]
        + [g_peer(k)[1] for k in range(1, 8)]
        + [x_peer(k)[1] for k in range(1, 4)]
    )

    half = PIECES // 2
    order = [p for k in range(half) for p in (k, half + k)]
    way = {p: (1 if p < half else -1) for p in order}
    peer = {1: right, -1: left}

    def cols(p):
        return slice(p * PW, (p + 1) * PW)

    def chunk(p, back):
        return lax.rem(me - way[p] * back + 2 * NF, NF)

    def reduce_hop(p, s):
        return pltpu.make_async_remote_copy(
            src_ref=staged.at[s, p], dst_ref=landed.at[s, p],
            send_sem=send_sem.at[s, p], recv_sem=recv_sem.at[s, p],
            device_id={"feat": peer[way[p]]}, device_id_type=MESH,
        )

    def gather_hop(p, s):
        owner = chunk(p, s)
        return pltpu.make_async_remote_copy(
            src_ref=slopes.at[p, owner], dst_ref=slopes.at[p, owner],
            send_sem=send_sem.at[3 + s, p], recv_sem=recv_sem.at[3 + s, p],
            device_id={"feat": peer[way[p]]}, device_id_type=MESH,
        )

    wst[...] = ws_ref[...].T
    wnt[...] = wn_ref[...].T
    bias = as_column(bias_ref[...])
    hops = {}
    for p in order:
        pre = jnp.dot(wst[...], feat_ref[:, cols(p)], preferred_element_type=F32)
        pre += jnp.dot(wnt[...], mean_ref[:, cols(p)], preferred_element_type=F32)
        part[p] = pre.reshape(NF, HC, PW)
        staged[0, p] = part[p, chunk(p, 1)].astype(BF16)
        hops[0, p] = reduce_hop(p, 0)
        hops[0, p].start()
    for s in range(1, 3):
        for p in order:
            hops[s - 1, p].wait_recv()
            staged[s, p] = (landed[s - 1, p].astype(F32) + part[p, chunk(p, 1 + s)]).astype(BF16)
            hops[s, p] = reduce_hop(p, s)
            hops[s, p].start()
    for p in order:
        hops[2, p].wait_recv()
        pre = landed[2, p].astype(F32) + part[p, me] + bias
        squash = 1.0 / (1.0 + jnp.exp(-pre))
        hidden_ref[:, cols(p)] = (pre * squash).astype(BF16)
        slope = cot_ref[:, cols(p)].astype(F32) * squash * (1.0 + pre * (1.0 - squash))
        slopes[p, me] = slope.astype(BF16)
        hops[3, p] = gather_hop(p, 0)
        hops[3, p].start()
    for s in range(1, 3):
        for p in order:
            hops[2 + s, p].wait_recv()
            hops[3 + s, p] = gather_hop(p, s)
            hops[3 + s, p].start()
    total[...] = jnp.zeros_like(total)
    lanes = (((1,), (1,)), ((), ()))
    for p in order:
        hops[5, p].wait_recv()
        full = slopes[p].reshape(HID, PW)
        near = jnp.dot(ws_ref[...], full, preferred_element_type=F32)
        far = jnp.dot(wn_ref[...], full, preferred_element_type=F32)
        for k in range(PW // BS):
            b = p * (PW // BS) + k
            part_of = slice(k * BS, (k + 1) * BS)
            direct[b] = near[:, part_of]
            back[b] = (far[:, part_of] / degree_ref[b : b + 1, :].astype(F32)).astype(BF16)
        total[0] += lax.dot_general(feat_ref[:, cols(p)], full, lanes, preferred_element_type=F32)
        total[1] += lax.dot_general(mean_ref[:, cols(p)], full, lanes, preferred_element_type=F32)
    for k in range(2):
        for c in range(2):
            at = (2 * k + c) * FC
            grads[at : at + FC] = total[k, :, c * BS : (c + 1) * BS]

    def exchange(peers, src_of, dst, mine, send, recv):
        trips = []
        for k in range(1, peers + 1):
            other, device = (g_peer if peers == 7 else x_peer)(k)
            trips.append(pltpu.make_async_remote_copy(
                src_ref=src_of(other), dst_ref=dst.at[mine], send_sem=send.at[k - 1], recv_sem=recv.at[k - 1],
                device_id=device, device_id_type=MESH,
            ))
        for trip in trips:
            trip.start()
        return trips

    def rows_a(k):
        return pl.ds(pl.multiple_of(k * SL_A, 8), SL_A)

    def rows_b(k):
        return pl.ds(pl.multiple_of(k * SL_B, 8), SL_B)

    trips = exchange(7, lambda k: grads.at[rows_a(k)], land_a, g, as_, ar)
    for load in loads:
        load.wait()

    def product(t):
        a = jnp.concatenate([vals[plan[4, 2 * t]], vals[plan[4, 2 * t + 1]]], axis=0)
        b = jnp.concatenate([back[plan[5, 2 * t]], back[plan[5, 2 * t + 1]]], axis=1)
        return jnp.dot(b, a, preferred_element_type=F32)

    sums[PAIRS_B] = jnp.zeros((FC, BS), F32)
    sparse_sums(product, lambda t: plan[6, 2 * t], sums, 0, PAIRS_B, jnp.zeros((FC, BS), F32))
    halo_hops = []
    for q in range(4):
        for d, towards in ((0, v_left), (1, v_right)):
            for j in range(4 * q, 4 * q + 4):
                out[d, j] = sums[plan[7, (HALO + NB) * d + j]].astype(BF16)
            hop = pltpu.make_async_remote_copy(
                src_ref=out.at[d, pl.ds(4 * q, 4)], dst_ref=arrived.at[d, pl.ds(4 * q, 4)],
                send_sem=hs.at[d, q], recv_sem=hr.at[d, q],
                device_id={"vtx": towards}, device_id_type=MESH,
            )
            hop.start()
            halo_hops.append(hop)
    for trip in trips:
        trip.wait()
    land_a[g] = grads[rows_a(g)]
    sum_a[...] = jnp.sum(land_a[...], axis=0)
    trips = exchange(3, lambda k: sum_a.at[rows_b(k)], land_b, x, bs, br)
    for b in range(NB):
        direct[b] += sums[plan[7, HALO + b]]
    for d in range(2):
        arrived[d, HALO] = jnp.zeros((FC, BS), BF16)
    for trip in trips:
        trip.wait()
    land_b[x] = sum_a[rows_b(x)]
    sum_b[x] = jnp.sum(land_b[...], axis=0) * float(NV * ROWS) ** -0.5
    trips = exchange(3, lambda k: sum_b.at[x], sum_b, x, cs, cr)
    for trip in trips:
        trip.wait()
    whole[g] = sum_b[...].reshape(SL_A, BS)
    trips = exchange(7, lambda k: whole.at[g], whole, g, ds, dr)
    for hop in halo_hops:
        hop.wait()
    for b in range(NB):
        extra = arrived[0, plan[8, b]].astype(F32) + arrived[1, plan[8, BS + b]].astype(F32)
        features_ref[:, b * BS : (b + 1) * BS] = (direct[b] + extra).astype(BF16)
    for trip in trips:
        trip.wait()
    every = whole[...].reshape(4 * FC, BS)
    for k, ref in ((0, self_ref), (1, neigh_ref)):
        for c in range(2):
            at = (2 * k + c) * FC
            ref[:, c * BS : (c + 1) * BS] = every[at : at + FC]
    for hop in hops.values():
        hop.wait_send()


def ring_call(plan, feat, mean, cot, ws, wn, bias, degree, vals):
    dma = pltpu.SemaphoreType.DMA
    return pl.pallas_call(
        ring_kernel,
        out_shape=(
            jax.ShapeDtypeStruct((HC, ROWS), BF16),
            jax.ShapeDtypeStruct((FC, ROWS), BF16),
            jax.ShapeDtypeStruct((FC, HID), F32),
            jax.ShapeDtypeStruct((FC, HID), F32),
        ),
        in_specs=[smem()] + [vmem()] * 7 + [anyspace()],
        out_specs=(vmem(),) * 4,
        scratch_shapes=[
            pltpu.VMEM((HID, FC), BF16),
            pltpu.VMEM((HID, FC), BF16),
            pltpu.VMEM((PIECES, NF, HC, PW), F32),
            pltpu.VMEM((3, PIECES, HC, PW), BF16),
            pltpu.VMEM((3, PIECES, HC, PW), BF16),
            pltpu.VMEM((PIECES, NF, HC, PW), BF16),
            pltpu.VMEM((2, FC, HID), F32),
            pltpu.VMEM((NNZ + 1, BS, BS), BF16),
            pltpu.VMEM((PAIRS_B + 1, FC, BS), F32),
            pltpu.VMEM((NB, FC, BS), BF16),
            pltpu.VMEM((NB, FC, BS), F32),
            pltpu.VMEM((2, HALO, FC, BS), BF16),
            pltpu.VMEM((2, HALO + 1, FC, BS), BF16),
            pltpu.VMEM((4 * FC, BS), F32),
            pltpu.VMEM((8, SL_A, BS), F32),
            pltpu.VMEM((SL_A, BS), F32),
            pltpu.VMEM((4, SL_B, BS), F32),
            pltpu.VMEM((4, SL_B, BS), F32),
            pltpu.VMEM((8, SL_A, BS), F32),
            dma((6, PIECES)), dma((6, PIECES)), dma((8,)), dma((2, 4)), dma((2, 4)),
            dma((7,)), dma((7,)), dma((3,)), dma((3,)), dma((3,)), dma((3,)), dma((7,)), dma((7,)),
        ],
        compiler_params=pltpu.CompilerParams(collective_id=1, has_side_effects=True, vmem_limit_bytes=60 * MB),
        name="ring_and_back",
    )(plan, feat, mean, cot, ws, wn, bias, degree, vals)


def on_device(
    features, w_self, w_neigh, bias_terms, block_vals, block_rows, block_cols, block_count, recv_lists, degree, cotangent
):
    feat, cot = features.T, cotangent.T
    degree = degree.reshape(NB, BS)
    mean, plan = gather_call(
        block_rows.reshape(1, NNZ), block_cols.reshape(1, NNZ), block_count, recv_lists.reshape(1, 2 * HALO),
        feat, block_vals, degree,
    )
    hidden, grad_features, grad_self, grad_neigh = ring_call(
        plan, feat, mean, cot, w_self, w_neigh, bias_terms.reshape(1, HC), degree, block_vals
    )
    return hidden.T, grad_features.T, grad_self, grad_neigh


def solution(mesh):
    placed = (
        P("vtx", "feat"), P("feat", None), P("feat", None), P("feat"), P("vtx", None, None), P("vtx"), P("vtx"), P("vtx"),
        P("vtx"), P("vtx"), P("vtx", "feat"),
    )
    return jax.shard_map(
        on_device,
        mesh=mesh,
        in_specs=placed,
        out_specs=(P("vtx", "feat"), P("vtx", "feat"), P("feat", None), P("feat", None)),
        check_vma=False,
    )
```

```python
import functools

import jax
import jax.numpy as jnp
from jax import lax
from jax.experimental import pallas as pl
from jax.experimental.pallas import tpu as pltpu
from jax.sharding import PartitionSpec as P

MESH = pl.DeviceIdType.MESH
F32, BF16, I32 = jnp.float32, jnp.bfloat16, jnp.int32
BS = 128
NB = 32
HALO = 16
NNZ = 320
EXT = NB + 2 * HALO
FC = 192
HID = 256
HC = 64
ROWS = NB * BS
NV, NF = 32, 4
ENT = 384
PIECES = 8
PB = NB // PIECES
PAIRS_F = (NNZ + NB) // 2
PAIRS_B = (NNZ + EXT) // 2
PIECE_PAIRS = PAIRS_F // PIECES
GROUP = 24
ZERO = NB
SL_A = 4 * FC // 8
SL_B = SL_A // 4
MB = 1 << 20


def vmem():
    return pl.BlockSpec(memory_space=pltpu.VMEM)


def smem():
    return pl.BlockSpec(memory_space=pltpu.SMEM)


def anyspace():
    return pl.BlockSpec(memory_space=pl.ANY)


def greet(peers):
    barrier = pltpu.get_barrier_semaphore()
    for peer in peers:
        pl.semaphore_signal(barrier, inc=1, device_id=peer, device_id_type=MESH)
    pl.semaphore_wait(barrier, len(peers))


def iota(shape, dim):
    return lax.broadcasted_iota(I32, shape, dim)


def as_column(row):
    n = row.shape[1]
    diagonal = iota((n, n), 0) == iota((n, n), 1)
    return jnp.sum(jnp.where(diagonal, row, jnp.zeros_like(row)), axis=1, keepdims=True, dtype=row.dtype)


def down(values):
    return jnp.sum(values, axis=0, keepdims=True, dtype=I32)


def group_sizes(key):
    size = jnp.sum(jnp.where(iota((EXT, ENT), 0) == key, 1, 0), axis=1, keepdims=True, dtype=I32)
    return ((size + 1) >> 1) << 1


def order_groups(key):
    block, lane = iota((EXT, ENT), 0), iota((EXT, ENT), 1)
    size = group_sizes(key)
    size_row = down(jnp.where(block == lane, size, 0))
    earlier = (size < size_row) | ((size == size_row) & (block < lane))
    place = down(jnp.where(earlier & (block < NB), 1, 0))
    place_col = as_column(place)[:EXT]
    at_place = down(jnp.where((place_col == lane) & (block < NB), block, 0))
    of_entry = down(jnp.where(block == key, place_col, 0))
    return place, at_place, of_entry


def pair_schedule(key, other, active):
    far = 1000
    sub, lane = iota((ENT, ENT), 0), iota((ENT, ENT), 1)
    key = jnp.where(active, key, far)
    key_col = as_column(key)
    rank = down(jnp.where((key_col == key) & (sub < lane), 1, 0))
    group, at = iota((EXT, ENT), 0), iota((EXT, ENT), 1)
    size = group_sizes(key)
    start = down(jnp.where(group < key, size, 0))
    slot = jnp.where(active, start + rank, far)
    hit = as_column(slot) == lane

    def at_slots(column, default):
        return down(jnp.where(hit, column - default, 0)) + default

    entry = at_slots(sub[:, :1], NNZ)
    source = at_slots(as_column(other), 0)
    goes_on = jnp.minimum(at_slots(as_column(rank), 1), 1)
    end = down(jnp.where(group <= at, size, 0))
    own = down(jnp.where(group == at, size, 0))
    done = jnp.where(own > 0, (end >> 1) - 1, PAIRS_B)
    return [jnp.clip(entry, 0, NNZ), jnp.clip(source, 0, EXT), goes_on, jnp.clip(done, 0, PAIRS_B)]


def inverse(lists, first):
    ours = as_column(lists)
    sub, lane = iota((BS, BS), 0), iota((BS, BS), 1)
    hit = (ours == lane) & (sub >= first) & (sub < first + HALO)
    return jnp.clip(down(jnp.where(hit, sub - (first + HALO), 0)) + HALO, 0, HALO)


def layer_kernel(
    rows_hbm, cols_hbm, count_ref, lists_hbm, feat_hbm, cot_hbm, degree_hbm, ws_ref, wn_ref, bias_hbm, vals_hbm,
    hidden_hbm, base_hbm, arrived, grads_hbm, plan_hbm,
    rows_v, cols_v, lists_v, bias_v, degree_v, rdeg, lists_out, lists_in, lists_sm, plan_v, plan,
    ext, landed_halo, cot, vals, sums, sent, mean, wst, wnt, part, staged, landed, slopes, hid, back, base, hidden,
    total, grads, land_a, sum_a, land_b, sum_b, whole,
    small_sem, feat_sem, cot_sem, vals_sem, sm_sem, ls, lr, hs, hr,
    send_sem, recv_sem, bs, br, as_, ar, zs, zr, cs, cr, ds, dr, out_sem,
):
    me = lax.axis_index("feat")
    right, left = lax.rem(me + 1, NF), lax.rem(me + NF - 1, NF)
    v = lax.axis_index("vtx")
    v_right, v_left = lax.rem(v + 1, NV), lax.rem(v + NV - 1, NV)
    h, z = lax.rem(v, 8), v // 8

    def h_peer(k):
        other = lax.rem(h + k, 8)
        return other, {"vtx": z * 8 + other}

    def z_peer(k):
        other = lax.rem(z + k, 4)
        return other, {"vtx": other * 8 + h}

    small = [
        pltpu.make_async_copy(src, dst, small_sem.at[k])
        for k, (src, dst) in enumerate(
            [(lists_hbm, lists_v), (rows_hbm, rows_v), (cols_hbm, cols_v), (bias_hbm, bias_v), (degree_hbm, degree_v)]
        )
    ]
    feat_loads = [
        pltpu.make_async_copy(feat_hbm.at[:, pl.ds(b * BS, BS)], ext.at[b], feat_sem.at[b]) for b in range(NB)
    ]
    cot_loads = [
        pltpu.make_async_copy(cot_hbm.at[:, pl.ds(b * BS, BS)], cot.at[b], cot_sem.at[b]) for b in range(NB)
    ]
    share = NNZ // 8
    val_loads = [
        pltpu.make_async_copy(vals_hbm.at[pl.ds(k * share, share)], vals.at[pl.ds(k * share, share)], vals_sem.at[k])
        for k in range(8)
    ]
    for load in small + feat_loads:
        load.start()
    barrier = pltpu.get_barrier_semaphore()
    peers = (
        [{"vtx": v_left}, {"vtx": v_right}, {"feat": left}, {"feat": right}]
        + [h_peer(k)[1] for k in range(1, 8)]
        + [z_peer(k)[1] for k in range(1, 4)]
    )
    for peer in peers:
        pl.semaphore_signal(barrier, inc=1, device_id=peer, device_id_type=MESH)
    for load in val_loads + cot_loads:
        load.start()
    small[0].wait()
    lists_out[...] = jnp.full((8, BS), -1, I32)
    lists_out[0:1, : 2 * HALO] = lists_v[...].reshape(1, 2 * HALO)
    ext[ZERO] = jnp.zeros((FC, BS), BF16)
    vals[NNZ] = jnp.zeros((BS, BS), BF16)
    sums[PAIRS_B] = jnp.zeros((FC, BS), F32)
    pl.semaphore_wait(barrier, len(peers))

    trips = []
    for k, peer in ((0, v_right), (1, v_left)):
        trip = pltpu.make_async_remote_copy(
            src_ref=lists_out, dst_ref=lists_in.at[k], send_sem=ls.at[k], recv_sem=lr.at[k],
            device_id={"vtx": peer}, device_id_type=MESH,
        )
        trip.start()
        trips.append(trip)
    for load in small[1:] + feat_loads:
        load.wait()
    wst[...] = ws_ref[...].T
    wnt[...] = wn_ref[...].T
    bias = as_column(bias_v[...].reshape(1, HC))
    for b in range(NB):
        rdeg[b] = jnp.broadcast_to(1.0 / degree_v[b : b + 1, :].astype(F32), (8, BS))
    for trip in trips:
        trip.wait()
    local = pltpu.make_async_copy(lists_in, lists_sm, sm_sem)
    local.start()
    local.wait()
    halo_trips = []
    for q in range(4):
        for d in range(2):
            for j in range(4 * q, 4 * q + 4):
                sent[d, j] = ext[lax.rem(lists_sm[1 - d, 0, j + HALO * d] + NB + 1, NB + 1)]
            trip = pltpu.make_async_remote_copy(
                src_ref=sent.at[d, pl.ds(4 * q, 4)], dst_ref=landed_halo.at[d, pl.ds(4 * q, 4)],
                send_sem=hs.at[d, q], recv_sem=hr.at[d, q],
                device_id={"vtx": v_right if d == 0 else v_left}, device_id_type=MESH,
            )
            trip.start()
            halo_trips.append(trip)

    def wide(ref):
        return jnp.concatenate([ref[...].reshape(1, NNZ), jnp.zeros((1, ENT - NNZ), I32)], axis=1)

    rows, cols = wide(rows_v), wide(cols_v)
    active = iota((1, ENT), 1) < count_ref[0]
    where_col = jnp.where(cols < HALO, cols + NB + 1, jnp.where(cols < HALO + NB, cols - HALO, cols + 1))
    place, at_place, entry_place = order_groups(jnp.where(active, rows, 1000))
    table = pair_schedule(entry_place, where_col, active) + pair_schedule(cols, entry_place, active)
    from_right = inverse(lists_in[1, 0:1], 0)
    from_left = inverse(lists_in[0, 0:1], HALO)
    table.append(jnp.concatenate([from_right, from_left, jnp.zeros((1, BS), I32)], axis=1))
    table += [jnp.clip(place, 0, NB - 1), jnp.clip(at_place, 0, NB - 1)]
    for k, row in enumerate(table):
        plan_v[k : k + 1] = row
    for k in range(len(table), 16):
        plan_v[k : k + 1] = jnp.zeros((1, ENT), I32)
    local = pltpu.make_async_copy(plan_v, plan, sm_sem)
    local.start()
    plan_out = pltpu.make_async_copy(plan_v, plan_hbm, out_sem.at[0])
    plan_out.start()
    local.wait()

    def block_at(q):
        return plan[10, q]

    def side_by_side(blocks):
        return jnp.concatenate(blocks, axis=1)

    for p in range(PIECES):
        own = side_by_side([ext[block_at(p * PB + k)] for k in range(PB)])
        pre = jnp.dot(wst[...], own, preferred_element_type=F32)
        for k in range(PB):
            part[p * PB + k] = pre[:, k * BS : (k + 1) * BS]
    for load in val_loads + cot_loads:
        load.wait()
    for trip in halo_trips:
        trip.wait()
    for d in range(2):
        for j in range(HALO):
            ext[NB + 1 + HALO * d + j] = landed_halo[d, j]

    way = {p: 1 - 2 * (p % 2) for p in range(PIECES)}
    peer_of = {1: right, -1: left}

    def chunk(w, back_by):
        return lax.rem(me - w * back_by + 2 * NF, NF)

    def reduce_hop(p, s, w):
        return pltpu.make_async_remote_copy(
            src_ref=staged.at[s, p], dst_ref=landed.at[s, p],
            send_sem=send_sem.at[s, p], recv_sem=recv_sem.at[s, p],
            device_id={"feat": peer_of[w]}, device_id_type=MESH,
        )

    def gather_hop(p, s, w):
        owner = chunk(w, s)
        return pltpu.make_async_remote_copy(
            src_ref=slopes.at[p, owner], dst_ref=slopes.at[p, owner],
            send_sem=send_sem.at[3 + s, p], recv_sem=recv_sem.at[3 + s, p],
            device_id={"feat": peer_of[w]}, device_id_type=MESH,
        )

    def chunk_rows(c):
        return pl.ds(pl.multiple_of(c * HC, HC), HC)

    def forward_product(t):
        a = side_by_side([vals[plan[0, 2 * t]], vals[plan[0, 2 * t + 1]]])
        x = side_by_side([ext[plan[1, 2 * t]], ext[plan[1, 2 * t + 1]]])
        return lax.dot_general(x, a, (((1,), (1,)), ((), ())), preferred_element_type=F32)

    def reduce_on(p, s, w):
        reduce_hop(p, s - 1, w).wait_recv()
        for k in range(PB):
            more = part[p * PB + k, chunk_rows(chunk(w, 1 + s))]
            staged[s, p, k] = (landed[s - 1, p, k].astype(F32) + more).astype(BF16)
        reduce_hop(p, s, w).start()

    def forward_pieces(i, acc):
        for w in (1, -1):
            p = 2 * i + (0 if w == 1 else 1)
            for u in range(PIECE_PAIRS):
                t = p * PIECE_PAIRS + u
                acc = acc * plan[2, 2 * t].astype(F32) + forward_product(t)
                sums[t] = acc
            for k in range(PB):
                q = p * PB + k
                scale = rdeg[block_at(q)][0:1]
                mean[q] = (sums[plan[3, q]] * scale).astype(BF16)
            pre = jnp.dot(wnt[...], side_by_side([mean[p * PB + k] for k in range(PB)]), preferred_element_type=F32)
            for k in range(PB):
                q = p * PB + k
                part[q] = part[q] + pre[:, k * BS : (k + 1) * BS]
                staged[0, p, k] = part[q, chunk_rows(chunk(w, 1))].astype(BF16)
            reduce_hop(p, 0, w).start()
        return acc

    acc = forward_pieces(0, jnp.zeros((FC, BS), F32))

    def forward_step(i, acc):
        acc = forward_pieces(i, acc)
        for w in (1, -1):
            reduce_on(2 * i - 2 + (0 if w == 1 else 1), 1, w)
        return acc

    lax.fori_loop(1, PIECES // 2, forward_step, acc)
    for p in (PIECES - 2, PIECES - 1):
        reduce_on(p, 1, way[p])
    for p in range(PIECES):
        reduce_on(p, 2, way[p])
    for p in range(PIECES):
        reduce_hop(p, 2, way[p]).wait_recv()
        for k in range(PB):
            q = p * PB + k
            pre = landed[2, p, k].astype(F32) + part[q, chunk_rows(me)] + bias
            squash = 1.0 / (1.0 + jnp.exp(-pre))
            hid[q] = (pre * squash).astype(BF16)
            slope = cot[block_at(q)].astype(F32) * squash * (1.0 + pre * (1.0 - squash))
            slopes[p, me, k] = slope.astype(BF16)
        gather_hop(p, 0, way[p]).start()
    for s in range(1, 3):
        for p in range(PIECES):
            gather_hop(p, s - 1, way[p]).wait_recv()
            gather_hop(p, s, way[p]).start()
    total[...] = jnp.zeros_like(total)
    lanes = (((1,), (1,)), ((), ()))

    def slopes_of(p):
        return side_by_side([slopes[p, :, k].reshape(HID, BS) for k in range(PB)])

    for p in range(PIECES):
        gather_hop(p, 2, way[p]).wait_recv()
        full = slopes_of(p)
        far = jnp.dot(wn_ref[...], full, preferred_element_type=F32)
        for k in range(PB):
            q = p * PB + k
            back[q] = (far[:, k * BS : (k + 1) * BS] * rdeg[block_at(q)][0:1]).astype(BF16)
        own = side_by_side([ext[block_at(p * PB + k)] for k in range(PB)])
        near = side_by_side([mean[p * PB + k] for k in range(PB)])
        total[0] += lax.dot_general(own, full, lanes, preferred_element_type=F32)
        total[1] += lax.dot_general(near, full, lanes, preferred_element_type=F32)
    for k in range(2):
        for c in range(2):
            at = (2 * k + c) * FC
            grads[at : at + FC] = total[k, :, c * BS : (c + 1) * BS].astype(BF16)

    def exchange(peer_at, count, src_of, dst, mine, send, recv):
        trips = []
        for k in range(1, count + 1):
            other, device = peer_at(k)
            trips.append(pltpu.make_async_remote_copy(
                src_ref=src_of(other), dst_ref=dst.at[mine], send_sem=send.at[k - 1], recv_sem=recv.at[k - 1],
                device_id=device, device_id_type=MESH,
            ))
        for trip in trips:
            trip.start()
        return trips

    def rows_a(k):
        return pl.ds(pl.multiple_of(k * SL_A, 32), SL_A)

    def rows_b(k):
        return pl.ds(pl.multiple_of(k * SL_B, 8), SL_B)

    trips = exchange(h_peer, 7, lambda k: grads.at[rows_a(k)], land_a, h, as_, ar)

    def backward_product(t):
        a = jnp.concatenate([vals[plan[4, 2 * t]], vals[plan[4, 2 * t + 1]]], axis=0)
        b = side_by_side([back[plan[5, 2 * t]], back[plan[5, 2 * t + 1]]])
        return jnp.dot(b, a, preferred_element_type=F32)

    def backward_step(i, acc):
        for u in range(GROUP):
            t = i * GROUP + u
            acc = acc * plan[6, 2 * t].astype(F32) + backward_product(t)
            sums[t] = acc
        return acc

    lax.fori_loop(0, PAIRS_B // GROUP, backward_step, jnp.zeros((FC, BS), F32))
    back_trips = []
    for q in range(4):
        for d, towards in ((0, v_left), (1, v_right)):
            for j in range(4 * q, 4 * q + 4):
                sent[d, j] = sums[plan[7, (HALO + NB) * d + j]].astype(BF16)
            trip = pltpu.make_async_remote_copy(
                src_ref=sent.at[d, pl.ds(4 * q, 4)], dst_ref=arrived.at[d, pl.ds(4 * q, 4)],
                send_sem=bs.at[d, q], recv_sem=br.at[d, q],
                device_id={"vtx": towards}, device_id_type=MESH,
            )
            trip.start()
            back_trips.append(trip)
    for trip in trips:
        trip.wait()
    land_a[h] = grads[rows_a(h)]
    sum_a[...] = jnp.sum(land_a[...].astype(F32), axis=0)
    trips = exchange(z_peer, 3, lambda k: sum_a.at[rows_b(k)], land_b, z, zs, zr)
    for b in range(NB):
        hidden[:, b * BS : (b + 1) * BS] = hid[plan[9, b]]
    outs = [plan_out, pltpu.make_async_copy(hidden, hidden_hbm, out_sem.at[1])]
    outs[1].start()
    for trip in trips:
        trip.wait()
    land_b[z] = sum_a[rows_b(z)]
    sum_b[z] = jnp.sum(land_b[...], axis=0) * float(NV * ROWS) ** -0.5
    trips = exchange(z_peer, 3, lambda k: sum_b.at[z], sum_b, z, cs, cr)
    for p in range(PIECES):
        near = jnp.dot(ws_ref[...], slopes_of(p), preferred_element_type=F32)
        for k in range(PB):
            part[p * PB + k, :FC] = near[:, k * BS : (k + 1) * BS]
    for trip in trips:
        trip.wait()
    whole[h] = sum_b[...].reshape(SL_A, BS)
    trips = exchange(h_peer, 7, lambda k: whole.at[h], whole, h, ds, dr)
    for c in range(4):
        for b in range(8 * c, 8 * c + 8):
            base[b] = part[plan[9, b], :FC] + sums[plan[7, HALO + b]]
        outs.append(pltpu.make_async_copy(base.at[pl.ds(8 * c, 8)], base_hbm.at[pl.ds(8 * c, 8)], out_sem.at[2 + c]))
        outs[-1].start()
    for trip in trips:
        trip.wait()
    outs.append(pltpu.make_async_copy(whole, grads_hbm, out_sem.at[6]))
    outs[-1].start()
    for trip in back_trips:
        trip.wait()
    for s in range(3):
        for p in range(PIECES):
            reduce_hop(p, s, way[p]).wait_send()
            gather_hop(p, s, way[p]).wait_send()
    for out in outs:
        out.wait()


def layer_call(rows, cols, count, lists, feat, cot, degree, ws, wn, bias, vals):
    dma = pltpu.SemaphoreType.DMA
    V = pltpu.VMEM
    return pl.pallas_call(
        layer_kernel,
        out_shape=(
            jax.ShapeDtypeStruct((HC, ROWS), BF16),
            jax.ShapeDtypeStruct((NB, FC, BS), F32),
            jax.ShapeDtypeStruct((2, HALO, FC, BS), BF16),
            jax.ShapeDtypeStruct((8, SL_A, BS), F32),
            jax.ShapeDtypeStruct((16, ENT), I32),
        ),
        in_specs=[anyspace(), anyspace(), smem()] + [anyspace()] * 4 + [vmem()] * 2 + [anyspace()] * 2,
        out_specs=(anyspace(),) * 5,
        scratch_shapes=[
            V((NNZ,), I32),
            V((NNZ,), I32),
            V((2 * HALO,), I32),
            V((HC,), F32),
            V((NB, BS), I32),
            V((NB, 8, BS), F32),
            V((8, BS), I32),
            V((2, 8, BS), I32),
            pltpu.SMEM((2, 8, BS), I32),
            V((16, ENT), I32),
            pltpu.SMEM((16, ENT), I32),
            V((EXT + 1, FC, BS), BF16),
            V((2, HALO, FC, BS), BF16),
            V((NB, HC, BS), BF16),
            V((NNZ + 1, BS, BS), BF16),
            V((PAIRS_B + 1, FC, BS), F32),
            V((2, HALO, FC, BS), BF16),
            V((NB, FC, BS), BF16),
            V((HID, FC), BF16),
            V((HID, FC), BF16),
            V((NB, HID, BS), F32),
            V((3, PIECES, PB, HC, BS), BF16),
            V((3, PIECES, PB, HC, BS), BF16),
            V((PIECES, NF, PB, HC, BS), BF16),
            V((NB, HC, BS), BF16),
            V((NB, FC, BS), BF16),
            V((NB, FC, BS), F32),
            V((HC, ROWS), BF16),
            V((2, FC, HID), F32),
            V((4 * FC, BS), BF16),
            V((8, SL_A, BS), BF16),
            V((SL_A, BS), F32),
            V((4, SL_B, BS), F32),
            V((4, SL_B, BS), F32),
            V((8, SL_A, BS), F32),
            dma((5,)), dma((NB,)), dma((NB,)), dma((8,)), dma, dma((2,)), dma((2,)), dma((2, 4)), dma((2, 4)),
            dma((6, PIECES)), dma((6, PIECES)), dma((2, 4)), dma((2, 4)),
            dma((7,)), dma((7,)), dma((3,)), dma((3,)), dma((3,)), dma((3,)), dma((7,)), dma((7,)), dma((7,)),
        ],
        compiler_params=pltpu.CompilerParams(collective_id=0, has_side_effects=True, vmem_limit_bytes=60 * MB),
        name="layer",
    )(rows, cols, count, lists, feat, cot, degree, ws, wn, bias, vals)


def results_kernel(
    plan_hbm, base_hbm, arrived_hbm, hidden_in, grads_hbm,
    hidden_out, features_hbm, self_ref, neigh_ref,
    plan, base, arrived, features, grads, sems,
):
    loads = [pltpu.make_async_copy(plan_hbm, plan, sems.at[0]), pltpu.make_async_copy(grads_hbm, grads, sems.at[1])]
    loads += [pltpu.make_async_copy(arrived_hbm.at[d], arrived.at[d, pl.ds(0, HALO)], sems.at[2 + d]) for d in range(2)]
    pieces = [
        pltpu.make_async_copy(base_hbm.at[pl.ds(8 * c, 8)], base.at[pl.ds(8 * c, 8)], sems.at[4 + c]) for c in range(4)
    ]
    copy = pltpu.make_async_copy(hidden_in, hidden_out, sems.at[8])
    for load in loads + pieces + [copy]:
        load.start()
    for d in range(2):
        arrived[d, HALO] = jnp.zeros((FC, BS), BF16)
    for load in loads:
        load.wait()
    outs = []
    for c in range(4):
        pieces[c].wait()
        for b in range(8 * c, 8 * c + 8):
            extra = arrived[0, plan[8, b]].astype(F32) + arrived[1, plan[8, BS + b]].astype(F32)
            features[:, b * BS : (b + 1) * BS] = (base[b] + extra).astype(BF16)
        at = pl.ds(8 * c * BS, 8 * BS)
        outs.append(pltpu.make_async_copy(features.at[:, at], features_hbm.at[:, at], sems.at[9 + c]))
        outs[-1].start()
    every = grads[...].reshape(4 * FC, BS)
    for k, ref in ((0, self_ref), (1, neigh_ref)):
        for c in range(2):
            at = (2 * k + c) * FC
            ref[:, c * BS : (c + 1) * BS] = every[at : at + FC]
    for out in outs + [copy]:
        out.wait()


def results_call(plan, base, arrived, hidden, grads):
    V = pltpu.VMEM
    return pl.pallas_call(
        results_kernel,
        out_shape=(
            jax.ShapeDtypeStruct((HC, ROWS), BF16),
            jax.ShapeDtypeStruct((FC, ROWS), BF16),
            jax.ShapeDtypeStruct((FC, HID), F32),
            jax.ShapeDtypeStruct((FC, HID), F32),
        ),
        in_specs=[anyspace()] * 5,
        out_specs=(anyspace(), anyspace(), vmem(), vmem()),
        scratch_shapes=[
            pltpu.SMEM((16, ENT), I32),
            V((NB, FC, BS), F32),
            V((2, HALO + 1, FC, BS), BF16),
            V((FC, ROWS), BF16),
            V((8, SL_A, BS), F32),
            pltpu.SemaphoreType.DMA((13,)),
        ],
        compiler_params=pltpu.CompilerParams(vmem_limit_bytes=48 * MB),
        name="results",
    )(plan, base, arrived, hidden, grads)


def on_device(
    features, w_self, w_neigh, bias_terms, block_vals, block_rows, block_cols, block_count, recv_lists, degree, cotangent
):
    hidden, base, arrived, grads, plan = layer_call(
        block_rows, block_cols, block_count, recv_lists, features.T, cotangent.T, degree.reshape(NB, BS),
        w_self, w_neigh, bias_terms, block_vals,
    )
    hidden, grad_features, grad_self, grad_neigh = results_call(plan, base, arrived, hidden, grads)
    return hidden.T, grad_features.T, grad_self, grad_neigh


def solution(mesh):
    placed = (
        P("vtx", "feat"), P("feat", None), P("feat", None), P("feat"), P("vtx", None, None), P("vtx"), P("vtx"), P("vtx"),
        P("vtx"), P("vtx"), P("vtx", "feat"),
    )
    return jax.shard_map(
        on_device,
        mesh=mesh,
        in_specs=placed,
        out_specs=(P("vtx", "feat"), P("vtx", "feat"), P("feat", None), P("feat", None)),
        check_vma=False,
    )
```

```python
import functools

import jax
import jax.numpy as jnp
from jax import lax
from jax.experimental import pallas as pl
from jax.experimental.pallas import tpu as pltpu
from jax.sharding import PartitionSpec as P

MESH = pl.DeviceIdType.MESH
F32, BF16, I32 = jnp.float32, jnp.bfloat16, jnp.int32
BS = 128
NB = 32
HALO = 16
NNZ = 320
EXT = NB + 2 * HALO
FC = 192
HID = 256
HC = 64
ROWS = NB * BS
NV, NF = 32, 4
ENT = 384
PIECES = 8
PB = NB // PIECES
PAIRS_F = (NNZ + NB) // 2
PAIRS_B = (NNZ + EXT) // 2
PIECE_PAIRS = PAIRS_F // PIECES
QUARTER = (NNZ + 2 * HALO) // 8
REST = PAIRS_B - 4 * QUARTER
ZERO = NB
SL_A = 4 * FC // 8
MB = 1 << 20


def vmem():
    return pl.BlockSpec(memory_space=pltpu.VMEM)


def smem():
    return pl.BlockSpec(memory_space=pltpu.SMEM)


def anyspace():
    return pl.BlockSpec(memory_space=pl.ANY)


def greet(peers):
    barrier = pltpu.get_barrier_semaphore()
    for peer in peers:
        pl.semaphore_signal(barrier, inc=1, device_id=peer, device_id_type=MESH)
    pl.semaphore_wait(barrier, len(peers))


def iota(shape, dim):
    return lax.broadcasted_iota(I32, shape, dim)


def as_column(row):
    n = row.shape[1]
    diagonal = iota((n, n), 0) == iota((n, n), 1)
    return jnp.sum(jnp.where(diagonal, row, jnp.zeros_like(row)), axis=1, keepdims=True, dtype=row.dtype)


def down(values):
    return jnp.sum(values, axis=0, keepdims=True, dtype=I32)


def group_sizes(key):
    size = jnp.sum(jnp.where(iota((EXT, ENT), 0) == key, 1, 0), axis=1, keepdims=True, dtype=I32)
    return ((size + 1) >> 1) << 1


def order_groups(key):
    block, lane = iota((EXT, ENT), 0), iota((EXT, ENT), 1)
    size = group_sizes(key)
    size_row = down(jnp.where(block == lane, size, 0))
    earlier = (size < size_row) | ((size == size_row) & (block < lane))
    place = down(jnp.where(earlier & (block < NB), 1, 0))
    place_col = as_column(place)[:EXT]
    at_place = down(jnp.where((place_col == lane) & (block < NB), block, 0))
    of_entry = down(jnp.where(block == key, place_col, 0))
    return place, at_place, of_entry


def order_slots(key):
    slot, lane = iota((EXT, ENT), 0), iota((EXT, ENT), 1)
    size = group_sizes(key)
    size_row = down(jnp.where(slot == lane, size, 0))
    earlier = (size < size_row) | ((size == size_row) & (slot < lane))
    side = jnp.where(slot < HALO, 0, jnp.where(slot < HALO + NB, 1, 2))
    lane_side = jnp.where(lane < HALO, 0, jnp.where(lane < HALO + NB, 1, 2))
    at_side = as_column(down(jnp.where(earlier & (side == lane_side), 1, 0)))[:EXT]
    slot, side = slot[:, :1], side[:, :1]
    turn = ((at_side >> 2) << 3) + (at_side & 3)
    order = jnp.where(side == 1, 2 * HALO + slot - HALO, turn + jnp.where(side == 2, 4, 0))
    of_entry = down(jnp.where(iota((EXT, ENT), 0) == key, order, 0))
    told = iota((EXT, BS), 1)
    told = jnp.where(told < HALO, told, told + NB)
    return of_entry, down(jnp.where(iota((EXT, BS), 0) == told, at_side, 0))


def pair_schedule(key, other, active):
    far = 1000
    sub, lane = iota((ENT, ENT), 0), iota((ENT, ENT), 1)
    key = jnp.where(active, key, far)
    key_col = as_column(key)
    rank = down(jnp.where((key_col == key) & (sub < lane), 1, 0))
    group, at = iota((EXT, ENT), 0), iota((EXT, ENT), 1)
    size = group_sizes(key)
    start = down(jnp.where(group < key, size, 0))
    slot = jnp.where(active, start + rank, far)
    hit = as_column(slot) == lane

    def at_slots(column, default):
        return down(jnp.where(hit, column - default, 0)) + default

    entry = at_slots(sub[:, :1], NNZ)
    source = at_slots(as_column(other), 0)
    goes_on = jnp.minimum(at_slots(as_column(rank), 1), 1)
    end = down(jnp.where(group <= at, size, 0))
    own = down(jnp.where(group == at, size, 0))
    done = jnp.where(own > 0, (end >> 1) - 1, PAIRS_B)
    return [jnp.clip(entry, 0, NNZ), jnp.clip(source, 0, EXT), goes_on, jnp.clip(done, 0, PAIRS_B)]


def inverse(lists, places, first):
    ours, place = as_column(lists), as_column(places)
    sub, lane = iota((BS, BS), 0), iota((BS, BS), 1)
    hit = (ours == lane) & (sub >= first) & (sub < first + HALO)
    return jnp.clip(down(jnp.where(hit, place - HALO, 0)) + HALO, 0, HALO)


def layer_kernel(
    rows_hbm, cols_hbm, count_ref, lists_hbm, feat_hbm, cot_hbm, degree_hbm, ws_ref, wn_ref, bias_hbm, vals_hbm,
    hidden_hbm, base_hbm, arrived, grads_hbm, plan_hbm,
    rows_v, cols_v, lists_v, bias_v, degree_v, rdeg, lists_out, lists_in, lists_sm, places_out, places_in, plan_v, plan,
    ext, landed_halo, cot, vals, sums, sent, mean, wst, wnt, part, staged, landed, slopes, hid, back, base, hidden,
    total, grads, land_a, sum_a, whole,
    small_sem, feat_sem, cot_sem, vals_sem, sm_sem, ls, lr, hs, hr,
    send_sem, recv_sem, bs, br, as_, ar, zs, zr, ds, dr, out_sem,
):
    me = lax.axis_index("feat")
    right, left = lax.rem(me + 1, NF), lax.rem(me + NF - 1, NF)
    v = lax.axis_index("vtx")
    v_right, v_left = lax.rem(v + 1, NV), lax.rem(v + NV - 1, NV)
    core, x, z = lax.rem(v, 2), lax.rem(v // 2, 4), v // 8
    g = 2 * z + core

    def g_peer(k):
        other = lax.rem(g + k, 8)
        return other, {"vtx": ((other // 2) * 4 + x) * 2 + lax.rem(other, 2)}

    def x_peer(k):
        other = lax.rem(x + k, 4)
        return other, {"vtx": (z * 4 + other) * 2 + core}

    small = [
        pltpu.make_async_copy(src, dst, small_sem.at[k])
        for k, (src, dst) in enumerate(
            [(lists_hbm, lists_v), (rows_hbm, rows_v), (cols_hbm, cols_v), (bias_hbm, bias_v), (degree_hbm, degree_v)]
        )
    ]
    feat_loads = [
        pltpu.make_async_copy(feat_hbm.at[:, pl.ds(b * BS, BS)], ext.at[b], feat_sem.at[b]) for b in range(NB)
    ]
    cot_loads = [
        pltpu.make_async_copy(cot_hbm.at[:, pl.ds(b * BS, BS)], cot.at[b], cot_sem.at[b]) for b in range(NB)
    ]
    share = NNZ // 8
    val_loads = [
        pltpu.make_async_copy(vals_hbm.at[pl.ds(k * share, share)], vals.at[pl.ds(k * share, share)], vals_sem.at[k])
        for k in range(8)
    ]
    for load in small + feat_loads:
        load.start()
    barrier = pltpu.get_barrier_semaphore()
    peers = (
        [{"vtx": v_left}, {"vtx": v_right}, {"feat": left}, {"feat": right}]
        + [g_peer(k)[1] for k in range(1, 8)]
        + [x_peer(k)[1] for k in range(1, 4)]
    )
    for peer in peers:
        pl.semaphore_signal(barrier, inc=1, device_id=peer, device_id_type=MESH)
    for load in val_loads + cot_loads:
        load.start()
    small[0].wait()
    lists_out[...] = jnp.full((8, BS), -1, I32)
    lists_out[0:1, : 2 * HALO] = lists_v[...].reshape(1, 2 * HALO)
    ext[ZERO] = jnp.zeros((FC, BS), BF16)
    vals[NNZ] = jnp.zeros((BS, BS), BF16)
    sums[PAIRS_B] = jnp.zeros((FC, BS), F32)
    pl.semaphore_wait(barrier, len(peers))

    trips = []
    for k, peer in ((0, v_right), (1, v_left)):
        trip = pltpu.make_async_remote_copy(
            src_ref=lists_out, dst_ref=lists_in.at[k], send_sem=ls.at[k], recv_sem=lr.at[k],
            device_id={"vtx": peer}, device_id_type=MESH,
        )
        trip.start()
        trips.append(trip)
    for load in small[1:] + feat_loads:
        load.wait()
    wst[...] = ws_ref[...].T
    wnt[...] = wn_ref[...].T
    bias = as_column(bias_v[...].reshape(1, HC))
    for b in range(NB):
        rdeg[b] = jnp.broadcast_to(1.0 / degree_v[b : b + 1, :].astype(F32), (8, BS))
    for trip in trips:
        trip.wait()
    local = pltpu.make_async_copy(lists_in, lists_sm, sm_sem)
    local.start()
    local.wait()
    halo_trips = []
    for q in range(4):
        for d in range(2):
            for j in range(4 * q, 4 * q + 4):
                sent[d, j] = ext[lax.rem(lists_sm[1 - d, 0, j + HALO * d] + NB + 1, NB + 1)]
            trip = pltpu.make_async_remote_copy(
                src_ref=sent.at[d, pl.ds(4 * q, 4)], dst_ref=landed_halo.at[d, pl.ds(4 * q, 4)],
                send_sem=hs.at[d, q], recv_sem=hr.at[d, q],
                device_id={"vtx": v_right if d == 0 else v_left}, device_id_type=MESH,
            )
            trip.start()
            halo_trips.append(trip)

    def wide(ref):
        return jnp.concatenate([ref[...].reshape(1, NNZ), jnp.zeros((1, ENT - NNZ), I32)], axis=1)

    rows, cols = wide(rows_v), wide(cols_v)
    active = iota((1, ENT), 1) < count_ref[0]
    where_col = jnp.where(cols < HALO, cols + NB + 1, jnp.where(cols < HALO + NB, cols - HALO, cols + 1))
    slot_place, places = order_slots(jnp.where(active, cols, 1000))
    places_out[...] = jnp.broadcast_to(places, (8, BS))
    place_trips = []
    for k, peer in ((0, v_right), (1, v_left)):
        trip = pltpu.make_async_remote_copy(
            src_ref=places_out, dst_ref=places_in.at[k], send_sem=ls.at[2 + k], recv_sem=lr.at[2 + k],
            device_id={"vtx": peer}, device_id_type=MESH,
        )
        trip.start()
        place_trips.append(trip)
    place, at_place, entry_place = order_groups(jnp.where(active, rows, 1000))
    table = pair_schedule(entry_place, where_col, active) + pair_schedule(slot_place, entry_place, active)
    table += [jnp.zeros((1, ENT), I32), jnp.clip(place, 0, NB - 1), jnp.clip(at_place, 0, NB - 1)]
    for k, row in enumerate(table):
        plan_v[k : k + 1] = row
    for k in range(len(table), 16):
        plan_v[k : k + 1] = jnp.zeros((1, ENT), I32)
    local = pltpu.make_async_copy(plan_v, plan, sm_sem)
    local.start()
    local.wait()

    def block_at(q):
        return plan[10, q]

    def side_by_side(blocks):
        return jnp.concatenate(blocks, axis=1)

    for p in range(PIECES):
        own = side_by_side([ext[block_at(p * PB + k)] for k in range(PB)])
        pre = jnp.dot(wst[...], own, preferred_element_type=F32)
        for k in range(PB):
            part[p * PB + k] = pre[:, k * BS : (k + 1) * BS]
    for trip in place_trips:
        trip.wait()
    from_right = inverse(lists_in[1, 0:1], places_in[1, 0:1], 0)
    from_left = inverse(lists_in[0, 0:1], places_in[0, 0:1], HALO)
    plan_v[8:9] = jnp.concatenate([from_right, from_left, jnp.zeros((1, BS), I32)], axis=1)
    plan_out = pltpu.make_async_copy(plan_v, plan_hbm, out_sem.at[0])
    plan_out.start()
    for load in val_loads + cot_loads:
        load.wait()
    for trip in halo_trips:
        trip.wait()
    for d in range(2):
        for j in range(HALO):
            ext[NB + 1 + HALO * d + j] = landed_halo[d, j]

    way = {p: 1 - 2 * (p % 2) for p in range(PIECES)}
    peer_of = {1: right, -1: left}

    def chunk(w, back_by):
        return lax.rem(me - w * back_by + 2 * NF, NF)

    def reduce_hop(p, s, w):
        return pltpu.make_async_remote_copy(
            src_ref=staged.at[s, p], dst_ref=landed.at[s, p],
            send_sem=send_sem.at[s, p], recv_sem=recv_sem.at[s, p],
            device_id={"feat": peer_of[w]}, device_id_type=MESH,
        )

    def gather_hop(p, s, w):
        owner = chunk(w, s)
        return pltpu.make_async_remote_copy(
            src_ref=slopes.at[p, owner], dst_ref=slopes.at[p, owner],
            send_sem=send_sem.at[3 + s, p], recv_sem=recv_sem.at[3 + s, p],
            device_id={"feat": peer_of[w]}, device_id_type=MESH,
        )

    def chunk_rows(c):
        return pl.ds(pl.multiple_of(c * HC, HC), HC)

    def forward_product(t):
        a = side_by_side([vals[plan[0, 2 * t]], vals[plan[0, 2 * t + 1]]])
        x = side_by_side([ext[plan[1, 2 * t]], ext[plan[1, 2 * t + 1]]])
        return lax.dot_general(x, a, (((1,), (1,)), ((), ())), preferred_element_type=F32)

    def reduce_on(p, s, w):
        reduce_hop(p, s - 1, w).wait_recv()
        for k in range(PB):
            more = part[p * PB + k, chunk_rows(chunk(w, 1 + s))]
            staged[s, p, k] = (landed[s - 1, p, k].astype(F32) + more).astype(BF16)
        reduce_hop(p, s, w).start()

    def forward_pieces(i, acc):
        for w in (1, -1):
            p = 2 * i + (0 if w == 1 else 1)
            for u in range(PIECE_PAIRS):
                t = p * PIECE_PAIRS + u
                acc = acc * plan[2, 2 * t].astype(F32) + forward_product(t)
                sums[t] = acc
            for k in range(PB):
                q = p * PB + k
                scale = rdeg[block_at(q)][0:1]
                mean[q] = (sums[plan[3, q]] * scale).astype(BF16)
            pre = jnp.dot(wnt[...], side_by_side([mean[p * PB + k] for k in range(PB)]), preferred_element_type=F32)
            for k in range(PB):
                q = p * PB + k
                part[q] = part[q] + pre[:, k * BS : (k + 1) * BS]
                staged[0, p, k] = part[q, chunk_rows(chunk(w, 1))].astype(BF16)
            reduce_hop(p, 0, w).start()
        return acc

    acc = forward_pieces(0, jnp.zeros((FC, BS), F32))

    def forward_step(i, acc):
        acc = forward_pieces(i, acc)
        for w in (1, -1):
            reduce_on(2 * i - 2 + (0 if w == 1 else 1), 1, w)
        return acc

    lax.fori_loop(1, PIECES // 2, forward_step, acc)
    for p in (PIECES - 2, PIECES - 1):
        reduce_on(p, 1, way[p])
    for p in range(PIECES):
        reduce_on(p, 2, way[p])
    for p in range(PIECES):
        reduce_hop(p, 2, way[p]).wait_recv()
        for k in range(PB):
            q = p * PB + k
            pre = landed[2, p, k].astype(F32) + part[q, chunk_rows(me)] + bias
            squash = 1.0 / (1.0 + jnp.exp(-pre))
            hid[q] = (pre * squash).astype(BF16)
            slope = cot[block_at(q)].astype(F32) * squash * (1.0 + pre * (1.0 - squash))
            slopes[p, me, k] = slope.astype(BF16)
        gather_hop(p, 0, way[p]).start()
    for s in range(1, 3):
        for p in range(PIECES):
            gather_hop(p, s - 1, way[p]).wait_recv()
            gather_hop(p, s, way[p]).start()
    total[...] = jnp.zeros_like(total)
    lanes = (((1,), (1,)), ((), ()))

    def slopes_of(p):
        return side_by_side([slopes[p, :, k].reshape(HID, BS) for k in range(PB)])

    for p in range(PIECES):
        gather_hop(p, 2, way[p]).wait_recv()
        full = slopes_of(p)
        far = jnp.dot(wn_ref[...], full, preferred_element_type=F32)
        for k in range(PB):
            q = p * PB + k
            back[q] = (far[:, k * BS : (k + 1) * BS] * rdeg[block_at(q)][0:1]).astype(BF16)
        own = side_by_side([ext[block_at(p * PB + k)] for k in range(PB)])
        near = side_by_side([mean[p * PB + k] for k in range(PB)])
        total[0] += lax.dot_general(own, full, lanes, preferred_element_type=F32)
        total[1] += lax.dot_general(near, full, lanes, preferred_element_type=F32)
    for k in range(2):
        for c in range(2):
            at = (2 * k + c) * FC
            grads[at : at + FC] = total[k, :, c * BS : (c + 1) * BS].astype(BF16)

    def exchange(peer_at, count, src_of, dst, mine, send, recv):
        trips = []
        for k in range(1, count + 1):
            other, device = peer_at(k)
            trips.append(pltpu.make_async_remote_copy(
                src_ref=src_of(other), dst_ref=dst.at[mine], send_sem=send.at[k - 1], recv_sem=recv.at[k - 1],
                device_id=device, device_id_type=MESH,
            ))
        for trip in trips:
            trip.start()
        return trips

    def rows_a(k):
        return pl.ds(pl.multiple_of(k * SL_A, 32), SL_A)

    a_trips = exchange(g_peer, 7, lambda k: grads.at[rows_a(k)], land_a, g, as_, ar)

    def backward_pair(t, acc):
        a = jnp.concatenate([vals[plan[4, 2 * t]], vals[plan[4, 2 * t + 1]]], axis=0)
        b = side_by_side([back[plan[5, 2 * t]], back[plan[5, 2 * t + 1]]])
        acc = acc * plan[6, 2 * t].astype(F32) + jnp.dot(b, a, preferred_element_type=F32)
        sums[t] = acc
        return acc

    def back_hop(q, d):
        return pltpu.make_async_remote_copy(
            src_ref=sent.at[d, pl.ds(4 * q, 4)], dst_ref=arrived.at[d, pl.ds(4 * q, 4)],
            send_sem=bs.at[d, q], recv_sem=br.at[d, q],
            device_id={"vtx": v_right if d else v_left}, device_id_type=MESH,
        )

    def backward_quarter(q, acc):
        for u in range(QUARTER):
            acc = backward_pair(q * QUARTER + u, acc)
        for d in range(2):
            for j in range(4):
                sent[d, 4 * q + j] = sums[plan[7, 8 * q + 4 * d + j]].astype(BF16)
            back_hop(q, d).start()
        return acc

    acc = lax.fori_loop(0, 3, backward_quarter, jnp.zeros((FC, BS), F32))
    for trip in a_trips:
        trip.wait()
    land_a[g] = grads[rows_a(g)]
    sum_a[x] = jnp.sum(land_a[...].astype(F32), axis=0)
    x_trips = exchange(x_peer, 3, lambda k: sum_a.at[x], sum_a, x, zs, zr)
    acc = backward_quarter(3, acc)
    for u in range(REST):
        acc = backward_pair(4 * QUARTER + u, acc)
    for b in range(NB):
        hidden[:, b * BS : (b + 1) * BS] = hid[plan[9, b]]
    outs = [plan_out, pltpu.make_async_copy(hidden, hidden_hbm, out_sem.at[1])]
    outs[1].start()
    for trip in x_trips:
        trip.wait()
    whole[...] = jnp.sum(sum_a[...], axis=0) * float(NV * ROWS) ** -0.5
    d_trips = exchange(g_peer, 7, lambda k: whole, grads_hbm, g, ds, dr)
    outs.append(pltpu.make_async_copy(whole, grads_hbm.at[g], out_sem.at[6]))
    outs[-1].start()
    for p in range(PIECES):
        near = jnp.dot(ws_ref[...], slopes_of(p), preferred_element_type=F32)
        for k in range(PB):
            part[p * PB + k, :FC] = near[:, k * BS : (k + 1) * BS]
    for c in range(4):
        for b in range(8 * c, 8 * c + 8):
            base[b] = part[plan[9, b], :FC] + sums[plan[7, 2 * HALO + b]]
        outs.append(pltpu.make_async_copy(base.at[pl.ds(8 * c, 8)], base_hbm.at[pl.ds(8 * c, 8)], out_sem.at[2 + c]))
        outs[-1].start()
    for s in range(3):
        for p in range(PIECES):
            reduce_hop(p, s, way[p]).wait_send()
            gather_hop(p, s, way[p]).wait_send()
    for out in outs:
        out.wait()
    for q in range(4):
        for d in range(2):
            back_hop(q, d).wait()
    for trip in d_trips:
        trip.wait()


def layer_call(rows, cols, count, lists, feat, cot, degree, ws, wn, bias, vals):
    dma = pltpu.SemaphoreType.DMA
    V = pltpu.VMEM
    return pl.pallas_call(
        layer_kernel,
        out_shape=(
            jax.ShapeDtypeStruct((HC, ROWS), BF16),
            jax.ShapeDtypeStruct((NB, FC, BS), F32),
            jax.ShapeDtypeStruct((2, HALO, FC, BS), BF16),
            jax.ShapeDtypeStruct((8, SL_A, BS), F32),
            jax.ShapeDtypeStruct((16, ENT), I32),
        ),
        in_specs=[anyspace(), anyspace(), smem()] + [anyspace()] * 4 + [vmem()] * 2 + [anyspace()] * 2,
        out_specs=(anyspace(),) * 5,
        scratch_shapes=[
            V((NNZ,), I32),
            V((NNZ,), I32),
            V((2 * HALO,), I32),
            V((HC,), F32),
            V((NB, BS), I32),
            V((NB, 8, BS), F32),
            V((8, BS), I32),
            V((2, 8, BS), I32),
            pltpu.SMEM((2, 8, BS), I32),
            V((8, BS), I32),
            V((2, 8, BS), I32),
            V((16, ENT), I32),
            pltpu.SMEM((16, ENT), I32),
            V((EXT + 1, FC, BS), BF16),
            V((2, HALO, FC, BS), BF16),
            V((NB, HC, BS), BF16),
            V((NNZ + 1, BS, BS), BF16),
            V((PAIRS_B + 1, FC, BS), F32),
            V((2, HALO, FC, BS), BF16),
            V((NB, FC, BS), BF16),
            V((HID, FC), BF16),
            V((HID, FC), BF16),
            V((NB, HID, BS), F32),
            V((3, PIECES, PB, HC, BS), BF16),
            V((3, PIECES, PB, HC, BS), BF16),
            V((PIECES, NF, PB, HC, BS), BF16),
            V((NB, HC, BS), BF16),
            V((NB, FC, BS), BF16),
            V((NB, FC, BS), F32),
            V((HC, ROWS), BF16),
            V((2, FC, HID), F32),
            V((4 * FC, BS), BF16),
            V((8, SL_A, BS), BF16),
            V((4, SL_A, BS), F32),
            V((SL_A, BS), F32),
            dma((5,)), dma((NB,)), dma((NB,)), dma((8,)), dma, dma((4,)), dma((4,)), dma((2, 4)), dma((2, 4)),
            dma((6, PIECES)), dma((6, PIECES)), dma((2, 4)), dma((2, 4)),
            dma((7,)), dma((7,)), dma((3,)), dma((3,)), dma((7,)), dma((7,)), dma((7,)),
        ],
        compiler_params=pltpu.CompilerParams(collective_id=0, has_side_effects=True, vmem_limit_bytes=60 * MB),
        name="layer",
    )(rows, cols, count, lists, feat, cot, degree, ws, wn, bias, vals)


def results_kernel(
    plan_hbm, base_hbm, arrived_hbm, hidden_in, grads_hbm,
    hidden_out, features_hbm, self_ref, neigh_ref,
    plan, base, arrived, features, grads, sems,
):
    loads = [pltpu.make_async_copy(plan_hbm, plan, sems.at[0]), pltpu.make_async_copy(grads_hbm, grads, sems.at[1])]
    loads += [pltpu.make_async_copy(arrived_hbm.at[d], arrived.at[d, pl.ds(0, HALO)], sems.at[2 + d]) for d in range(2)]
    pieces = [
        pltpu.make_async_copy(base_hbm.at[pl.ds(8 * c, 8)], base.at[pl.ds(8 * c, 8)], sems.at[4 + c]) for c in range(4)
    ]
    copy = pltpu.make_async_copy(hidden_in, hidden_out, sems.at[8])
    for load in loads + pieces + [copy]:
        load.start()
    for d in range(2):
        arrived[d, HALO] = jnp.zeros((FC, BS), BF16)
    for load in loads:
        load.wait()
    outs = []
    for c in range(4):
        pieces[c].wait()
        for b in range(8 * c, 8 * c + 8):
            extra = arrived[0, plan[8, b]].astype(F32) + arrived[1, plan[8, BS + b]].astype(F32)
            features[:, b * BS : (b + 1) * BS] = (base[b] + extra).astype(BF16)
        at = pl.ds(8 * c * BS, 8 * BS)
        outs.append(pltpu.make_async_copy(features.at[:, at], features_hbm.at[:, at], sems.at[9 + c]))
        outs[-1].start()
    every = grads[...].reshape(4 * FC, BS)
    for k, ref in ((0, self_ref), (1, neigh_ref)):
        for c in range(2):
            at = (2 * k + c) * FC
            ref[:, c * BS : (c + 1) * BS] = every[at : at + FC]
    for out in outs + [copy]:
        out.wait()


def results_call(plan, base, arrived, hidden, grads):
    V = pltpu.VMEM
    return pl.pallas_call(
        results_kernel,
        out_shape=(
            jax.ShapeDtypeStruct((HC, ROWS), BF16),
            jax.ShapeDtypeStruct((FC, ROWS), BF16),
            jax.ShapeDtypeStruct((FC, HID), F32),
            jax.ShapeDtypeStruct((FC, HID), F32),
        ),
        in_specs=[anyspace()] * 5,
        out_specs=(anyspace(), anyspace(), vmem(), vmem()),
        scratch_shapes=[
            pltpu.SMEM((16, ENT), I32),
            V((NB, FC, BS), F32),
            V((2, HALO + 1, FC, BS), BF16),
            V((FC, ROWS), BF16),
            V((8, SL_A, BS), F32),
            pltpu.SemaphoreType.DMA((13,)),
        ],
        compiler_params=pltpu.CompilerParams(vmem_limit_bytes=60 * MB),
        name="results",
    )(plan, base, arrived, hidden, grads)


def on_device(
    features, w_self, w_neigh, bias_terms, block_vals, block_rows, block_cols, block_count, recv_lists, degree, cotangent
):
    hidden, base, arrived, grads, plan = layer_call(
        block_rows, block_cols, block_count, recv_lists, features.T, cotangent.T, degree.reshape(NB, BS),
        w_self, w_neigh, bias_terms, block_vals,
    )
    hidden, grad_features, grad_self, grad_neigh = results_call(plan, base, arrived, hidden, grads)
    return hidden.T, grad_features.T, grad_self, grad_neigh


def solution(mesh):
    placed = (
        P("vtx", "feat"), P("feat", None), P("feat", None), P("feat"), P("vtx", None, None), P("vtx"), P("vtx"), P("vtx"),
        P("vtx"), P("vtx"), P("vtx", "feat"),
    )
    return jax.shard_map(
        on_device,
        mesh=mesh,
        in_specs=placed,
        out_specs=(P("vtx", "feat"), P("vtx", "feat"), P("feat", None), P("feat", None)),
        check_vma=False,
    )
```

```python
import functools

import jax
import jax.numpy as jnp
from jax import lax
from jax.experimental import pallas as pl
from jax.experimental.pallas import tpu as pltpu
from jax.sharding import PartitionSpec as P

MESH = pl.DeviceIdType.MESH
F32, BF16, I32 = jnp.float32, jnp.bfloat16, jnp.int32
BS = 128
NB = 32
HALO = 16
NNZ = 320
EXT = NB + 2 * HALO
FC = 192
HID = 256
HC = 64
ROWS = NB * BS
NV, NF = 32, 4
ENT = 384
PIECES = 8
PB = NB // PIECES
PAIRS_F = (NNZ + NB) // 2
PAIRS_B = (NNZ + EXT) // 2
PIECE_PAIRS = PAIRS_F // PIECES
QUARTER = (NNZ + 2 * HALO) // 8
REST = PAIRS_B - 4 * QUARTER
ZERO = NB
SL_A = 4 * FC // 8
MB = 1 << 20


def vmem():
    return pl.BlockSpec(memory_space=pltpu.VMEM)


def smem():
    return pl.BlockSpec(memory_space=pltpu.SMEM)


def anyspace():
    return pl.BlockSpec(memory_space=pl.ANY)


def greet(peers):
    barrier = pltpu.get_barrier_semaphore()
    for peer in peers:
        pl.semaphore_signal(barrier, inc=1, device_id=peer, device_id_type=MESH)
    pl.semaphore_wait(barrier, len(peers))


def iota(shape, dim):
    return lax.broadcasted_iota(I32, shape, dim)


def as_column(row):
    n = row.shape[1]
    diagonal = iota((n, n), 0) == iota((n, n), 1)
    return jnp.sum(jnp.where(diagonal, row, jnp.zeros_like(row)), axis=1, keepdims=True, dtype=row.dtype)


def down(values):
    return jnp.sum(values, axis=0, keepdims=True, dtype=I32)


def group_sizes(key):
    size = jnp.sum(jnp.where(iota((EXT, ENT), 0) == key, 1, 0), axis=1, keepdims=True, dtype=I32)
    return ((size + 1) >> 1) << 1


def order_groups(key):
    block, lane = iota((EXT, ENT), 0), iota((EXT, ENT), 1)
    size = group_sizes(key)
    size_row = down(jnp.where(block == lane, size, 0))
    earlier = (size < size_row) | ((size == size_row) & (block < lane))
    place = down(jnp.where(earlier & (block < NB), 1, 0))
    place_col = as_column(place)[:EXT]
    at_place = down(jnp.where((place_col == lane) & (block < NB), block, 0))
    of_entry = down(jnp.where(block == key, place_col, 0))
    return place, at_place, of_entry


def order_slots(key):
    slot, lane = iota((EXT, ENT), 0), iota((EXT, ENT), 1)
    size = group_sizes(key)
    size_row = down(jnp.where(slot == lane, size, 0))
    earlier = (size < size_row) | ((size == size_row) & (slot < lane))
    side = jnp.where(slot < HALO, 0, jnp.where(slot < HALO + NB, 1, 2))
    lane_side = jnp.where(lane < HALO, 0, jnp.where(lane < HALO + NB, 1, 2))
    at_side = as_column(down(jnp.where(earlier & (side == lane_side), 1, 0)))[:EXT]
    slot, side = slot[:, :1], side[:, :1]
    turn = ((at_side >> 2) << 3) + (at_side & 3)
    order = jnp.where(side == 1, 2 * HALO + slot - HALO, turn + jnp.where(side == 2, 4, 0))
    of_entry = down(jnp.where(iota((EXT, ENT), 0) == key, order, 0))
    told = iota((EXT, BS), 1)
    told = jnp.where(told < HALO, told, told + NB)
    return of_entry, down(jnp.where(iota((EXT, BS), 0) == told, at_side, 0))


def pair_schedule(key, other, active):
    far = 1000
    sub, lane = iota((ENT, ENT), 0), iota((ENT, ENT), 1)
    key = jnp.where(active, key, far)
    key_col = as_column(key)
    rank = down(jnp.where((key_col == key) & (sub < lane), 1, 0))
    group, at = iota((EXT, ENT), 0), iota((EXT, ENT), 1)
    size = group_sizes(key)
    start = down(jnp.where(group < key, size, 0))
    slot = jnp.where(active, start + rank, far)
    hit = as_column(slot) == lane

    def at_slots(column, default):
        return down(jnp.where(hit, column - default, 0)) + default

    entry = at_slots(sub[:, :1], NNZ)
    source = at_slots(as_column(other), 0)
    goes_on = jnp.minimum(at_slots(as_column(rank), 1), 1)
    end = down(jnp.where(group <= at, size, 0))
    own = down(jnp.where(group == at, size, 0))
    done = jnp.where(own > 0, (end >> 1) - 1, PAIRS_B)
    return [jnp.clip(entry, 0, NNZ), jnp.clip(source, 0, EXT), goes_on, jnp.clip(done, 0, PAIRS_B)]


def inverse(lists, places, first):
    ours, place = as_column(lists), as_column(places)
    sub, lane = iota((BS, BS), 0), iota((BS, BS), 1)
    hit = (ours == lane) & (sub >= first) & (sub < first + HALO)
    return jnp.clip(down(jnp.where(hit, place - HALO, 0)) + HALO, 0, HALO)


def layer_kernel(
    rows_hbm, cols_hbm, count_ref, lists_hbm, feat_hbm, cot_hbm, degree_hbm, ws_ref, wn_ref, bias_hbm, vals_hbm,
    hidden_hbm, base_hbm, arrived, grads_hbm, plan_hbm,
    rows_v, cols_v, lists_v, bias_v, degree_v, rdeg, lists_out, lists_in, lists_sm, places_out, places_in, plan_v, plan,
    ext, landed_halo, cot, vals, sums, sent, mean, wst, wnt, part, staged, landed, slopes, hid, back, base, hidden,
    total, grads, land_a, sum_a, whole,
    small_sem, feat_sem, cot_sem, vals_sem, sm_sem, ls, lr, hs, hr,
    send_sem, recv_sem, bs, br, as_, ar, zs, zr, ds, dr, out_sem,
):
    me = lax.axis_index("feat")
    right, left = lax.rem(me + 1, NF), lax.rem(me + NF - 1, NF)
    v = lax.axis_index("vtx")
    v_right, v_left = lax.rem(v + 1, NV), lax.rem(v + NV - 1, NV)
    core, x, z = lax.rem(v, 2), lax.rem(v // 2, 4), v // 8
    g = 2 * z + core

    def g_peer(k):
        other = lax.rem(g + k, 8)
        return other, {"vtx": ((other // 2) * 4 + x) * 2 + lax.rem(other, 2)}

    def x_peer(k):
        other = lax.rem(x + k, 4)
        return other, {"vtx": (z * 4 + other) * 2 + core}

    small = [
        pltpu.make_async_copy(src, dst, small_sem.at[k])
        for k, (src, dst) in enumerate(
            [(lists_hbm, lists_v), (rows_hbm, rows_v), (cols_hbm, cols_v), (bias_hbm, bias_v), (degree_hbm, degree_v)]
        )
    ]
    feat_loads = [
        pltpu.make_async_copy(feat_hbm.at[:, pl.ds(b * BS, BS)], ext.at[b], feat_sem.at[b]) for b in range(NB)
    ]
    cot_loads = [
        pltpu.make_async_copy(cot_hbm.at[:, pl.ds(b * BS, BS)], cot.at[b], cot_sem.at[b]) for b in range(NB)
    ]
    share = NNZ // 8
    val_loads = [
        pltpu.make_async_copy(vals_hbm.at[pl.ds(k * share, share)], vals.at[pl.ds(k * share, share)], vals_sem.at[k])
        for k in range(8)
    ]
    for load in small + feat_loads:
        load.start()
    barrier = pltpu.get_barrier_semaphore()
    peers = (
        [{"vtx": v_left}, {"vtx": v_right}, {"feat": left}, {"feat": right}]
        + [g_peer(k)[1] for k in range(1, 8)]
        + [x_peer(k)[1] for k in range(1, 4)]
    )
    for peer in peers:
        pl.semaphore_signal(barrier, inc=1, device_id=peer, device_id_type=MESH)
    for load in val_loads + cot_loads:
        load.start()
    small[0].wait()
    lists_out[...] = jnp.full((8, BS), -1, I32)
    lists_out[0:1, : 2 * HALO] = lists_v[...].reshape(1, 2 * HALO)
    ext[ZERO] = jnp.zeros((FC, BS), BF16)
    vals[NNZ] = jnp.zeros((BS, BS), BF16)
    sums[PAIRS_B] = jnp.zeros((FC, BS), F32)
    pl.semaphore_wait(barrier, len(peers))

    trips = []
    for k, peer in ((0, v_right), (1, v_left)):
        trip = pltpu.make_async_remote_copy(
            src_ref=lists_out, dst_ref=lists_in.at[k], send_sem=ls.at[k], recv_sem=lr.at[k],
            device_id={"vtx": peer}, device_id_type=MESH,
        )
        trip.start()
        trips.append(trip)
    for load in small[1:] + feat_loads:
        load.wait()
    wst[...] = ws_ref[...].T
    wnt[...] = wn_ref[...].T
    bias = as_column(bias_v[...].reshape(1, HC))
    for b in range(NB):
        rdeg[b] = jnp.broadcast_to(1.0 / degree_v[b : b + 1, :].astype(F32), (8, BS))
    for trip in trips:
        trip.wait()
    local = pltpu.make_async_copy(lists_in, lists_sm, sm_sem)
    local.start()
    local.wait()
    halo_trips = []
    for q in range(4):
        for d in range(2):
            for j in range(4 * q, 4 * q + 4):
                sent[d, j] = ext[lax.rem(lists_sm[1 - d, 0, j + HALO * d] + NB + 1, NB + 1)]
            trip = pltpu.make_async_remote_copy(
                src_ref=sent.at[d, pl.ds(4 * q, 4)], dst_ref=landed_halo.at[d, pl.ds(4 * q, 4)],
                send_sem=hs.at[d, q], recv_sem=hr.at[d, q],
                device_id={"vtx": v_right if d == 0 else v_left}, device_id_type=MESH,
            )
            trip.start()
            halo_trips.append(trip)

    def wide(ref):
        return jnp.concatenate([ref[...].reshape(1, NNZ), jnp.zeros((1, ENT - NNZ), I32)], axis=1)

    rows, cols = wide(rows_v), wide(cols_v)
    active = iota((1, ENT), 1) < count_ref[0]
    where_col = jnp.where(cols < HALO, cols + NB + 1, jnp.where(cols < HALO + NB, cols - HALO, cols + 1))
    slot_place, places = order_slots(jnp.where(active, cols, 1000))
    places_out[...] = jnp.broadcast_to(places, (8, BS))
    place_trips = []
    for k, peer in ((0, v_right), (1, v_left)):
        trip = pltpu.make_async_remote_copy(
            src_ref=places_out, dst_ref=places_in.at[k], send_sem=ls.at[2 + k], recv_sem=lr.at[2 + k],
            device_id={"vtx": peer}, device_id_type=MESH,
        )
        trip.start()
        place_trips.append(trip)
    place, at_place, entry_place = order_groups(jnp.where(active, rows, 1000))
    table = pair_schedule(entry_place, where_col, active) + pair_schedule(slot_place, entry_place, active)
    table += [jnp.zeros((1, ENT), I32), jnp.clip(place, 0, NB - 1), jnp.clip(at_place, 0, NB - 1)]
    for k, row in enumerate(table):
        plan_v[k : k + 1] = row
    for k in range(len(table), 16):
        plan_v[k : k + 1] = jnp.zeros((1, ENT), I32)
    local = pltpu.make_async_copy(plan_v, plan, sm_sem)
    local.start()
    local.wait()

    def block_at(q):
        return plan[10, q]

    def side_by_side(blocks):
        return jnp.concatenate(blocks, axis=1)

    for p in range(PIECES):
        own = side_by_side([ext[block_at(p * PB + k)] for k in range(PB)])
        pre = jnp.dot(wst[...], own, preferred_element_type=F32)
        for k in range(PB):
            part[p * PB + k] = pre[:, k * BS : (k + 1) * BS]
    for trip in place_trips:
        trip.wait()
    from_right = inverse(lists_in[1, 0:1], places_in[1, 0:1], 0)
    from_left = inverse(lists_in[0, 0:1], places_in[0, 0:1], HALO)
    plan_v[8:9] = jnp.concatenate([from_right, from_left, jnp.zeros((1, BS), I32)], axis=1)
    plan_out = pltpu.make_async_copy(plan_v, plan_hbm, out_sem.at[0])
    plan_out.start()
    for load in val_loads + cot_loads:
        load.wait()
    for trip in halo_trips:
        trip.wait()
    for d in range(2):
        for j in range(HALO):
            ext[NB + 1 + HALO * d + j] = landed_halo[d, j]

    way = {p: 1 - 2 * (p % 2) for p in range(PIECES)}
    peer_of = {1: right, -1: left}

    def chunk(w, back_by):
        return lax.rem(me - w * back_by + 2 * NF, NF)

    def reduce_hop(p, s, w):
        return pltpu.make_async_remote_copy(
            src_ref=staged.at[s, p], dst_ref=landed.at[s, p],
            send_sem=send_sem.at[s, p], recv_sem=recv_sem.at[s, p],
            device_id={"feat": peer_of[w]}, device_id_type=MESH,
        )

    def gather_hop(p, s, w):
        owner = chunk(w, s)
        return pltpu.make_async_remote_copy(
            src_ref=slopes.at[p, owner], dst_ref=slopes.at[p, owner],
            send_sem=send_sem.at[3 + s, p], recv_sem=recv_sem.at[3 + s, p],
            device_id={"feat": peer_of[w]}, device_id_type=MESH,
        )

    def chunk_rows(c):
        return pl.ds(pl.multiple_of(c * HC, HC), HC)

    def forward_product(t):
        a = side_by_side([vals[plan[0, 2 * t]], vals[plan[0, 2 * t + 1]]])
        x = side_by_side([ext[plan[1, 2 * t]], ext[plan[1, 2 * t + 1]]])
        return lax.dot_general(x, a, (((1,), (1,)), ((), ())), preferred_element_type=F32)

    def reduce_on(p, s, w):
        reduce_hop(p, s - 1, w).wait_recv()
        for k in range(PB):
            more = part[p * PB + k, chunk_rows(chunk(w, 1 + s))]
            staged[s, p, k] = (landed[s - 1, p, k].astype(F32) + more).astype(BF16)
        reduce_hop(p, s, w).start()

    def forward_pieces(i, acc):
        for w in (1, -1):
            p = 2 * i + (0 if w == 1 else 1)
            for u in range(PIECE_PAIRS):
                t = p * PIECE_PAIRS + u
                acc = acc * plan[2, 2 * t].astype(F32) + forward_product(t)
                sums[t] = acc
            for k in range(PB):
                q = p * PB + k
                scale = rdeg[block_at(q)][0:1]
                mean[q] = (sums[plan[3, q]] * scale).astype(BF16)
            pre = jnp.dot(wnt[...], side_by_side([mean[p * PB + k] for k in range(PB)]), preferred_element_type=F32)
            for k in range(PB):
                q = p * PB + k
                part[q] = part[q] + pre[:, k * BS : (k + 1) * BS]
                staged[0, p, k] = part[q, chunk_rows(chunk(w, 1))].astype(BF16)
            reduce_hop(p, 0, w).start()
        return acc

    acc = forward_pieces(0, jnp.zeros((FC, BS), F32))

    def forward_step(i, acc):
        acc = forward_pieces(i, acc)
        for w in (1, -1):
            reduce_on(2 * i - 2 + (0 if w == 1 else 1), 1, w)
        return acc

    lax.fori_loop(1, PIECES // 2, forward_step, acc)
    for p in (PIECES - 2, PIECES - 1):
        reduce_on(p, 1, way[p])
    for p in range(PIECES):
        reduce_on(p, 2, way[p])
    for p in range(PIECES):
        reduce_hop(p, 2, way[p]).wait_recv()
        for k in range(PB):
            q = p * PB + k
            pre = landed[2, p, k].astype(F32) + part[q, chunk_rows(me)] + bias
            squash = 1.0 / (1.0 + jnp.exp(-pre))
            hid[q] = (pre * squash).astype(BF16)
            slope = cot[block_at(q)].astype(F32) * squash * (1.0 + pre * (1.0 - squash))
            slopes[p, me, k] = slope.astype(BF16)
        gather_hop(p, 0, way[p]).start()
    for s in range(1, 3):
        for p in range(PIECES):
            gather_hop(p, s - 1, way[p]).wait_recv()
            gather_hop(p, s, way[p]).start()
    total[...] = jnp.zeros_like(total)
    lanes = (((1,), (1,)), ((), ()))

    def slopes_of(p):
        return side_by_side([slopes[p, :, k].reshape(HID, BS) for k in range(PB)])

    for p in range(PIECES):
        gather_hop(p, 2, way[p]).wait_recv()
        full = slopes_of(p)
        far = jnp.dot(wn_ref[...], full, preferred_element_type=F32)
        for k in range(PB):
            q = p * PB + k
            back[q] = (far[:, k * BS : (k + 1) * BS] * rdeg[block_at(q)][0:1]).astype(BF16)
        own = side_by_side([ext[block_at(p * PB + k)] for k in range(PB)])
        near = side_by_side([mean[p * PB + k] for k in range(PB)])
        total[0] += lax.dot_general(own, full, lanes, preferred_element_type=F32)
        total[1] += lax.dot_general(near, full, lanes, preferred_element_type=F32)
    for k in range(2):
        for c in range(2):
            at = (2 * k + c) * FC
            grads[at : at + FC] = total[k, :, c * BS : (c + 1) * BS].astype(BF16)

    def exchange(peer_at, count, src_of, dst, mine, send, recv):
        trips = []
        for k in range(1, count + 1):
            other, device = peer_at(k)
            trips.append(pltpu.make_async_remote_copy(
                src_ref=src_of(other), dst_ref=dst.at[mine], send_sem=send.at[k - 1], recv_sem=recv.at[k - 1],
                device_id=device, device_id_type=MESH,
            ))
        for trip in trips:
            trip.start()
        return trips

    def rows_a(k):
        return pl.ds(pl.multiple_of(k * SL_A, 32), SL_A)

    a_trips = exchange(g_peer, 7, lambda k: grads.at[rows_a(k)], land_a, g, as_, ar)

    def backward_pair(t, acc):
        a = jnp.concatenate([vals[plan[4, 2 * t]], vals[plan[4, 2 * t + 1]]], axis=0)
        b = side_by_side([back[plan[5, 2 * t]], back[plan[5, 2 * t + 1]]])
        acc = acc * plan[6, 2 * t].astype(F32) + jnp.dot(b, a, preferred_element_type=F32)
        sums[t] = acc
        return acc

    def back_hop(q, d):
        return pltpu.make_async_remote_copy(
            src_ref=sent.at[d, pl.ds(4 * q, 4)], dst_ref=arrived.at[d, pl.ds(4 * q, 4)],
            send_sem=bs.at[d, q], recv_sem=br.at[d, q],
            device_id={"vtx": v_right if d else v_left}, device_id_type=MESH,
        )

    def backward_quarter(q, acc):
        for u in range(QUARTER):
            acc = backward_pair(q * QUARTER + u, acc)
        for d in range(2):
            for j in range(4):
                sent[d, 4 * q + j] = sums[plan[7, 8 * q + 4 * d + j]].astype(BF16)
            back_hop(q, d).start()
        return acc

    acc = lax.fori_loop(0, 3, backward_quarter, jnp.zeros((FC, BS), F32))
    for trip in a_trips:
        trip.wait()
    land_a[g] = grads[rows_a(g)]
    sum_a[x] = jnp.sum(land_a[...].astype(F32), axis=0)
    x_trips = exchange(x_peer, 3, lambda k: sum_a.at[x], sum_a, x, zs, zr)
    acc = backward_quarter(3, acc)
    for u in range(REST):
        acc = backward_pair(4 * QUARTER + u, acc)
    for b in range(NB):
        hidden[:, b * BS : (b + 1) * BS] = hid[plan[9, b]]
    outs = [plan_out, pltpu.make_async_copy(hidden, hidden_hbm, out_sem.at[1])]
    outs[1].start()
    for trip in x_trips:
        trip.wait()
    whole[...] = (jnp.sum(sum_a[...], axis=0) * float(NV * ROWS) ** -0.5).astype(BF16)
    d_trips = exchange(g_peer, 7, lambda k: whole, grads_hbm, g, ds, dr)
    outs.append(pltpu.make_async_copy(whole, grads_hbm.at[g], out_sem.at[6]))
    outs[-1].start()
    for p in range(PIECES):
        near = jnp.dot(ws_ref[...], slopes_of(p), preferred_element_type=F32)
        for k in range(PB):
            part[p * PB + k, :FC] = near[:, k * BS : (k + 1) * BS]
    for c in range(4):
        for b in range(8 * c, 8 * c + 8):
            base[b] = part[plan[9, b], :FC] + sums[plan[7, 2 * HALO + b]]
        outs.append(pltpu.make_async_copy(base.at[pl.ds(8 * c, 8)], base_hbm.at[pl.ds(8 * c, 8)], out_sem.at[2 + c]))
        outs[-1].start()
    for s in range(3):
        for p in range(PIECES):
            reduce_hop(p, s, way[p]).wait_send()
            gather_hop(p, s, way[p]).wait_send()
    for out in outs:
        out.wait()
    for q in range(4):
        for d in range(2):
            back_hop(q, d).wait()
    for trip in d_trips:
        trip.wait()


def layer_call(rows, cols, count, lists, feat, cot, degree, ws, wn, bias, vals):
    dma = pltpu.SemaphoreType.DMA
    V = pltpu.VMEM
    return pl.pallas_call(
        layer_kernel,
        out_shape=(
            jax.ShapeDtypeStruct((HC, ROWS), BF16),
            jax.ShapeDtypeStruct((NB, FC, BS), F32),
            jax.ShapeDtypeStruct((2, HALO, FC, BS), BF16),
            jax.ShapeDtypeStruct((8, SL_A, BS), BF16),
            jax.ShapeDtypeStruct((16, ENT), I32),
        ),
        in_specs=[anyspace(), anyspace(), smem()] + [anyspace()] * 4 + [vmem()] * 2 + [anyspace()] * 2,
        out_specs=(anyspace(),) * 5,
        scratch_shapes=[
            V((NNZ,), I32),
            V((NNZ,), I32),
            V((2 * HALO,), I32),
            V((HC,), F32),
            V((NB, BS), I32),
            V((NB, 8, BS), F32),
            V((8, BS), I32),
            V((2, 8, BS), I32),
            pltpu.SMEM((2, 8, BS), I32),
            V((8, BS), I32),
            V((2, 8, BS), I32),
            V((16, ENT), I32),
            pltpu.SMEM((16, ENT), I32),
            V((EXT + 1, FC, BS), BF16),
            V((2, HALO, FC, BS), BF16),
            V((NB, HC, BS), BF16),
            V((NNZ + 1, BS, BS), BF16),
            V((PAIRS_B + 1, FC, BS), F32),
            V((2, HALO, FC, BS), BF16),
            V((NB, FC, BS), BF16),
            V((HID, FC), BF16),
            V((HID, FC), BF16),
            V((NB, HID, BS), F32),
            V((3, PIECES, PB, HC, BS), BF16),
            V((3, PIECES, PB, HC, BS), BF16),
            V((PIECES, NF, PB, HC, BS), BF16),
            V((NB, HC, BS), BF16),
            V((NB, FC, BS), BF16),
            V((NB, FC, BS), F32),
            V((HC, ROWS), BF16),
            V((2, FC, HID), F32),
            V((4 * FC, BS), BF16),
            V((8, SL_A, BS), BF16),
            V((4, SL_A, BS), F32),
            V((SL_A, BS), BF16),
            dma((5,)), dma((NB,)), dma((NB,)), dma((8,)), dma, dma((4,)), dma((4,)), dma((2, 4)), dma((2, 4)),
            dma((6, PIECES)), dma((6, PIECES)), dma((2, 4)), dma((2, 4)),
            dma((7,)), dma((7,)), dma((3,)), dma((3,)), dma((7,)), dma((7,)), dma((7,)),
        ],
        compiler_params=pltpu.CompilerParams(collective_id=0, has_side_effects=True, vmem_limit_bytes=60 * MB),
        name="layer",
    )(rows, cols, count, lists, feat, cot, degree, ws, wn, bias, vals)


def results_kernel(
    plan_hbm, base_hbm, arrived_hbm, hidden_in, grads_hbm,
    hidden_out, features_hbm, self_hbm, neigh_hbm,
    plan, base, arrived, features, hidden, grads, weights, sems, out_sems,
):
    grads_load = pltpu.make_async_copy(grads_hbm, grads, sems.at[0])
    plan_load = pltpu.make_async_copy(plan_hbm, plan, sems.at[1])
    arrivals = [
        pltpu.make_async_copy(arrived_hbm.at[d], arrived.at[d, pl.ds(0, HALO)], sems.at[2 + d]) for d in range(2)
    ]
    hidden_load = pltpu.make_async_copy(hidden_in, hidden, sems.at[4])
    pieces = [
        pltpu.make_async_copy(base_hbm.at[pl.ds(4 * c, 4)], base.at[pl.ds(4 * c, 4)], sems.at[5 + c]) for c in range(8)
    ]
    for load in [plan_load, grads_load] + arrivals + pieces[:2] + [hidden_load] + pieces[2:]:
        load.start()
    for d in range(2):
        arrived[d, HALO] = jnp.zeros((FC, BS), BF16)
    grads_load.wait()
    every = grads[...].reshape(4 * FC, BS).astype(F32)
    outs = []
    for k, ref in ((0, self_hbm), (1, neigh_hbm)):
        for c in range(2):
            at = (2 * k + c) * FC
            weights[k, :, c * BS : (c + 1) * BS] = every[at : at + FC]
        outs.append(pltpu.make_async_copy(weights.at[k], ref, out_sems.at[k]))
        outs[-1].start()
    for load in [plan_load] + arrivals:
        load.wait()
    for c in range(8):
        pieces[c].wait()
        for b in range(4 * c, 4 * c + 4):
            extra = arrived[0, plan[8, b]].astype(F32) + arrived[1, plan[8, BS + b]].astype(F32)
            features[:, b * BS : (b + 1) * BS] = (base[b] + extra).astype(BF16)
        at = pl.ds(4 * c * BS, 4 * BS)
        outs.append(pltpu.make_async_copy(features.at[:, at], features_hbm.at[:, at], out_sems.at[3 + c]))
        outs[-1].start()
        if c == 2:
            hidden_load.wait()
            outs.append(pltpu.make_async_copy(hidden, hidden_out, out_sems.at[2]))
            outs[-1].start()
    for out in outs:
        out.wait()


def results_call(plan, base, arrived, hidden, grads):
    V = pltpu.VMEM
    return pl.pallas_call(
        results_kernel,
        out_shape=(
            jax.ShapeDtypeStruct((HC, ROWS), BF16),
            jax.ShapeDtypeStruct((FC, ROWS), BF16),
            jax.ShapeDtypeStruct((FC, HID), F32),
            jax.ShapeDtypeStruct((FC, HID), F32),
        ),
        in_specs=[anyspace()] * 5,
        out_specs=(anyspace(),) * 4,
        scratch_shapes=[
            pltpu.SMEM((16, ENT), I32),
            V((NB, FC, BS), F32),
            V((2, HALO + 1, FC, BS), BF16),
            V((FC, ROWS), BF16),
            V((HC, ROWS), BF16),
            V((8, SL_A, BS), BF16),
            V((2, FC, HID), F32),
            pltpu.SemaphoreType.DMA((13,)),
            pltpu.SemaphoreType.DMA((11,)),
        ],
        compiler_params=pltpu.CompilerParams(vmem_limit_bytes=60 * MB),
        name="results",
    )(plan, base, arrived, hidden, grads)


def on_device(
    features, w_self, w_neigh, bias_terms, block_vals, block_rows, block_cols, block_count, recv_lists, degree, cotangent
):
    hidden, base, arrived, grads, plan = layer_call(
        block_rows, block_cols, block_count, recv_lists, features.T, cotangent.T, degree.reshape(NB, BS),
        w_self, w_neigh, bias_terms, block_vals,
    )
    hidden, grad_features, grad_self, grad_neigh = results_call(plan, base, arrived, hidden, grads)
    return hidden.T, grad_features.T, grad_self, grad_neigh


def solution(mesh):
    placed = (
        P("vtx", "feat"), P("feat", None), P("feat", None), P("feat"), P("vtx", None, None), P("vtx"), P("vtx"), P("vtx"),
        P("vtx"), P("vtx"), P("vtx", "feat"),
    )
    return jax.shard_map(
        on_device,
        mesh=mesh,
        in_specs=placed,
        out_specs=(P("vtx", "feat"), P("vtx", "feat"), P("feat", None), P("feat", None)),
        check_vma=False,
    )
```

```python
import functools

import jax
import jax.numpy as jnp
from jax import lax
from jax.experimental import pallas as pl
from jax.experimental.pallas import tpu as pltpu
from jax.sharding import PartitionSpec as P

MESH = pl.DeviceIdType.MESH
F32, BF16, I32 = jnp.float32, jnp.bfloat16, jnp.int32
BS = 128
NB = 32
HALO = 16
NNZ = 320
EXT = NB + 2 * HALO
FC = 192
HID = 256
HC = 64
ROWS = NB * BS
NV, NF = 32, 4
ENT = 384
PIECES = 8
PB = NB // PIECES
PAIRS_F = (NNZ + NB) // 2
PAIRS_B = (NNZ + EXT) // 2
PIECE_PAIRS = PAIRS_F // PIECES
QUARTER = (NNZ + 2 * HALO) // 8
REST = PAIRS_B - 4 * QUARTER
ZERO = NB
SL_A = 4 * FC // 8
MB = 1 << 20


def vmem():
    return pl.BlockSpec(memory_space=pltpu.VMEM)


def smem():
    return pl.BlockSpec(memory_space=pltpu.SMEM)


def anyspace():
    return pl.BlockSpec(memory_space=pl.ANY)


def greet(peers):
    barrier = pltpu.get_barrier_semaphore()
    for peer in peers:
        pl.semaphore_signal(barrier, inc=1, device_id=peer, device_id_type=MESH)
    pl.semaphore_wait(barrier, len(peers))


def iota(shape, dim):
    return lax.broadcasted_iota(I32, shape, dim)


def as_column(row):
    n = row.shape[1]
    diagonal = iota((n, n), 0) == iota((n, n), 1)
    return jnp.sum(jnp.where(diagonal, row, jnp.zeros_like(row)), axis=1, keepdims=True, dtype=row.dtype)


def down(values):
    return jnp.sum(values, axis=0, keepdims=True, dtype=I32)


def group_sizes(key):
    size = jnp.sum(jnp.where(iota((EXT, ENT), 0) == key, 1, 0), axis=1, keepdims=True, dtype=I32)
    return ((size + 1) >> 1) << 1


def order_groups(key):
    block, lane = iota((EXT, ENT), 0), iota((EXT, ENT), 1)
    size = group_sizes(key)
    size_row = down(jnp.where(block == lane, size, 0))
    earlier = (size < size_row) | ((size == size_row) & (block < lane))
    place = down(jnp.where(earlier & (block < NB), 1, 0))
    place_col = as_column(place)[:EXT]
    at_place = down(jnp.where((place_col == lane) & (block < NB), block, 0))
    of_entry = down(jnp.where(block == key, place_col, 0))
    return place, at_place, of_entry


def order_slots(key):
    slot, lane = iota((EXT, ENT), 0), iota((EXT, ENT), 1)
    size = group_sizes(key)
    size_row = down(jnp.where(slot == lane, size, 0))
    earlier = (size < size_row) | ((size == size_row) & (slot < lane))
    side = jnp.where(slot < HALO, 0, jnp.where(slot < HALO + NB, 1, 2))
    lane_side = jnp.where(lane < HALO, 0, jnp.where(lane < HALO + NB, 1, 2))
    at_side = as_column(down(jnp.where(earlier & (side == lane_side), 1, 0)))[:EXT]
    slot, side = slot[:, :1], side[:, :1]
    turn = ((at_side >> 2) << 3) + (at_side & 3)
    order = jnp.where(side == 1, 2 * HALO + slot - HALO, turn + jnp.where(side == 2, 4, 0))
    of_entry = down(jnp.where(iota((EXT, ENT), 0) == key, order, 0))
    told = iota((EXT, BS), 1)
    told = jnp.where(told < HALO, told, told + NB)
    return of_entry, down(jnp.where(iota((EXT, BS), 0) == told, at_side, 0))


def pair_schedule(key, other, active):
    far = 1000
    sub, lane = iota((ENT, ENT), 0), iota((ENT, ENT), 1)
    key = jnp.where(active, key, far)
    key_col = as_column(key)
    rank = down(jnp.where((key_col == key) & (sub < lane), 1, 0))
    group, at = iota((EXT, ENT), 0), iota((EXT, ENT), 1)
    size = group_sizes(key)
    start = down(jnp.where(group < key, size, 0))
    slot = jnp.where(active, start + rank, far)
    hit = as_column(slot) == lane

    def at_slots(column, default):
        return down(jnp.where(hit, column - default, 0)) + default

    entry = at_slots(sub[:, :1], NNZ)
    source = at_slots(as_column(other), 0)
    goes_on = jnp.minimum(at_slots(as_column(rank), 1), 1)
    end = down(jnp.where(group <= at, size, 0))
    own = down(jnp.where(group == at, size, 0))
    done = jnp.where(own > 0, (end >> 1) - 1, PAIRS_B)
    return [jnp.clip(entry, 0, NNZ), jnp.clip(source, 0, EXT), goes_on, jnp.clip(done, 0, PAIRS_B)]


def inverse(lists, places, first):
    ours, place = as_column(lists), as_column(places)
    sub, lane = iota((BS, BS), 0), iota((BS, BS), 1)
    hit = (ours == lane) & (sub >= first) & (sub < first + HALO)
    return jnp.clip(down(jnp.where(hit, place - HALO, 0)) + HALO, 0, HALO)


def layer_kernel(
    rows_hbm, cols_hbm, count_ref, lists_hbm, feat_hbm, cot_hbm, degree_hbm, ws_ref, wn_ref, bias_hbm, vals_hbm,
    hidden_hbm, base_hbm, arrived, grads_hbm, plan_hbm,
    rows_v, cols_v, lists_v, bias_v, degree_v, rdeg, lists_out, lists_in, lists_sm, places_out, places_in, plan_v, plan,
    ext, landed_halo, cot, vals, sums, sent, mean, wst, wnt, part, staged, landed, slopes, hid, back, base, hidden,
    total, grads, land_a, sum_a, whole,
    small_sem, feat_sem, cot_sem, vals_sem, sm_sem, ls, lr, hs, hr,
    send_sem, recv_sem, bs, br, as_, ar, zs, zr, ds, dr, out_sem,
):
    me = lax.axis_index("feat")
    right, left = lax.rem(me + 1, NF), lax.rem(me + NF - 1, NF)
    v = lax.axis_index("vtx")
    v_right, v_left = lax.rem(v + 1, NV), lax.rem(v + NV - 1, NV)
    core, x, z = lax.rem(v, 2), lax.rem(v // 2, 4), v // 8
    g = 2 * z + core

    def g_peer(k):
        other = lax.rem(g + k, 8)
        return other, {"vtx": ((other // 2) * 4 + x) * 2 + lax.rem(other, 2)}

    def x_peer(k):
        other = lax.rem(x + k, 4)
        return other, {"vtx": (z * 4 + other) * 2 + core}

    small = [
        pltpu.make_async_copy(src, dst, small_sem.at[k])
        for k, (src, dst) in enumerate(
            [(lists_hbm, lists_v), (rows_hbm, rows_v), (cols_hbm, cols_v), (bias_hbm, bias_v), (degree_hbm, degree_v)]
        )
    ]
    feat_loads = [
        pltpu.make_async_copy(feat_hbm.at[:, pl.ds(b * BS, BS)], ext.at[b], feat_sem.at[b]) for b in range(NB)
    ]
    cot_loads = [
        pltpu.make_async_copy(cot_hbm.at[:, pl.ds(b * BS, BS)], cot.at[b], cot_sem.at[b]) for b in range(NB)
    ]
    share = NNZ // 8
    val_loads = [
        pltpu.make_async_copy(vals_hbm.at[pl.ds(k * share, share)], vals.at[pl.ds(k * share, share)], vals_sem.at[k])
        for k in range(8)
    ]
    for load in small + feat_loads:
        load.start()
    barrier = pltpu.get_barrier_semaphore()
    peers = (
        [{"vtx": v_left}, {"vtx": v_right}, {"feat": left}, {"feat": right}]
        + [g_peer(k)[1] for k in range(1, 8)]
        + [x_peer(k)[1] for k in range(1, 4)]
    )
    for peer in peers:
        pl.semaphore_signal(barrier, inc=1, device_id=peer, device_id_type=MESH)
    for load in val_loads + cot_loads:
        load.start()
    small[0].wait()
    lists_out[...] = jnp.full((8, BS), -1, I32)
    lists_out[0:1, : 2 * HALO] = lists_v[...].reshape(1, 2 * HALO)
    ext[ZERO] = jnp.zeros((FC, BS), BF16)
    vals[NNZ] = jnp.zeros((BS, BS), BF16)
    sums[PAIRS_B] = jnp.zeros((FC, BS), F32)
    pl.semaphore_wait(barrier, len(peers))

    trips = []
    for k, peer in ((0, v_right), (1, v_left)):
        trip = pltpu.make_async_remote_copy(
            src_ref=lists_out, dst_ref=lists_in.at[k], send_sem=ls.at[k], recv_sem=lr.at[k],
            device_id={"vtx": peer}, device_id_type=MESH,
        )
        trip.start()
        trips.append(trip)
    for load in small[1:] + feat_loads:
        load.wait()
    wst[...] = ws_ref[...].T
    wnt[...] = wn_ref[...].T
    bias = as_column(bias_v[...].reshape(1, HC))
    for b in range(NB):
        rdeg[b] = jnp.broadcast_to(1.0 / degree_v[b : b + 1, :].astype(F32), (8, BS))
    for trip in trips:
        trip.wait()
    local = pltpu.make_async_copy(lists_in, lists_sm, sm_sem)
    local.start()
    local.wait()
    halo_trips = []
    for q in range(4):
        for d in range(2):
            for j in range(4 * q, 4 * q + 4):
                sent[d, j] = ext[lax.rem(lists_sm[1 - d, 0, j + HALO * d] + NB + 1, NB + 1)]
            trip = pltpu.make_async_remote_copy(
                src_ref=sent.at[d, pl.ds(4 * q, 4)], dst_ref=landed_halo.at[d, pl.ds(4 * q, 4)],
                send_sem=hs.at[d, q], recv_sem=hr.at[d, q],
                device_id={"vtx": v_right if d == 0 else v_left}, device_id_type=MESH,
            )
            trip.start()
            halo_trips.append(trip)

    def wide(ref):
        return jnp.concatenate([ref[...].reshape(1, NNZ), jnp.zeros((1, ENT - NNZ), I32)], axis=1)

    rows, cols = wide(rows_v), wide(cols_v)
    active = iota((1, ENT), 1) < count_ref[0]
    where_col = jnp.where(cols < HALO, cols + NB + 1, jnp.where(cols < HALO + NB, cols - HALO, cols + 1))
    slot_place, places = order_slots(jnp.where(active, cols, 1000))
    places_out[...] = jnp.broadcast_to(places, (8, BS))
    place_trips = []
    for k, peer in ((0, v_right), (1, v_left)):
        trip = pltpu.make_async_remote_copy(
            src_ref=places_out, dst_ref=places_in.at[k], send_sem=ls.at[2 + k], recv_sem=lr.at[2 + k],
            device_id={"vtx": peer}, device_id_type=MESH,
        )
        trip.start()
        place_trips.append(trip)
    place, at_place, entry_place = order_groups(jnp.where(active, rows, 1000))
    table = pair_schedule(entry_place, where_col, active) + pair_schedule(slot_place, entry_place, active)
    table += [jnp.zeros((1, ENT), I32), jnp.clip(place, 0, NB - 1), jnp.clip(at_place, 0, NB - 1)]
    for k, row in enumerate(table):
        plan_v[k : k + 1] = row
    for k in range(len(table), 16):
        plan_v[k : k + 1] = jnp.zeros((1, ENT), I32)
    local = pltpu.make_async_copy(plan_v, plan, sm_sem)
    local.start()
    local.wait()

    def block_at(q):
        return plan[10, q]

    def side_by_side(blocks):
        return jnp.concatenate(blocks, axis=1)

    for p in range(PIECES):
        own = side_by_side([ext[block_at(p * PB + k)] for k in range(PB)])
        pre = jnp.dot(wst[...], own, preferred_element_type=F32)
        for k in range(PB):
            part[p * PB + k] = pre[:, k * BS : (k + 1) * BS]
    for trip in place_trips:
        trip.wait()
    from_right = inverse(lists_in[1, 0:1], places_in[1, 0:1], 0)
    from_left = inverse(lists_in[0, 0:1], places_in[0, 0:1], HALO)
    plan_v[8:9] = jnp.concatenate([from_right, from_left, jnp.zeros((1, BS), I32)], axis=1)
    plan_out = pltpu.make_async_copy(plan_v, plan_hbm, out_sem.at[0])
    plan_out.start()
    for load in val_loads + cot_loads:
        load.wait()
    for trip in halo_trips:
        trip.wait()
    for d in range(2):
        for j in range(HALO):
            ext[NB + 1 + HALO * d + j] = landed_halo[d, j]

    way = {p: 1 - 2 * (p % 2) for p in range(PIECES)}
    peer_of = {1: right, -1: left}

    def chunk(w, back_by):
        return lax.rem(me - w * back_by + 2 * NF, NF)

    def reduce_hop(p, s, w):
        return pltpu.make_async_remote_copy(
            src_ref=staged.at[s, p], dst_ref=landed.at[s, p],
            send_sem=send_sem.at[s, p], recv_sem=recv_sem.at[s, p],
            device_id={"feat": peer_of[w]}, device_id_type=MESH,
        )

    def gather_hop(p, s, w):
        owner = chunk(w, s)
        return pltpu.make_async_remote_copy(
            src_ref=slopes.at[p, owner], dst_ref=slopes.at[p, owner],
            send_sem=send_sem.at[3 + s, p], recv_sem=recv_sem.at[3 + s, p],
            device_id={"feat": peer_of[w]}, device_id_type=MESH,
        )

    def chunk_rows(c):
        return pl.ds(pl.multiple_of(c * HC, HC), HC)

    def forward_product(t):
        a = side_by_side([vals[plan[0, 2 * t]], vals[plan[0, 2 * t + 1]]])
        x = side_by_side([ext[plan[1, 2 * t]], ext[plan[1, 2 * t + 1]]])
        return lax.dot_general(x, a, (((1,), (1,)), ((), ())), preferred_element_type=F32)

    def reduce_on(p, s, w):
        reduce_hop(p, s - 1, w).wait_recv()
        for k in range(PB):
            more = part[p * PB + k, chunk_rows(chunk(w, 1 + s))]
            staged[s, p, k] = (landed[s - 1, p, k].astype(F32) + more).astype(BF16)
        reduce_hop(p, s, w).start()

    def forward_pieces(i, acc):
        for w in (1, -1):
            p = 2 * i + (0 if w == 1 else 1)
            for u in range(PIECE_PAIRS):
                t = p * PIECE_PAIRS + u
                acc = acc * plan[2, 2 * t].astype(F32) + forward_product(t)
                sums[t] = acc
            for k in range(PB):
                q = p * PB + k
                scale = rdeg[block_at(q)][0:1]
                mean[q] = (sums[plan[3, q]] * scale).astype(BF16)
            pre = jnp.dot(wnt[...], side_by_side([mean[p * PB + k] for k in range(PB)]), preferred_element_type=F32)
            for k in range(PB):
                q = p * PB + k
                part[q] = part[q] + pre[:, k * BS : (k + 1) * BS]
                staged[0, p, k] = part[q, chunk_rows(chunk(w, 1))].astype(BF16)
            reduce_hop(p, 0, w).start()
        return acc

    acc = forward_pieces(0, jnp.zeros((FC, BS), F32))

    def forward_step(i, acc):
        acc = forward_pieces(i, acc)
        for w in (1, -1):
            reduce_on(2 * i - 2 + (0 if w == 1 else 1), 1, w)
        return acc

    lax.fori_loop(1, PIECES // 2, forward_step, acc)
    for p in (PIECES - 2, PIECES - 1):
        reduce_on(p, 1, way[p])
    for p in range(PIECES):
        reduce_on(p, 2, way[p])
    for p in range(PIECES):
        reduce_hop(p, 2, way[p]).wait_recv()
        for k in range(PB):
            q = p * PB + k
            pre = landed[2, p, k].astype(F32) + part[q, chunk_rows(me)] + bias
            squash = 1.0 / (1.0 + jnp.exp(-pre))
            hid[q] = (pre * squash).astype(BF16)
            slope = cot[block_at(q)].astype(F32) * squash * (1.0 + pre * (1.0 - squash))
            slopes[p, me, k] = slope.astype(BF16)
        gather_hop(p, 0, way[p]).start()
    for s in range(1, 3):
        for p in range(PIECES):
            gather_hop(p, s - 1, way[p]).wait_recv()
            gather_hop(p, s, way[p]).start()
    total[...] = jnp.zeros_like(total)
    lanes = (((1,), (1,)), ((), ()))

    def slopes_of(p):
        return side_by_side([slopes[p, :, k].reshape(HID, BS) for k in range(PB)])

    for p in range(PIECES):
        gather_hop(p, 2, way[p]).wait_recv()
        full = slopes_of(p)
        far = jnp.dot(wn_ref[...], full, preferred_element_type=F32)
        for k in range(PB):
            q = p * PB + k
            back[q] = (far[:, k * BS : (k + 1) * BS] * rdeg[block_at(q)][0:1]).astype(BF16)
        own = side_by_side([ext[block_at(p * PB + k)] for k in range(PB)])
        near = side_by_side([mean[p * PB + k] for k in range(PB)])
        total[0] += lax.dot_general(own, full, lanes, preferred_element_type=F32)
        total[1] += lax.dot_general(near, full, lanes, preferred_element_type=F32)
    for k in range(2):
        for c in range(2):
            at = (2 * k + c) * FC
            grads[at : at + FC] = total[k, :, c * BS : (c + 1) * BS].astype(BF16)

    def exchange(peer_at, count, src_of, dst, mine, send, recv):
        trips = []
        for k in range(1, count + 1):
            other, device = peer_at(k)
            trips.append(pltpu.make_async_remote_copy(
                src_ref=src_of(other), dst_ref=dst.at[mine], send_sem=send.at[k - 1], recv_sem=recv.at[k - 1],
                device_id=device, device_id_type=MESH,
            ))
        for trip in trips:
            trip.start()
        return trips

    def rows_a(k):
        return pl.ds(pl.multiple_of(k * SL_A, 32), SL_A)

    a_trips = exchange(g_peer, 7, lambda k: grads.at[rows_a(k)], land_a, g, as_, ar)

    def backward_pair(t, acc):
        a = jnp.concatenate([vals[plan[4, 2 * t]], vals[plan[4, 2 * t + 1]]], axis=0)
        b = side_by_side([back[plan[5, 2 * t]], back[plan[5, 2 * t + 1]]])
        acc = acc * plan[6, 2 * t].astype(F32) + jnp.dot(b, a, preferred_element_type=F32)
        sums[t] = acc
        return acc

    def back_hop(q, d):
        return pltpu.make_async_remote_copy(
            src_ref=sent.at[d, pl.ds(4 * q, 4)], dst_ref=arrived.at[d, pl.ds(4 * q, 4)],
            send_sem=bs.at[d, q], recv_sem=br.at[d, q],
            device_id={"vtx": v_right if d else v_left}, device_id_type=MESH,
        )

    def backward_quarter(q, acc):
        for u in range(QUARTER):
            acc = backward_pair(q * QUARTER + u, acc)
        for d in range(2):
            for j in range(4):
                sent[d, 4 * q + j] = sums[plan[7, 8 * q + 4 * d + j]].astype(BF16)
            back_hop(q, d).start()
        return acc

    acc = lax.fori_loop(0, 2, backward_quarter, jnp.zeros((FC, BS), F32))
    for trip in a_trips:
        trip.wait()
    land_a[g] = grads[rows_a(g)]
    sum_a[x] = jnp.sum(land_a[...].astype(F32), axis=0).astype(BF16)
    x_trips = exchange(x_peer, 3, lambda k: sum_a.at[x], sum_a, x, zs, zr)
    acc = lax.fori_loop(2, 4, backward_quarter, acc)
    for u in range(REST):
        acc = backward_pair(4 * QUARTER + u, acc)
    for trip in x_trips:
        trip.wait()
    whole[...] = (jnp.sum(sum_a[...].astype(F32), axis=0) * float(NV * ROWS) ** -0.5).astype(BF16)
    d_trips = exchange(g_peer, 7, lambda k: whole, grads_hbm, g, ds, dr)
    outs = [plan_out, pltpu.make_async_copy(whole, grads_hbm.at[g], out_sem.at[6])]
    outs[-1].start()
    for b in range(NB):
        hidden[:, b * BS : (b + 1) * BS] = hid[plan[9, b]]
    outs.append(pltpu.make_async_copy(hidden, hidden_hbm, out_sem.at[1]))
    outs[-1].start()
    for p in range(PIECES):
        near = jnp.dot(ws_ref[...], slopes_of(p), preferred_element_type=F32)
        for k in range(PB):
            part[p * PB + k, :FC] = near[:, k * BS : (k + 1) * BS]
    for c in range(4):
        for b in range(8 * c, 8 * c + 8):
            base[b] = part[plan[9, b], :FC] + sums[plan[7, 2 * HALO + b]]
        outs.append(pltpu.make_async_copy(base.at[pl.ds(8 * c, 8)], base_hbm.at[pl.ds(8 * c, 8)], out_sem.at[2 + c]))
        outs[-1].start()
    for s in range(3):
        for p in range(PIECES):
            reduce_hop(p, s, way[p]).wait_send()
            gather_hop(p, s, way[p]).wait_send()
    for out in outs:
        out.wait()
    for q in range(4):
        for d in range(2):
            back_hop(q, d).wait()
    for trip in d_trips:
        trip.wait()


def layer_call(rows, cols, count, lists, feat, cot, degree, ws, wn, bias, vals):
    dma = pltpu.SemaphoreType.DMA
    V = pltpu.VMEM
    return pl.pallas_call(
        layer_kernel,
        out_shape=(
            jax.ShapeDtypeStruct((HC, ROWS), BF16),
            jax.ShapeDtypeStruct((NB, FC, BS), F32),
            jax.ShapeDtypeStruct((2, HALO, FC, BS), BF16),
            jax.ShapeDtypeStruct((8, SL_A, BS), BF16),
            jax.ShapeDtypeStruct((16, ENT), I32),
        ),
        in_specs=[anyspace(), anyspace(), smem()] + [anyspace()] * 4 + [vmem()] * 2 + [anyspace()] * 2,
        out_specs=(anyspace(),) * 5,
        scratch_shapes=[
            V((NNZ,), I32),
            V((NNZ,), I32),
            V((2 * HALO,), I32),
            V((HC,), F32),
            V((NB, BS), I32),
            V((NB, 8, BS), F32),
            V((8, BS), I32),
            V((2, 8, BS), I32),
            pltpu.SMEM((2, 8, BS), I32),
            V((8, BS), I32),
            V((2, 8, BS), I32),
            V((16, ENT), I32),
            pltpu.SMEM((16, ENT), I32),
            V((EXT + 1, FC, BS), BF16),
            V((2, HALO, FC, BS), BF16),
            V((NB, HC, BS), BF16),
            V((NNZ + 1, BS, BS), BF16),
            V((PAIRS_B + 1, FC, BS), F32),
            V((2, HALO, FC, BS), BF16),
            V((NB, FC, BS), BF16),
            V((HID, FC), BF16),
            V((HID, FC), BF16),
            V((NB, HID, BS), F32),
            V((3, PIECES, PB, HC, BS), BF16),
            V((3, PIECES, PB, HC, BS), BF16),
            V((PIECES, NF, PB, HC, BS), BF16),
            V((NB, HC, BS), BF16),
            V((NB, FC, BS), BF16),
            V((NB, FC, BS), F32),
            V((HC, ROWS), BF16),
            V((2, FC, HID), F32),
            V((4 * FC, BS), BF16),
            V((8, SL_A, BS), BF16),
            V((4, SL_A, BS), BF16),
            V((SL_A, BS), BF16),
            dma((5,)), dma((NB,)), dma((NB,)), dma((8,)), dma, dma((4,)), dma((4,)), dma((2, 4)), dma((2, 4)),
            dma((6, PIECES)), dma((6, PIECES)), dma((2, 4)), dma((2, 4)),
            dma((7,)), dma((7,)), dma((3,)), dma((3,)), dma((7,)), dma((7,)), dma((7,)),
        ],
        compiler_params=pltpu.CompilerParams(collective_id=0, has_side_effects=True, vmem_limit_bytes=60 * MB),
        name="layer",
    )(rows, cols, count, lists, feat, cot, degree, ws, wn, bias, vals)


def results_kernel(
    plan_hbm, base_hbm, arrived_hbm, hidden_in, grads_hbm,
    hidden_out, features_hbm, self_hbm, neigh_hbm,
    plan, base, arrived, features, hidden, grads, weights, sems, out_sems,
):
    grads_load = pltpu.make_async_copy(grads_hbm, grads, sems.at[0])
    plan_load = pltpu.make_async_copy(plan_hbm, plan, sems.at[1])
    arrivals = [
        pltpu.make_async_copy(arrived_hbm.at[d], arrived.at[d, pl.ds(0, HALO)], sems.at[2 + d]) for d in range(2)
    ]
    hidden_load = pltpu.make_async_copy(hidden_in, hidden, sems.at[4])
    pieces = [
        pltpu.make_async_copy(base_hbm.at[pl.ds(4 * c, 4)], base.at[pl.ds(4 * c, 4)], sems.at[5 + c]) for c in range(8)
    ]
    for load in [plan_load, grads_load] + arrivals + pieces[:2] + [hidden_load] + pieces[2:]:
        load.start()
    for d in range(2):
        arrived[d, HALO] = jnp.zeros((FC, BS), BF16)
    grads_load.wait()
    every = grads[...].reshape(4 * FC, BS).astype(F32)
    outs = []
    for k, ref in ((0, self_hbm), (1, neigh_hbm)):
        for c in range(2):
            at = (2 * k + c) * FC
            weights[k, :, c * BS : (c + 1) * BS] = every[at : at + FC]
        outs.append(pltpu.make_async_copy(weights.at[k], ref, out_sems.at[k]))
        outs[-1].start()
    for load in [plan_load] + arrivals:
        load.wait()
    for c in range(8):
        pieces[c].wait()
        for b in range(4 * c, 4 * c + 4):
            extra = arrived[0, plan[8, b]].astype(F32) + arrived[1, plan[8, BS + b]].astype(F32)
            features[:, b * BS : (b + 1) * BS] = (base[b] + extra).astype(BF16)
        at = pl.ds(4 * c * BS, 4 * BS)
        outs.append(pltpu.make_async_copy(features.at[:, at], features_hbm.at[:, at], out_sems.at[3 + c]))
        outs[-1].start()
        if c == 2:
            hidden_load.wait()
            outs.append(pltpu.make_async_copy(hidden, hidden_out, out_sems.at[2]))
            outs[-1].start()
    for out in outs:
        out.wait()


def results_call(plan, base, arrived, hidden, grads):
    V = pltpu.VMEM
    return pl.pallas_call(
        results_kernel,
        out_shape=(
            jax.ShapeDtypeStruct((HC, ROWS), BF16),
            jax.ShapeDtypeStruct((FC, ROWS), BF16),
            jax.ShapeDtypeStruct((FC, HID), F32),
            jax.ShapeDtypeStruct((FC, HID), F32),
        ),
        in_specs=[anyspace()] * 5,
        out_specs=(anyspace(),) * 4,
        scratch_shapes=[
            pltpu.SMEM((16, ENT), I32),
            V((NB, FC, BS), F32),
            V((2, HALO + 1, FC, BS), BF16),
            V((FC, ROWS), BF16),
            V((HC, ROWS), BF16),
            V((8, SL_A, BS), BF16),
            V((2, FC, HID), F32),
            pltpu.SemaphoreType.DMA((13,)),
            pltpu.SemaphoreType.DMA((11,)),
        ],
        compiler_params=pltpu.CompilerParams(vmem_limit_bytes=60 * MB),
        name="results",
    )(plan, base, arrived, hidden, grads)


def on_device(
    features, w_self, w_neigh, bias_terms, block_vals, block_rows, block_cols, block_count, recv_lists, degree, cotangent
):
    hidden, base, arrived, grads, plan = layer_call(
        block_rows, block_cols, block_count, recv_lists, features.T, cotangent.T, degree.reshape(NB, BS),
        w_self, w_neigh, bias_terms, block_vals,
    )
    hidden, grad_features, grad_self, grad_neigh = results_call(plan, base, arrived, hidden, grads)
    return hidden.T, grad_features.T, grad_self, grad_neigh


def solution(mesh):
    placed = (
        P("vtx", "feat"), P("feat", None), P("feat", None), P("feat"), P("vtx", None, None), P("vtx"), P("vtx"), P("vtx"),
        P("vtx"), P("vtx"), P("vtx", "feat"),
    )
    return jax.shard_map(
        on_device,
        mesh=mesh,
        in_specs=placed,
        out_specs=(P("vtx", "feat"), P("vtx", "feat"), P("feat", None), P("feat", None)),
        check_vma=False,
    )
```

```python
import functools

import jax
import jax.numpy as jnp
from jax import lax
from jax.experimental import pallas as pl
from jax.experimental.pallas import tpu as pltpu
from jax.sharding import PartitionSpec as P

MESH = pl.DeviceIdType.MESH
F32, BF16, I32 = jnp.float32, jnp.bfloat16, jnp.int32
BS = 128
NB = 32
HALO = 16
NNZ = 320
EXT = NB + 2 * HALO
FC = 192
HID = 256
HC = 64
ROWS = NB * BS
NV, NF = 32, 4
ENT = 384
PIECES = 8
PB = NB // PIECES
PAIRS_F = (NNZ + NB) // 2
PAIRS_B = (NNZ + EXT) // 2
PIECE_PAIRS = PAIRS_F // PIECES
QUARTER = (NNZ + 2 * HALO) // 8
REST = PAIRS_B - 4 * QUARTER
ZERO = NB
SL_A = 4 * FC // 8
MB = 1 << 20


def vmem():
    return pl.BlockSpec(memory_space=pltpu.VMEM)


def smem():
    return pl.BlockSpec(memory_space=pltpu.SMEM)


def anyspace():
    return pl.BlockSpec(memory_space=pl.ANY)


def greet(peers):
    barrier = pltpu.get_barrier_semaphore()
    for peer in peers:
        pl.semaphore_signal(barrier, inc=1, device_id=peer, device_id_type=MESH)
    pl.semaphore_wait(barrier, len(peers))


def iota(shape, dim):
    return lax.broadcasted_iota(I32, shape, dim)


def as_column(row):
    n = row.shape[1]
    diagonal = iota((n, n), 0) == iota((n, n), 1)
    return jnp.sum(jnp.where(diagonal, row, jnp.zeros_like(row)), axis=1, keepdims=True, dtype=row.dtype)


def down(values):
    return jnp.sum(values, axis=0, keepdims=True, dtype=I32)


def group_sizes(key):
    size = jnp.sum(jnp.where(iota((EXT, ENT), 0) == key, 1, 0), axis=1, keepdims=True, dtype=I32)
    return ((size + 1) >> 1) << 1


def order_groups(key):
    block, lane = iota((EXT, ENT), 0), iota((EXT, ENT), 1)
    size = group_sizes(key)
    size_row = down(jnp.where(block == lane, size, 0))
    earlier = (size < size_row) | ((size == size_row) & (block < lane))
    place = down(jnp.where(earlier & (block < NB), 1, 0))
    place_col = as_column(place)[:EXT]
    at_place = down(jnp.where((place_col == lane) & (block < NB), block, 0))
    of_entry = down(jnp.where(block == key, place_col, 0))
    return place, at_place, of_entry


def order_slots(key):
    slot, lane = iota((EXT, ENT), 0), iota((EXT, ENT), 1)
    size = group_sizes(key)
    size_row = down(jnp.where(slot == lane, size, 0))
    earlier = (size < size_row) | ((size == size_row) & (slot < lane))
    side = jnp.where(slot < HALO, 0, jnp.where(slot < HALO + NB, 1, 2))
    lane_side = jnp.where(lane < HALO, 0, jnp.where(lane < HALO + NB, 1, 2))
    at_side = as_column(down(jnp.where(earlier & (side == lane_side), 1, 0)))[:EXT]
    slot, side = slot[:, :1], side[:, :1]
    turn = ((at_side >> 2) << 3) + (at_side & 3)
    order = jnp.where(side == 1, 2 * HALO + slot - HALO, turn + jnp.where(side == 2, 4, 0))
    of_entry = down(jnp.where(iota((EXT, ENT), 0) == key, order, 0))
    told = iota((EXT, BS), 1)
    told = jnp.where(told < HALO, told, told + NB)
    return of_entry, down(jnp.where(iota((EXT, BS), 0) == told, at_side, 0))


def pair_schedule(key, other, active):
    far = 1000
    sub, lane = iota((ENT, ENT), 0), iota((ENT, ENT), 1)
    key = jnp.where(active, key, far)
    key_col = as_column(key)
    rank = down(jnp.where((key_col == key) & (sub < lane), 1, 0))
    group, at = iota((EXT, ENT), 0), iota((EXT, ENT), 1)
    size = group_sizes(key)
    start = down(jnp.where(group < key, size, 0))
    slot = jnp.where(active, start + rank, far)
    hit = as_column(slot) == lane

    def at_slots(column, default):
        return down(jnp.where(hit, column - default, 0)) + default

    entry = at_slots(sub[:, :1], NNZ)
    source = at_slots(as_column(other), 0)
    goes_on = jnp.minimum(at_slots(as_column(rank), 1), 1)
    end = down(jnp.where(group <= at, size, 0))
    own = down(jnp.where(group == at, size, 0))
    done = jnp.where(own > 0, (end >> 1) - 1, PAIRS_B)
    return [jnp.clip(entry, 0, NNZ), jnp.clip(source, 0, EXT), goes_on, jnp.clip(done, 0, PAIRS_B)]


def inverse(lists, places, first):
    ours, place = as_column(lists), as_column(places)
    sub, lane = iota((BS, BS), 0), iota((BS, BS), 1)
    hit = (ours == lane) & (sub >= first) & (sub < first + HALO)
    return jnp.clip(down(jnp.where(hit, place - HALO, 0)) + HALO, 0, HALO)


def layer_kernel(
    rows_hbm, cols_hbm, count_ref, lists_hbm, feat_hbm, cot_hbm, degree_hbm, ws_ref, wn_ref, bias_hbm, vals_hbm,
    hidden_hbm, features_hbm, grads_hbm,
    rows_v, cols_v, lists_v, bias_v, degree_v, rdeg, lists_out, lists_in, lists_sm, places_out, places_in, plan_v, plan,
    ext, landed_halo, cot, vals, sums, sent, mean, wst, wnt, part, staged, landed, slopes, hid, back, base, hidden, arrived, features,
    total, grads, land_a, sum_a, whole,
    small_sem, feat_sem, cot_sem, vals_sem, sm_sem, ls, lr, hs, hr,
    send_sem, recv_sem, bs, br, as_, ar, zs, zr, ds, dr, out_sem,
):
    me = lax.axis_index("feat")
    right, left = lax.rem(me + 1, NF), lax.rem(me + NF - 1, NF)
    v = lax.axis_index("vtx")
    v_right, v_left = lax.rem(v + 1, NV), lax.rem(v + NV - 1, NV)
    core, x, z = lax.rem(v, 2), lax.rem(v // 2, 4), v // 8
    g = 2 * z + core

    def g_peer(k):
        other = lax.rem(g + k, 8)
        return other, {"vtx": ((other // 2) * 4 + x) * 2 + lax.rem(other, 2)}

    def x_peer(k):
        other = lax.rem(x + k, 4)
        return other, {"vtx": (z * 4 + other) * 2 + core}

    small = [
        pltpu.make_async_copy(src, dst, small_sem.at[k])
        for k, (src, dst) in enumerate(
            [(lists_hbm, lists_v), (rows_hbm, rows_v), (cols_hbm, cols_v), (bias_hbm, bias_v), (degree_hbm, degree_v)]
        )
    ]
    feat_loads = [
        pltpu.make_async_copy(feat_hbm.at[:, pl.ds(b * BS, BS)], ext.at[b], feat_sem.at[b]) for b in range(NB)
    ]
    cot_loads = [
        pltpu.make_async_copy(cot_hbm.at[:, pl.ds(b * BS, BS)], cot.at[b], cot_sem.at[b]) for b in range(NB)
    ]
    share = NNZ // 8
    val_loads = [
        pltpu.make_async_copy(vals_hbm.at[pl.ds(k * share, share)], vals.at[pl.ds(k * share, share)], vals_sem.at[k])
        for k in range(8)
    ]
    for load in small + feat_loads:
        load.start()
    barrier = pltpu.get_barrier_semaphore()
    peers = (
        [{"vtx": v_left}, {"vtx": v_right}, {"feat": left}, {"feat": right}]
        + [g_peer(k)[1] for k in range(1, 8)]
        + [x_peer(k)[1] for k in range(1, 4)]
    )
    for peer in peers:
        pl.semaphore_signal(barrier, inc=1, device_id=peer, device_id_type=MESH)
    for load in val_loads + cot_loads:
        load.start()
    small[0].wait()
    lists_out[...] = jnp.full((8, BS), -1, I32)
    lists_out[0:1, : 2 * HALO] = lists_v[...].reshape(1, 2 * HALO)
    ext[ZERO] = jnp.zeros((FC, BS), BF16)
    vals[NNZ] = jnp.zeros((BS, BS), BF16)
    sums[PAIRS_B] = jnp.zeros((FC, BS), F32)
    pl.semaphore_wait(barrier, len(peers))

    trips = []
    for k, peer in ((0, v_right), (1, v_left)):
        trip = pltpu.make_async_remote_copy(
            src_ref=lists_out, dst_ref=lists_in.at[k], send_sem=ls.at[k], recv_sem=lr.at[k],
            device_id={"vtx": peer}, device_id_type=MESH,
        )
        trip.start()
        trips.append(trip)
    for load in small[1:] + feat_loads:
        load.wait()
    wst[...] = ws_ref[...].T
    wnt[...] = wn_ref[...].T
    bias = as_column(bias_v[...].reshape(1, HC))
    for b in range(NB):
        rdeg[b] = jnp.broadcast_to(1.0 / degree_v[b : b + 1, :].astype(F32), (8, BS))
    for trip in trips:
        trip.wait()
    local = pltpu.make_async_copy(lists_in, lists_sm, sm_sem)
    local.start()
    local.wait()
    halo_trips = []
    for q in range(4):
        for d in range(2):
            for j in range(4 * q, 4 * q + 4):
                sent[d, j] = ext[lax.rem(lists_sm[1 - d, 0, j + HALO * d] + NB + 1, NB + 1)]
            trip = pltpu.make_async_remote_copy(
                src_ref=sent.at[d, pl.ds(4 * q, 4)], dst_ref=landed_halo.at[d, pl.ds(4 * q, 4)],
                send_sem=hs.at[d, q], recv_sem=hr.at[d, q],
                device_id={"vtx": v_right if d == 0 else v_left}, device_id_type=MESH,
            )
            trip.start()
            halo_trips.append(trip)

    def wide(ref):
        return jnp.concatenate([ref[...].reshape(1, NNZ), jnp.zeros((1, ENT - NNZ), I32)], axis=1)

    rows, cols = wide(rows_v), wide(cols_v)
    active = iota((1, ENT), 1) < count_ref[0]
    where_col = jnp.where(cols < HALO, cols + NB + 1, jnp.where(cols < HALO + NB, cols - HALO, cols + 1))
    slot_place, places = order_slots(jnp.where(active, cols, 1000))
    places_out[...] = jnp.broadcast_to(places, (8, BS))
    place_trips = []
    for k, peer in ((0, v_right), (1, v_left)):
        trip = pltpu.make_async_remote_copy(
            src_ref=places_out, dst_ref=places_in.at[k], send_sem=ls.at[2 + k], recv_sem=lr.at[2 + k],
            device_id={"vtx": peer}, device_id_type=MESH,
        )
        trip.start()
        place_trips.append(trip)
    place, at_place, entry_place = order_groups(jnp.where(active, rows, 1000))
    table = pair_schedule(entry_place, where_col, active) + pair_schedule(slot_place, entry_place, active)
    table += [jnp.zeros((1, ENT), I32), jnp.clip(place, 0, NB - 1), jnp.clip(at_place, 0, NB - 1)]
    for k, row in enumerate(table):
        plan_v[k : k + 1] = row
    for k in range(len(table), 16):
        plan_v[k : k + 1] = jnp.zeros((1, ENT), I32)
    local = pltpu.make_async_copy(plan_v, plan, sm_sem)
    local.start()
    local.wait()

    def block_at(q):
        return plan[10, q]

    def side_by_side(blocks):
        return jnp.concatenate(blocks, axis=1)

    for p in range(PIECES):
        own = side_by_side([ext[block_at(p * PB + k)] for k in range(PB)])
        pre = jnp.dot(wst[...], own, preferred_element_type=F32)
        for k in range(PB):
            part[p * PB + k] = pre[:, k * BS : (k + 1) * BS]
    for trip in place_trips:
        trip.wait()
    from_right = inverse(lists_in[1, 0:1], places_in[1, 0:1], 0)
    from_left = inverse(lists_in[0, 0:1], places_in[0, 0:1], HALO)
    plan_v[8:9] = jnp.concatenate([from_right, from_left, jnp.zeros((1, BS), I32)], axis=1)
    local = pltpu.make_async_copy(plan_v.at[pl.ds(8, 8)], plan.at[pl.ds(8, 8)], sm_sem)
    local.start()
    for d in range(2):
        arrived[d, HALO] = jnp.zeros((FC, BS), BF16)
    local.wait()
    for load in val_loads + cot_loads:
        load.wait()
    for trip in halo_trips:
        trip.wait()
    for d in range(2):
        for j in range(HALO):
            ext[NB + 1 + HALO * d + j] = landed_halo[d, j]

    way = {p: 1 - 2 * (p % 2) for p in range(PIECES)}
    peer_of = {1: right, -1: left}

    def chunk(w, back_by):
        return lax.rem(me - w * back_by + 2 * NF, NF)

    def reduce_hop(p, s, w):
        return pltpu.make_async_remote_copy(
            src_ref=staged.at[s, p], dst_ref=landed.at[s, p],
            send_sem=send_sem.at[s, p], recv_sem=recv_sem.at[s, p],
            device_id={"feat": peer_of[w]}, device_id_type=MESH,
        )

    def gather_hop(p, s, w):
        owner = chunk(w, s)
        return pltpu.make_async_remote_copy(
            src_ref=slopes.at[p, owner], dst_ref=slopes.at[p, owner],
            send_sem=send_sem.at[3 + s, p], recv_sem=recv_sem.at[3 + s, p],
            device_id={"feat": peer_of[w]}, device_id_type=MESH,
        )

    def chunk_rows(c):
        return pl.ds(pl.multiple_of(c * HC, HC), HC)

    def forward_product(t):
        a = side_by_side([vals[plan[0, 2 * t]], vals[plan[0, 2 * t + 1]]])
        x = side_by_side([ext[plan[1, 2 * t]], ext[plan[1, 2 * t + 1]]])
        return lax.dot_general(x, a, (((1,), (1,)), ((), ())), preferred_element_type=F32)

    def reduce_on(p, s, w):
        reduce_hop(p, s - 1, w).wait_recv()
        for k in range(PB):
            more = part[p * PB + k, chunk_rows(chunk(w, 1 + s))]
            staged[s, p, k] = (landed[s - 1, p, k].astype(F32) + more).astype(BF16)
        reduce_hop(p, s, w).start()

    def forward_pieces(i, acc):
        for w in (1, -1):
            p = 2 * i + (0 if w == 1 else 1)
            for u in range(PIECE_PAIRS):
                t = p * PIECE_PAIRS + u
                acc = acc * plan[2, 2 * t].astype(F32) + forward_product(t)
                sums[t] = acc
            for k in range(PB):
                q = p * PB + k
                scale = rdeg[block_at(q)][0:1]
                mean[q] = (sums[plan[3, q]] * scale).astype(BF16)
            pre = jnp.dot(wnt[...], side_by_side([mean[p * PB + k] for k in range(PB)]), preferred_element_type=F32)
            for k in range(PB):
                q = p * PB + k
                part[q] = part[q] + pre[:, k * BS : (k + 1) * BS]
                staged[0, p, k] = part[q, chunk_rows(chunk(w, 1))].astype(BF16)
            reduce_hop(p, 0, w).start()
        return acc

    acc = forward_pieces(0, jnp.zeros((FC, BS), F32))

    def forward_step(i, acc):
        acc = forward_pieces(i, acc)
        for w in (1, -1):
            reduce_on(2 * i - 2 + (0 if w == 1 else 1), 1, w)
        return acc

    lax.fori_loop(1, PIECES // 2, forward_step, acc)
    for p in (PIECES - 2, PIECES - 1):
        reduce_on(p, 1, way[p])
    for p in range(PIECES):
        reduce_on(p, 2, way[p])
    for p in range(PIECES):
        reduce_hop(p, 2, way[p]).wait_recv()
        for k in range(PB):
            q = p * PB + k
            pre = landed[2, p, k].astype(F32) + part[q, chunk_rows(me)] + bias
            squash = 1.0 / (1.0 + jnp.exp(-pre))
            hid[q] = (pre * squash).astype(BF16)
            slope = cot[block_at(q)].astype(F32) * squash * (1.0 + pre * (1.0 - squash))
            slopes[p, me, k] = slope.astype(BF16)
        gather_hop(p, 0, way[p]).start()
    for s in range(1, 3):
        for p in range(PIECES):
            gather_hop(p, s - 1, way[p]).wait_recv()
            gather_hop(p, s, way[p]).start()
    total[...] = jnp.zeros_like(total)
    lanes = (((1,), (1,)), ((), ()))

    def slopes_of(p):
        return side_by_side([slopes[p, :, k].reshape(HID, BS) for k in range(PB)])


    def back_of(p, full):
        far = jnp.dot(wn_ref[...], full, preferred_element_type=F32)
        for k in range(PB):
            q = p * PB + k
            back[q] = (far[:, k * BS : (k + 1) * BS] * rdeg[block_at(q)][0:1]).astype(BF16)

    for p in range(PIECES):
        gather_hop(p, 2, way[p]).wait_recv()
        full = slopes_of(p)
        if p < PIECES - 2:
            back_of(p, full)
        own = side_by_side([ext[block_at(p * PB + k)] for k in range(PB)])
        near = side_by_side([mean[p * PB + k] for k in range(PB)])
        total[0] += lax.dot_general(own, full, lanes, preferred_element_type=F32)
        total[1] += lax.dot_general(near, full, lanes, preferred_element_type=F32)
    for k in range(2):
        for c in range(2):
            at = (2 * k + c) * FC
            grads[at : at + FC] = total[k, :, c * BS : (c + 1) * BS].astype(BF16)

    def exchange(peer_at, count, src_of, dst, mine, send, recv):
        trips = []
        for k in range(1, count + 1):
            other, device = peer_at(k)
            trips.append(pltpu.make_async_remote_copy(
                src_ref=src_of(other), dst_ref=dst.at[mine], send_sem=send.at[k - 1], recv_sem=recv.at[k - 1],
                device_id=device, device_id_type=MESH,
            ))
        for trip in trips:
            trip.start()
        return trips

    def rows_a(k):
        return pl.ds(pl.multiple_of(k * SL_A, 32), SL_A)

    a_trips = exchange(g_peer, 7, lambda k: grads.at[rows_a(k)], land_a, g, as_, ar)
    for p in range(PIECES - 2, PIECES):
        back_of(p, slopes_of(p))

    def backward_pair(t, acc):
        a = jnp.concatenate([vals[plan[4, 2 * t]], vals[plan[4, 2 * t + 1]]], axis=0)
        b = side_by_side([back[plan[5, 2 * t]], back[plan[5, 2 * t + 1]]])
        acc = acc * plan[6, 2 * t].astype(F32) + jnp.dot(b, a, preferred_element_type=F32)
        sums[t] = acc
        return acc

    def back_hop(q, d):
        return pltpu.make_async_remote_copy(
            src_ref=sent.at[d, pl.ds(4 * q, 4)], dst_ref=arrived.at[d, pl.ds(4 * q, 4)],
            send_sem=bs.at[d, q], recv_sem=br.at[d, q],
            device_id={"vtx": v_right if d else v_left}, device_id_type=MESH,
        )

    def backward_quarter(q, acc):
        for u in range(QUARTER):
            acc = backward_pair(q * QUARTER + u, acc)
        for d in range(2):
            for j in range(4):
                sent[d, 4 * q + j] = sums[plan[7, 8 * q + 4 * d + j]].astype(BF16)
            back_hop(q, d).start()
        return acc

    acc = lax.fori_loop(0, 2, backward_quarter, jnp.zeros((FC, BS), F32))
    for trip in a_trips:
        trip.wait()
    land_a[g] = grads[rows_a(g)]
    sum_a[x] = jnp.sum(land_a[...].astype(F32), axis=0).astype(BF16)
    x_trips = exchange(x_peer, 3, lambda k: sum_a.at[x], sum_a, x, zs, zr)
    acc = lax.fori_loop(2, 4, backward_quarter, acc)
    for u in range(REST):
        acc = backward_pair(4 * QUARTER + u, acc)
    for trip in x_trips:
        trip.wait()
    whole[...] = (jnp.sum(sum_a[...].astype(F32), axis=0) * float(NV * ROWS) ** -0.5).astype(BF16)
    d_trips = exchange(g_peer, 7, lambda k: whole, grads_hbm, g, ds, dr)
    outs = [pltpu.make_async_copy(whole, grads_hbm.at[g], out_sem.at[6])]
    outs[-1].start()
    for b in range(NB):
        hidden[:, b * BS : (b + 1) * BS] = hid[plan[9, b]]
    outs.append(pltpu.make_async_copy(hidden, hidden_hbm, out_sem.at[1]))
    outs[-1].start()
    for p in range(PIECES):
        near = jnp.dot(ws_ref[...], slopes_of(p), preferred_element_type=F32)
        for k in range(PB):
            part[p * PB + k, :FC] = near[:, k * BS : (k + 1) * BS]
    for b in range(NB):
        base[b] = part[plan[9, b], :FC] + sums[plan[7, 2 * HALO + b]]
    for s in range(3):
        for p in range(PIECES):
            reduce_hop(p, s, way[p]).wait_send()
            gather_hop(p, s, way[p]).wait_send()
    for q in range(4):
        for d in range(2):
            back_hop(q, d).wait()
    for c in range(4):
        for b in range(8 * c, 8 * c + 8):
            extra = arrived[0, plan[8, b]].astype(F32) + arrived[1, plan[8, BS + b]].astype(F32)
            features[:, b * BS : (b + 1) * BS] = (base[b] + extra).astype(BF16)
        at = pl.ds(8 * c * BS, 8 * BS)
        outs.append(pltpu.make_async_copy(features.at[:, at], features_hbm.at[:, at], out_sem.at[2 + c]))
        outs[-1].start()
    for out in outs:
        out.wait()
    for trip in d_trips:
        trip.wait()


def layer_call(rows, cols, count, lists, feat, cot, degree, ws, wn, bias, vals):
    dma = pltpu.SemaphoreType.DMA
    V = pltpu.VMEM
    return pl.pallas_call(
        layer_kernel,
        out_shape=(
            jax.ShapeDtypeStruct((HC, ROWS), BF16),
            jax.ShapeDtypeStruct((FC, ROWS), BF16),
            jax.ShapeDtypeStruct((8, SL_A, BS), BF16),
        ),
        in_specs=[anyspace(), anyspace(), smem()] + [anyspace()] * 4 + [vmem()] * 2 + [anyspace()] * 2,
        out_specs=(anyspace(),) * 3,
        scratch_shapes=[
            V((NNZ,), I32),
            V((NNZ,), I32),
            V((2 * HALO,), I32),
            V((HC,), F32),
            V((NB, BS), I32),
            V((NB, 8, BS), F32),
            V((8, BS), I32),
            V((2, 8, BS), I32),
            pltpu.SMEM((2, 8, BS), I32),
            V((8, BS), I32),
            V((2, 8, BS), I32),
            V((16, ENT), I32),
            pltpu.SMEM((16, ENT), I32),
            V((EXT + 1, FC, BS), BF16),
            V((2, HALO, FC, BS), BF16),
            V((NB, HC, BS), BF16),
            V((NNZ + 1, BS, BS), BF16),
            V((PAIRS_B + 1, FC, BS), F32),
            V((2, HALO, FC, BS), BF16),
            V((NB, FC, BS), BF16),
            V((HID, FC), BF16),
            V((HID, FC), BF16),
            V((NB, HID, BS), F32),
            V((3, PIECES, PB, HC, BS), BF16),
            V((3, PIECES, PB, HC, BS), BF16),
            V((PIECES, NF, PB, HC, BS), BF16),
            V((NB, HC, BS), BF16),
            V((NB, FC, BS), BF16),
            V((NB, FC, BS), F32),
            V((HC, ROWS), BF16),
            V((2, HALO + 1, FC, BS), BF16),
            V((FC, ROWS), BF16),
            V((2, FC, HID), F32),
            V((4 * FC, BS), BF16),
            V((8, SL_A, BS), BF16),
            V((4, SL_A, BS), BF16),
            V((SL_A, BS), BF16),
            dma((5,)), dma((NB,)), dma((NB,)), dma((8,)), dma, dma((4,)), dma((4,)), dma((2, 4)), dma((2, 4)),
            dma((6, PIECES)), dma((6, PIECES)), dma((2, 4)), dma((2, 4)),
            dma((7,)), dma((7,)), dma((3,)), dma((3,)), dma((7,)), dma((7,)), dma((7,)),
        ],
        compiler_params=pltpu.CompilerParams(collective_id=0, has_side_effects=True, vmem_limit_bytes=60 * MB),
        name="layer",
    )(rows, cols, count, lists, feat, cot, degree, ws, wn, bias, vals)


def results_kernel(
    features_in, hidden_in, grads_hbm, hidden_out, features_out, self_hbm, neigh_hbm,
    features, hidden, grads, weights, in_sems, out_sems,
):
    share = FC // 4
    routes = [(hidden_in, hidden, hidden_out)]
    for c in range(4):
        at = pl.ds(c * share, share)
        routes.append((features_in.at[at], features.at[at], features_out.at[at]))
    grads_load = pltpu.make_async_copy(grads_hbm, grads, in_sems.at[5])
    grads_load.start()
    loads = [pltpu.make_async_copy(src, via, in_sems.at[k]) for k, (src, via, dst) in enumerate(routes)]
    outs = [pltpu.make_async_copy(via, dst, out_sems.at[k]) for k, (src, via, dst) in enumerate(routes)]
    for load in loads:
        load.start()
    grads_load.wait()
    every = grads[...].reshape(4 * FC, BS).astype(F32)
    for k, ref in ((0, self_hbm), (1, neigh_hbm)):
        for c in range(2):
            at = (2 * k + c) * FC
            weights[k, :, c * BS : (c + 1) * BS] = every[at : at + FC]
        outs.append(pltpu.make_async_copy(weights.at[k], ref, out_sems.at[5 + k]))
        outs[-1].start()
    for k in range(5):
        loads[k].wait()
        outs[k].start()
    for out in outs:
        out.wait()


def results_call(features, hidden, grads):
    V = pltpu.VMEM
    return pl.pallas_call(
        results_kernel,
        out_shape=(
            jax.ShapeDtypeStruct((HC, ROWS), BF16),
            jax.ShapeDtypeStruct((FC, ROWS), BF16),
            jax.ShapeDtypeStruct((FC, HID), F32),
            jax.ShapeDtypeStruct((FC, HID), F32),
        ),
        in_specs=[anyspace()] * 3,
        out_specs=(anyspace(),) * 4,
        scratch_shapes=[
            V((FC, ROWS), BF16),
            V((HC, ROWS), BF16),
            V((8, SL_A, BS), BF16),
            V((2, FC, HID), F32),
            pltpu.SemaphoreType.DMA((6,)),
            pltpu.SemaphoreType.DMA((7,)),
        ],
        compiler_params=pltpu.CompilerParams(vmem_limit_bytes=60 * MB),
        name="results",
    )(features, hidden, grads)


def on_device(
    features, w_self, w_neigh, bias_terms, block_vals, block_rows, block_cols, block_count, recv_lists, degree, cotangent
):
    hidden, grad_features, grads = layer_call(
        block_rows, block_cols, block_count, recv_lists, features.T, cotangent.T, degree.reshape(NB, BS),
        w_self, w_neigh, bias_terms, block_vals,
    )
    hidden, grad_features, grad_self, grad_neigh = results_call(grad_features, hidden, grads)
    return hidden.T, grad_features.T, grad_self, grad_neigh


def solution(mesh):
    placed = (
        P("vtx", "feat"), P("feat", None), P("feat", None), P("feat"), P("vtx", None, None), P("vtx"), P("vtx"), P("vtx"),
        P("vtx"), P("vtx"), P("vtx", "feat"),
    )
    return jax.shard_map(
        on_device,
        mesh=mesh,
        in_specs=placed,
        out_specs=(P("vtx", "feat"), P("vtx", "feat"), P("feat", None), P("feat", None)),
        check_vma=False,
    )
```

```python
import functools

import jax
import jax.numpy as jnp
from jax import lax
from jax.experimental import pallas as pl
from jax.experimental.pallas import tpu as pltpu
from jax.sharding import PartitionSpec as P

MESH = pl.DeviceIdType.MESH
F32, BF16, I32 = jnp.float32, jnp.bfloat16, jnp.int32
BS = 128
NB = 32
HALO = 16
NNZ = 320
EXT = NB + 2 * HALO
FC = 192
HID = 256
HC = 64
ROWS = NB * BS
NV, NF = 32, 4
ENT = 384
PIECES = 8
PB = NB // PIECES
PAIRS_F = (NNZ + NB) // 2
PAIRS_B = (NNZ + EXT) // 2
PIECE_PAIRS = PAIRS_F // PIECES
QUARTER = (NNZ + 2 * HALO) // 8
REST = PAIRS_B - 4 * QUARTER
ZERO = NB
SL_A = 4 * FC // 8
MB = 1 << 20


def vmem():
    return pl.BlockSpec(memory_space=pltpu.VMEM)


def smem():
    return pl.BlockSpec(memory_space=pltpu.SMEM)


def anyspace():
    return pl.BlockSpec(memory_space=pl.ANY)


def greet(peers):
    barrier = pltpu.get_barrier_semaphore()
    for peer in peers:
        pl.semaphore_signal(barrier, inc=1, device_id=peer, device_id_type=MESH)
    pl.semaphore_wait(barrier, len(peers))


def iota(shape, dim):
    return lax.broadcasted_iota(I32, shape, dim)


def as_column(row):
    n = row.shape[1]
    diagonal = iota((n, n), 0) == iota((n, n), 1)
    return jnp.sum(jnp.where(diagonal, row, jnp.zeros_like(row)), axis=1, keepdims=True, dtype=row.dtype)


def down(values):
    return jnp.sum(values, axis=0, keepdims=True, dtype=I32)


def group_sizes(key):
    size = jnp.sum(jnp.where(iota((EXT, ENT), 0) == key, 1, 0), axis=1, keepdims=True, dtype=I32)
    return ((size + 1) >> 1) << 1


def order_groups(key):
    block, lane = iota((EXT, ENT), 0), iota((EXT, ENT), 1)
    size = group_sizes(key)
    size_row = down(jnp.where(block == lane, size, 0))
    earlier = (size < size_row) | ((size == size_row) & (block < lane))
    place = down(jnp.where(earlier & (block < NB), 1, 0))
    place_col = as_column(place)[:EXT]
    at_place = down(jnp.where((place_col == lane) & (block < NB), block, 0))
    of_entry = down(jnp.where(block == key, place_col, 0))
    return place, at_place, of_entry


def order_slots(key):
    slot, lane = iota((EXT, ENT), 0), iota((EXT, ENT), 1)
    size = group_sizes(key)
    size_row = down(jnp.where(slot == lane, size, 0))
    earlier = (size < size_row) | ((size == size_row) & (slot < lane))
    side = jnp.where(slot < HALO, 0, jnp.where(slot < HALO + NB, 1, 2))
    lane_side = jnp.where(lane < HALO, 0, jnp.where(lane < HALO + NB, 1, 2))
    at_side = as_column(down(jnp.where(earlier & (side == lane_side), 1, 0)))[:EXT]
    slot, side = slot[:, :1], side[:, :1]
    turn = ((at_side >> 2) << 3) + (at_side & 3)
    order = jnp.where(side == 1, 2 * HALO + slot - HALO, turn + jnp.where(side == 2, 4, 0))
    of_entry = down(jnp.where(iota((EXT, ENT), 0) == key, order, 0))
    told = iota((EXT, BS), 1)
    told = jnp.where(told < HALO, told, told + NB)
    return of_entry, down(jnp.where(iota((EXT, BS), 0) == told, at_side, 0))


def pair_schedule(key, other, active):
    far = 1000
    sub, lane = iota((ENT, ENT), 0), iota((ENT, ENT), 1)
    key = jnp.where(active, key, far)
    key_col = as_column(key)
    rank = down(jnp.where((key_col == key) & (sub < lane), 1, 0))
    group, at = iota((EXT, ENT), 0), iota((EXT, ENT), 1)
    size = group_sizes(key)
    start = down(jnp.where(group < key, size, 0))
    slot = jnp.where(active, start + rank, far)
    hit = as_column(slot) == lane

    def at_slots(column, default):
        return down(jnp.where(hit, column - default, 0)) + default

    entry = at_slots(sub[:, :1], NNZ)
    source = at_slots(as_column(other), 0)
    goes_on = jnp.minimum(at_slots(as_column(rank), 1), 1)
    end = down(jnp.where(group <= at, size, 0))
    own = down(jnp.where(group == at, size, 0))
    done = jnp.where(own > 0, (end >> 1) - 1, PAIRS_B)
    return [jnp.clip(entry, 0, NNZ), jnp.clip(source, 0, EXT), goes_on, jnp.clip(done, 0, PAIRS_B)]


def inverse(lists, places, first):
    ours, place = as_column(lists), as_column(places)
    sub, lane = iota((BS, BS), 0), iota((BS, BS), 1)
    hit = (ours == lane) & (sub >= first) & (sub < first + HALO)
    return jnp.clip(down(jnp.where(hit, place - HALO, 0)) + HALO, 0, HALO)


def layer_kernel(
    rows_hbm, cols_hbm, count_ref, lists_hbm, feat_hbm, cot_hbm, degree_hbm, ws_ref, wn_ref, bias_hbm, vals_hbm,
    hidden_hbm, features_hbm, grads_hbm,
    rows_v, cols_v, lists_v, bias_v, degree_v, rdeg, lists_out, lists_in, lists_sm, places_out, places_in, plan_v, plan,
    ext, landed_halo, cot, vals, sums, sent, mean, wst, wnt, part, staged, landed, slopes, hid, back, base, hidden, arrived, features,
    total, grads, land_a, sum_a, whole,
    small_sem, feat_sem, cot_sem, vals_sem, sm_sem, ls, lr, hs, hr,
    send_sem, recv_sem, bs, br, as_, ar, zs, zr, ds, dr, out_sem,
):
    me = lax.axis_index("feat")
    right, left = lax.rem(me + 1, NF), lax.rem(me + NF - 1, NF)
    v = lax.axis_index("vtx")
    v_right, v_left = lax.rem(v + 1, NV), lax.rem(v + NV - 1, NV)
    core, x, z = lax.rem(v, 2), lax.rem(v // 2, 4), v // 8
    g = 2 * z + core

    def g_peer(k):
        other = lax.rem(g + k, 8)
        return other, {"vtx": ((other // 2) * 4 + x) * 2 + lax.rem(other, 2)}

    def x_peer(k):
        other = lax.rem(x + k, 4)
        return other, {"vtx": (z * 4 + other) * 2 + core}

    small = [
        pltpu.make_async_copy(src, dst, small_sem.at[k])
        for k, (src, dst) in enumerate(
            [(lists_hbm, lists_v), (rows_hbm, rows_v), (cols_hbm, cols_v), (bias_hbm, bias_v), (degree_hbm, degree_v)]
        )
    ]
    feat_loads = [
        pltpu.make_async_copy(feat_hbm.at[:, pl.ds(b * BS, BS)], ext.at[b], feat_sem.at[b]) for b in range(NB)
    ]
    cot_loads = [
        pltpu.make_async_copy(cot_hbm.at[:, pl.ds(b * BS, BS)], cot.at[b], cot_sem.at[b]) for b in range(NB)
    ]
    share = NNZ // 8
    val_loads = [
        pltpu.make_async_copy(vals_hbm.at[pl.ds(k * share, share)], vals.at[pl.ds(k * share, share)], vals_sem.at[k])
        for k in range(8)
    ]
    for load in small + feat_loads:
        load.start()
    barrier = pltpu.get_barrier_semaphore()
    peers = (
        [{"vtx": v_left}, {"vtx": v_right}, {"feat": left}, {"feat": right}]
        + [g_peer(k)[1] for k in range(1, 8)]
        + [x_peer(k)[1] for k in range(1, 4)]
    )
    for peer in peers:
        pl.semaphore_signal(barrier, inc=1, device_id=peer, device_id_type=MESH)
    for load in val_loads + cot_loads:
        load.start()
    small[0].wait()
    lists_out[...] = jnp.full((8, BS), -1, I32)
    lists_out[0:1, : 2 * HALO] = lists_v[...].reshape(1, 2 * HALO)
    ext[ZERO] = jnp.zeros((FC, BS), BF16)
    vals[NNZ] = jnp.zeros((BS, BS), BF16)
    sums[PAIRS_B] = jnp.zeros((FC, BS), F32)
    pl.semaphore_wait(barrier, len(peers))

    trips = []
    for k, peer in ((0, v_right), (1, v_left)):
        trip = pltpu.make_async_remote_copy(
            src_ref=lists_out, dst_ref=lists_in.at[k], send_sem=ls.at[k], recv_sem=lr.at[k],
            device_id={"vtx": peer}, device_id_type=MESH,
        )
        trip.start()
        trips.append(trip)
    for load in small[1:] + feat_loads:
        load.wait()
    wst[...] = ws_ref[...].T
    wnt[...] = wn_ref[...].T
    bias = as_column(bias_v[...].reshape(1, HC))
    for b in range(NB):
        rdeg[b] = jnp.broadcast_to(1.0 / degree_v[b : b + 1, :].astype(F32), (8, BS))
    for trip in trips:
        trip.wait()
    local = pltpu.make_async_copy(lists_in, lists_sm, sm_sem)
    local.start()
    local.wait()
    halo_trips = []
    for q in range(4):
        for d in range(2):
            for j in range(4 * q, 4 * q + 4):
                sent[d, j] = ext[lax.rem(lists_sm[1 - d, 0, j + HALO * d] + NB + 1, NB + 1)]
            trip = pltpu.make_async_remote_copy(
                src_ref=sent.at[d, pl.ds(4 * q, 4)], dst_ref=landed_halo.at[d, pl.ds(4 * q, 4)],
                send_sem=hs.at[d, q], recv_sem=hr.at[d, q],
                device_id={"vtx": v_right if d == 0 else v_left}, device_id_type=MESH,
            )
            trip.start()
            halo_trips.append(trip)

    def wide(ref):
        return jnp.concatenate([ref[...].reshape(1, NNZ), jnp.zeros((1, ENT - NNZ), I32)], axis=1)

    rows, cols = wide(rows_v), wide(cols_v)
    active = iota((1, ENT), 1) < count_ref[0]
    where_col = jnp.where(cols < HALO, cols + NB + 1, jnp.where(cols < HALO + NB, cols - HALO, cols + 1))
    slot_place, places = order_slots(jnp.where(active, cols, 1000))
    places_out[...] = jnp.broadcast_to(places, (8, BS))
    place_trips = []
    for k, peer in ((0, v_right), (1, v_left)):
        trip = pltpu.make_async_remote_copy(
            src_ref=places_out, dst_ref=places_in.at[k], send_sem=ls.at[2 + k], recv_sem=lr.at[2 + k],
            device_id={"vtx": peer}, device_id_type=MESH,
        )
        trip.start()
        place_trips.append(trip)
    place, at_place, entry_place = order_groups(jnp.where(active, rows, 1000))
    table = pair_schedule(entry_place, where_col, active) + pair_schedule(slot_place, entry_place, active)
    table += [jnp.zeros((1, ENT), I32), jnp.clip(place, 0, NB - 1), jnp.clip(at_place, 0, NB - 1)]
    for k, row in enumerate(table):
        plan_v[k : k + 1] = row
    for k in range(len(table), 16):
        plan_v[k : k + 1] = jnp.zeros((1, ENT), I32)
    local = pltpu.make_async_copy(plan_v, plan, sm_sem)
    local.start()
    local.wait()

    def block_at(q):
        return plan[10, q]

    def side_by_side(blocks):
        return jnp.concatenate(blocks, axis=1)

    for p in range(PIECES):
        own = side_by_side([ext[block_at(p * PB + k)] for k in range(PB)])
        pre = jnp.dot(wst[...], own, preferred_element_type=F32)
        for k in range(PB):
            part[p * PB + k] = pre[:, k * BS : (k + 1) * BS]
    for trip in place_trips:
        trip.wait()
    from_right = inverse(lists_in[1, 0:1], places_in[1, 0:1], 0)
    from_left = inverse(lists_in[0, 0:1], places_in[0, 0:1], HALO)
    plan_v[8:9] = jnp.concatenate([from_right, from_left, jnp.zeros((1, BS), I32)], axis=1)
    local = pltpu.make_async_copy(plan_v.at[pl.ds(8, 8)], plan.at[pl.ds(8, 8)], sm_sem)
    local.start()
    for d in range(2):
        arrived[d, HALO] = jnp.zeros((FC, BS), BF16)
    local.wait()
    for load in val_loads + cot_loads:
        load.wait()
    for trip in halo_trips:
        trip.wait()
    for d in range(2):
        for j in range(HALO):
            ext[NB + 1 + HALO * d + j] = landed_halo[d, j]

    way = {p: 1 - 2 * (p % 2) for p in range(PIECES)}
    peer_of = {1: right, -1: left}

    def chunk(w, back_by):
        return lax.rem(me - w * back_by + 2 * NF, NF)

    def reduce_hop(p, s, w):
        return pltpu.make_async_remote_copy(
            src_ref=staged.at[s, p], dst_ref=landed.at[s, p],
            send_sem=send_sem.at[s, p], recv_sem=recv_sem.at[s, p],
            device_id={"feat": peer_of[w]}, device_id_type=MESH,
        )

    def gather_hop(p, s, w):
        owner = chunk(w, s)
        return pltpu.make_async_remote_copy(
            src_ref=slopes.at[p, owner], dst_ref=slopes.at[p, owner],
            send_sem=send_sem.at[3 + s, p], recv_sem=recv_sem.at[3 + s, p],
            device_id={"feat": peer_of[w]}, device_id_type=MESH,
        )

    def chunk_rows(c):
        return pl.ds(pl.multiple_of(c * HC, HC), HC)

    def forward_product(t):
        a = side_by_side([vals[plan[0, 2 * t]], vals[plan[0, 2 * t + 1]]])
        x = side_by_side([ext[plan[1, 2 * t]], ext[plan[1, 2 * t + 1]]])
        return lax.dot_general(x, a, (((1,), (1,)), ((), ())), preferred_element_type=F32)

    def reduce_on(p, s, w):
        reduce_hop(p, s - 1, w).wait_recv()
        for k in range(PB):
            more = part[p * PB + k, chunk_rows(chunk(w, 1 + s))]
            staged[s, p, k] = (landed[s - 1, p, k].astype(F32) + more).astype(BF16)
        reduce_hop(p, s, w).start()

    def forward_pieces(i, acc):
        for w in (1, -1):
            p = 2 * i + (0 if w == 1 else 1)
            for u in range(PIECE_PAIRS):
                t = p * PIECE_PAIRS + u
                acc = acc * plan[2, 2 * t].astype(F32) + forward_product(t)
                sums[t] = acc
            for k in range(PB):
                q = p * PB + k
                scale = rdeg[block_at(q)][0:1]
                mean[q] = (sums[plan[3, q]] * scale).astype(BF16)
            pre = jnp.dot(wnt[...], side_by_side([mean[p * PB + k] for k in range(PB)]), preferred_element_type=F32)
            for k in range(PB):
                q = p * PB + k
                part[q] = part[q] + pre[:, k * BS : (k + 1) * BS]
                staged[0, p, k] = part[q, chunk_rows(chunk(w, 1))].astype(BF16)
            reduce_hop(p, 0, w).start()
        return acc

    acc = forward_pieces(0, jnp.zeros((FC, BS), F32))

    def forward_step(i, acc):
        acc = forward_pieces(i, acc)
        for w in (1, -1):
            reduce_on(2 * i - 2 + (0 if w == 1 else 1), 1, w)
        return acc

    lax.fori_loop(1, PIECES // 2, forward_step, acc)
    for p in (PIECES - 2, PIECES - 1):
        reduce_on(p, 1, way[p])
    for p in range(PIECES):
        reduce_on(p, 2, way[p])
    for p in range(PIECES):
        reduce_hop(p, 2, way[p]).wait_recv()
        for k in range(PB):
            q = p * PB + k
            pre = landed[2, p, k].astype(F32) + part[q, chunk_rows(me)] + bias
            squash = 1.0 / (1.0 + jnp.exp(-pre))
            hid[q] = (pre * squash).astype(BF16)
            slope = cot[block_at(q)].astype(F32) * squash * (1.0 + pre * (1.0 - squash))
            slopes[p, me, k] = slope.astype(BF16)
        gather_hop(p, 0, way[p]).start()
    for s in range(1, 3):
        for p in range(PIECES):
            gather_hop(p, s - 1, way[p]).wait_recv()
            gather_hop(p, s, way[p]).start()
    total[...] = jnp.zeros_like(total)
    lanes = (((1,), (1,)), ((), ()))

    def slopes_of(p):
        return side_by_side([slopes[p, :, k].reshape(HID, BS) for k in range(PB)])

    for p in range(PIECES):
        gather_hop(p, 2, way[p]).wait_recv()
        full = slopes_of(p)
        far = jnp.dot(wn_ref[...], full, preferred_element_type=F32)
        for k in range(PB):
            q = p * PB + k
            back[q] = (far[:, k * BS : (k + 1) * BS] * rdeg[block_at(q)][0:1]).astype(BF16)
        own = side_by_side([ext[block_at(p * PB + k)] for k in range(PB)])
        near = side_by_side([mean[p * PB + k] for k in range(PB)])
        total[0] += lax.dot_general(own, full, lanes, preferred_element_type=F32)
        total[1] += lax.dot_general(near, full, lanes, preferred_element_type=F32)
    for k in range(2):
        for c in range(2):
            at = (2 * k + c) * FC
            grads[at : at + FC] = total[k, :, c * BS : (c + 1) * BS].astype(BF16)

    def exchange(peer_at, count, src_of, dst, mine, send, recv):
        trips = []
        for k in range(1, count + 1):
            other, device = peer_at(k)
            trips.append(pltpu.make_async_remote_copy(
                src_ref=src_of(other), dst_ref=dst.at[mine], send_sem=send.at[k - 1], recv_sem=recv.at[k - 1],
                device_id=device, device_id_type=MESH,
            ))
        for trip in trips:
            trip.start()
        return trips

    def rows_a(k):
        return pl.ds(pl.multiple_of(k * SL_A, 32), SL_A)

    a_trips = exchange(g_peer, 7, lambda k: grads.at[rows_a(k)], land_a, g, as_, ar)

    def backward_pair(t, acc):
        a = jnp.concatenate([vals[plan[4, 2 * t]], vals[plan[4, 2 * t + 1]]], axis=0)
        b = side_by_side([back[plan[5, 2 * t]], back[plan[5, 2 * t + 1]]])
        acc = acc * plan[6, 2 * t].astype(F32) + jnp.dot(b, a, preferred_element_type=F32)
        sums[t] = acc
        return acc

    def back_hop(q, d):
        return pltpu.make_async_remote_copy(
            src_ref=sent.at[d, pl.ds(4 * q, 4)], dst_ref=arrived.at[d, pl.ds(4 * q, 4)],
            send_sem=bs.at[d, q], recv_sem=br.at[d, q],
            device_id={"vtx": v_right if d else v_left}, device_id_type=MESH,
        )

    def backward_quarter(q, acc):
        for u in range(QUARTER):
            acc = backward_pair(q * QUARTER + u, acc)
        for d in range(2):
            for j in range(4):
                sent[d, 4 * q + j] = sums[plan[7, 8 * q + 4 * d + j]].astype(BF16)
            back_hop(q, d).start()
        return acc

    acc = lax.fori_loop(0, 2, backward_quarter, jnp.zeros((FC, BS), F32))
    for trip in a_trips:
        trip.wait()
    land_a[g] = grads[rows_a(g)]
    sum_a[x] = jnp.sum(land_a[...].astype(F32), axis=0).astype(BF16)
    x_trips = exchange(x_peer, 3, lambda k: sum_a.at[x], sum_a, x, zs, zr)
    acc = lax.fori_loop(2, 4, backward_quarter, acc)
    for u in range(REST):
        acc = backward_pair(4 * QUARTER + u, acc)
    for trip in x_trips:
        trip.wait()
    whole[...] = (jnp.sum(sum_a[...].astype(F32), axis=0) * float(NV * ROWS) ** -0.5).astype(BF16)
    d_trips = exchange(g_peer, 7, lambda k: whole, grads_hbm, g, ds, dr)
    outs = [pltpu.make_async_copy(whole, grads_hbm.at[g], out_sem.at[6])]
    outs[-1].start()
    for b in range(NB):
        hidden[:, b * BS : (b + 1) * BS] = hid[plan[9, b]]
    outs.append(pltpu.make_async_copy(hidden, hidden_hbm, out_sem.at[1]))
    outs[-1].start()
    for p in range(PIECES):
        near = jnp.dot(ws_ref[...], slopes_of(p), preferred_element_type=F32)
        for k in range(PB):
            part[p * PB + k, :FC] = near[:, k * BS : (k + 1) * BS]
    for b in range(NB):
        base[b] = part[plan[9, b], :FC] + sums[plan[7, 2 * HALO + b]]
    for s in range(3):
        for p in range(PIECES):
            reduce_hop(p, s, way[p]).wait_send()
            gather_hop(p, s, way[p]).wait_send()
    for q in range(4):
        for d in range(2):
            back_hop(q, d).wait()
    for c in range(4):
        for b in range(8 * c, 8 * c + 8):
            extra = arrived[0, plan[8, b]].astype(F32) + arrived[1, plan[8, BS + b]].astype(F32)
            features[:, b * BS : (b + 1) * BS] = (base[b] + extra).astype(BF16)
        at = pl.ds(8 * c * BS, 8 * BS)
        outs.append(pltpu.make_async_copy(features.at[:, at], features_hbm.at[:, at], out_sem.at[2 + c]))
        outs[-1].start()
    for out in outs:
        out.wait()
    for trip in d_trips:
        trip.wait()


def layer_call(rows, cols, count, lists, feat, cot, degree, ws, wn, bias, vals):
    dma = pltpu.SemaphoreType.DMA
    V = pltpu.VMEM
    return pl.pallas_call(
        layer_kernel,
        out_shape=(
            jax.ShapeDtypeStruct((HC, ROWS), BF16),
            jax.ShapeDtypeStruct((FC, ROWS), BF16),
            jax.ShapeDtypeStruct((8, SL_A, BS), BF16),
        ),
        in_specs=[anyspace(), anyspace(), smem()] + [anyspace()] * 4 + [vmem()] * 2 + [anyspace()] * 2,
        out_specs=(anyspace(),) * 3,
        scratch_shapes=[
            V((NNZ,), I32),
            V((NNZ,), I32),
            V((2 * HALO,), I32),
            V((HC,), F32),
            V((NB, BS), I32),
            V((NB, 8, BS), F32),
            V((8, BS), I32),
            V((2, 8, BS), I32),
            pltpu.SMEM((2, 8, BS), I32),
            V((8, BS), I32),
            V((2, 8, BS), I32),
            V((16, ENT), I32),
            pltpu.SMEM((16, ENT), I32),
            V((EXT + 1, FC, BS), BF16),
            V((2, HALO, FC, BS), BF16),
            V((NB, HC, BS), BF16),
            V((NNZ + 1, BS, BS), BF16),
            V((PAIRS_B + 1, FC, BS), F32),
            V((2, HALO, FC, BS), BF16),
            V((NB, FC, BS), BF16),
            V((HID, FC), BF16),
            V((HID, FC), BF16),
            V((NB, HID, BS), F32),
            V((3, PIECES, PB, HC, BS), BF16),
            V((3, PIECES, PB, HC, BS), BF16),
            V((PIECES, NF, PB, HC, BS), BF16),
            V((NB, HC, BS), BF16),
            V((NB, FC, BS), BF16),
            V((NB, FC, BS), F32),
            V((HC, ROWS), BF16),
            V((2, HALO + 1, FC, BS), BF16),
            V((FC, ROWS), BF16),
            V((2, FC, HID), F32),
            V((4 * FC, BS), BF16),
            V((8, SL_A, BS), BF16),
            V((4, SL_A, BS), BF16),
            V((SL_A, BS), BF16),
            dma((5,)), dma((NB,)), dma((NB,)), dma((8,)), dma, dma((4,)), dma((4,)), dma((2, 4)), dma((2, 4)),
            dma((6, PIECES)), dma((6, PIECES)), dma((2, 4)), dma((2, 4)),
            dma((7,)), dma((7,)), dma((3,)), dma((3,)), dma((7,)), dma((7,)), dma((7,)),
        ],
        compiler_params=pltpu.CompilerParams(collective_id=0, has_side_effects=True, vmem_limit_bytes=60 * MB),
        name="layer",
    )(rows, cols, count, lists, feat, cot, degree, ws, wn, bias, vals)


def results_kernel(
    features_in, hidden_in, grads_hbm, hidden_out, features_out, self_hbm, neigh_hbm,
    features, hidden, grads, weights, in_sems, out_sems,
):
    share = FC // 4
    routes = [(hidden_in, hidden, hidden_out)]
    for c in range(4):
        at = pl.ds(c * share, share)
        routes.append((features_in.at[at], features.at[at], features_out.at[at]))
    grads_load = pltpu.make_async_copy(grads_hbm, grads, in_sems.at[5])
    grads_load.start()
    loads = [pltpu.make_async_copy(src, via, in_sems.at[k]) for k, (src, via, dst) in enumerate(routes)]
    outs = [pltpu.make_async_copy(via, dst, out_sems.at[k]) for k, (src, via, dst) in enumerate(routes)]
    for load in loads:
        load.start()
    grads_load.wait()
    every = grads[...].reshape(4 * FC, BS).astype(F32)
    for k, ref in ((0, self_hbm), (1, neigh_hbm)):
        for c in range(2):
            at = (2 * k + c) * FC
            weights[k, :, c * BS : (c + 1) * BS] = every[at : at + FC]
        outs.append(pltpu.make_async_copy(weights.at[k], ref, out_sems.at[5 + k]))
        outs[-1].start()
    for k in range(5):
        loads[k].wait()
        outs[k].start()
    for out in outs:
        out.wait()


def results_call(features, hidden, grads):
    V = pltpu.VMEM
    return pl.pallas_call(
        results_kernel,
        out_shape=(
            jax.ShapeDtypeStruct((HC, ROWS), BF16),
            jax.ShapeDtypeStruct((FC, ROWS), BF16),
            jax.ShapeDtypeStruct((FC, HID), F32),
            jax.ShapeDtypeStruct((FC, HID), F32),
        ),
        in_specs=[anyspace()] * 3,
        out_specs=(anyspace(),) * 4,
        scratch_shapes=[
            V((FC, ROWS), BF16),
            V((HC, ROWS), BF16),
            V((8, SL_A, BS), BF16),
            V((2, FC, HID), F32),
            pltpu.SemaphoreType.DMA((6,)),
            pltpu.SemaphoreType.DMA((7,)),
        ],
        compiler_params=pltpu.CompilerParams(vmem_limit_bytes=60 * MB),
        name="results",
    )(features, hidden, grads)


def on_device(
    features, w_self, w_neigh, bias_terms, block_vals, block_rows, block_cols, block_count, recv_lists, degree, cotangent
):
    hidden, grad_features, grads = layer_call(
        block_rows, block_cols, block_count, recv_lists, features.T, cotangent.T, degree.reshape(NB, BS),
        w_self, w_neigh, bias_terms, block_vals,
    )
    hidden, grad_features, grad_self, grad_neigh = results_call(grad_features, hidden, grads)
    return hidden.T, grad_features.T, grad_self, grad_neigh


def solution(mesh):
    placed = (
        P("vtx", "feat"), P("feat", None), P("feat", None), P("feat"), P("vtx", None, None), P("vtx"), P("vtx"), P("vtx"),
        P("vtx"), P("vtx"), P("vtx", "feat"),
    )
    return jax.shard_map(
        on_device,
        mesh=mesh,
        in_specs=placed,
        out_specs=(P("vtx", "feat"), P("vtx", "feat"), P("feat", None), P("feat", None)),
        check_vma=False,
    )
```

```python
import functools

import jax
import jax.numpy as jnp
from jax import lax
from jax.experimental import pallas as pl
from jax.experimental.pallas import tpu as pltpu
from jax.sharding import PartitionSpec as P

MESH = pl.DeviceIdType.MESH
F32, BF16, I32 = jnp.float32, jnp.bfloat16, jnp.int32
BS = 128
NB = 32
HALO = 16
NNZ = 320
EXT = NB + 2 * HALO
FC = 192
HID = 256
HC = 64
ROWS = NB * BS
NV, NF = 32, 4
ENT = 384
PIECES = 8
PB = NB // PIECES
PAIRS_F = (NNZ + NB) // 2
PAIRS_B = (NNZ + EXT) // 2
PIECE_PAIRS = PAIRS_F // PIECES
QUARTER = (NNZ + 2 * HALO) // 8
REST = PAIRS_B - 4 * QUARTER
ZERO = NB
SL_A = 4 * FC // 8
MB = 1 << 20


def vmem():
    return pl.BlockSpec(memory_space=pltpu.VMEM)


def smem():
    return pl.BlockSpec(memory_space=pltpu.SMEM)


def anyspace():
    return pl.BlockSpec(memory_space=pl.ANY)


def greet(peers):
    barrier = pltpu.get_barrier_semaphore()
    for peer in peers:
        pl.semaphore_signal(barrier, inc=1, device_id=peer, device_id_type=MESH)
    pl.semaphore_wait(barrier, len(peers))


def iota(shape, dim):
    return lax.broadcasted_iota(I32, shape, dim)


def as_column(row):
    n = row.shape[1]
    diagonal = iota((n, n), 0) == iota((n, n), 1)
    return jnp.sum(jnp.where(diagonal, row, jnp.zeros_like(row)), axis=1, keepdims=True, dtype=row.dtype)


def down(values):
    return jnp.sum(values, axis=0, keepdims=True, dtype=I32)


def group_sizes(key):
    size = jnp.sum(jnp.where(iota((EXT, ENT), 0) == key, 1, 0), axis=1, keepdims=True, dtype=I32)
    return ((size + 1) >> 1) << 1


def order_groups(key):
    block, lane = iota((EXT, ENT), 0), iota((EXT, ENT), 1)
    size = group_sizes(key)
    size_row = down(jnp.where(block == lane, size, 0))
    earlier = (size < size_row) | ((size == size_row) & (block < lane))
    place = down(jnp.where(earlier & (block < NB), 1, 0))
    place_col = as_column(place)[:EXT]
    at_place = down(jnp.where((place_col == lane) & (block < NB), block, 0))
    of_entry = down(jnp.where(block == key, place_col, 0))
    return place, at_place, of_entry


def order_slots(key):
    slot, lane = iota((EXT, ENT), 0), iota((EXT, ENT), 1)
    size = group_sizes(key)
    size_row = down(jnp.where(slot == lane, size, 0))
    earlier = (size < size_row) | ((size == size_row) & (slot < lane))
    side = jnp.where(slot < HALO, 0, jnp.where(slot < HALO + NB, 1, 2))
    lane_side = jnp.where(lane < HALO, 0, jnp.where(lane < HALO + NB, 1, 2))
    at_side = as_column(down(jnp.where(earlier & (side == lane_side), 1, 0)))[:EXT]
    slot, side = slot[:, :1], side[:, :1]
    turn = ((at_side >> 2) << 3) + (at_side & 3)
    order = jnp.where(side == 1, 2 * HALO + slot - HALO, turn + jnp.where(side == 2, 4, 0))
    of_entry = down(jnp.where(iota((EXT, ENT), 0) == key, order, 0))
    told = iota((EXT, BS), 1)
    told = jnp.where(told < HALO, told, told + NB)
    return of_entry, down(jnp.where(iota((EXT, BS), 0) == told, at_side, 0))


def pair_schedule(key, other, active):
    far = 1000
    sub, lane = iota((ENT, ENT), 0), iota((ENT, ENT), 1)
    key = jnp.where(active, key, far)
    key_col = as_column(key)
    rank = down(jnp.where((key_col == key) & (sub < lane), 1, 0))
    group, at = iota((EXT, ENT), 0), iota((EXT, ENT), 1)
    size = group_sizes(key)
    start = down(jnp.where(group < key, size, 0))
    slot = jnp.where(active, start + rank, far)
    hit = as_column(slot) == lane

    def at_slots(column, default):
        return down(jnp.where(hit, column - default, 0)) + default

    entry = at_slots(sub[:, :1], NNZ)
    source = at_slots(as_column(other), 0)
    goes_on = jnp.minimum(at_slots(as_column(rank), 1), 1)
    end = down(jnp.where(group <= at, size, 0))
    own = down(jnp.where(group == at, size, 0))
    done = jnp.where(own > 0, (end >> 1) - 1, PAIRS_B)
    return [jnp.clip(entry, 0, NNZ), jnp.clip(source, 0, EXT), goes_on, jnp.clip(done, 0, PAIRS_B)]


def inverse(lists, places, first):
    ours, place = as_column(lists), as_column(places)
    sub, lane = iota((BS, BS), 0), iota((BS, BS), 1)
    hit = (ours == lane) & (sub >= first) & (sub < first + HALO)
    return jnp.clip(down(jnp.where(hit, place - HALO, 0)) + HALO, 0, HALO)


def layer_kernel(
    rows_hbm, cols_hbm, count_ref, lists_hbm, feat_hbm, cot_hbm, degree_hbm, ws_ref, wn_ref, bias_hbm, vals_hbm,
    hidden_hbm, features_hbm, grads_hbm,
    rows_v, cols_v, lists_v, bias_v, degree_v, rdeg, lists_out, lists_in, lists_sm, places_out, places_in, plan_v, plan,
    ext, landed_halo, cot, vals, sums, sent, mean, wst, wnt, part, staged, landed, slopes, hid, back, base, hidden, arrived, features,
    total, grads, land_a, sum_a, whole,
    small_sem, feat_sem, cot_sem, vals_sem, sm_sem, ls, lr, hs, hr,
    send_sem, recv_sem, bs, br, as_, ar, zs, zr, ds, dr, out_sem,
):
    me = lax.axis_index("feat")
    right, left = lax.rem(me + 1, NF), lax.rem(me + NF - 1, NF)
    v = lax.axis_index("vtx")
    v_right, v_left = lax.rem(v + 1, NV), lax.rem(v + NV - 1, NV)
    core, x, z = lax.rem(v, 2), lax.rem(v // 2, 4), v // 8
    g = 2 * z + core

    def g_peer(k):
        other = lax.rem(g + k, 8)
        return other, {"vtx": ((other // 2) * 4 + x) * 2 + lax.rem(other, 2)}

    def x_peer(k):
        other = lax.rem(x + k, 4)
        return other, {"vtx": (z * 4 + other) * 2 + core}

    small = [
        pltpu.make_async_copy(src, dst, small_sem.at[k])
        for k, (src, dst) in enumerate(
            [(lists_hbm, lists_v), (rows_hbm, rows_v), (cols_hbm, cols_v), (bias_hbm, bias_v), (degree_hbm, degree_v)]
        )
    ]
    feat_loads = [
        pltpu.make_async_copy(feat_hbm.at[:, pl.ds(b * BS, BS)], ext.at[b], feat_sem.at[b]) for b in range(NB)
    ]
    cot_loads = [
        pltpu.make_async_copy(cot_hbm.at[:, pl.ds(b * BS, BS)], cot.at[b], cot_sem.at[b]) for b in range(NB)
    ]
    share = NNZ // 8
    val_loads = [
        pltpu.make_async_copy(vals_hbm.at[pl.ds(k * share, share)], vals.at[pl.ds(k * share, share)], vals_sem.at[k])
        for k in range(8)
    ]
    for load in small + feat_loads:
        load.start()
    barrier = pltpu.get_barrier_semaphore()
    peers = (
        [{"vtx": v_left}, {"vtx": v_right}, {"feat": left}, {"feat": right}]
        + [g_peer(k)[1] for k in range(1, 8)]
        + [x_peer(k)[1] for k in range(1, 4)]
    )
    for peer in peers:
        pl.semaphore_signal(barrier, inc=1, device_id=peer, device_id_type=MESH)
    for load in val_loads + cot_loads:
        load.start()
    small[0].wait()
    lists_out[...] = jnp.full((8, BS), -1, I32)
    lists_out[0:1, : 2 * HALO] = lists_v[...].reshape(1, 2 * HALO)
    ext[ZERO] = jnp.zeros((FC, BS), BF16)
    vals[NNZ] = jnp.zeros((BS, BS), BF16)
    sums[PAIRS_B] = jnp.zeros((FC, BS), F32)
    pl.semaphore_wait(barrier, len(peers))

    trips = []
    for k, peer in ((0, v_right), (1, v_left)):
        trip = pltpu.make_async_remote_copy(
            src_ref=lists_out, dst_ref=lists_in.at[k], send_sem=ls.at[k], recv_sem=lr.at[k],
            device_id={"vtx": peer}, device_id_type=MESH,
        )
        trip.start()
        trips.append(trip)
    for load in small[1:] + feat_loads:
        load.wait()
    wst[...] = ws_ref[...].T
    wnt[...] = wn_ref[...].T
    bias = as_column(bias_v[...].reshape(1, HC))
    for b in range(NB):
        rdeg[b] = jnp.broadcast_to(1.0 / degree_v[b : b + 1, :].astype(F32), (8, BS))
    for trip in trips:
        trip.wait()
    local = pltpu.make_async_copy(lists_in, lists_sm, sm_sem)
    local.start()
    local.wait()
    halo_trips = []
    for d in range(2):
        for j in range(HALO):
            sent[d, j] = ext[lax.rem(lists_sm[1 - d, 0, j + HALO * d] + NB + 1, NB + 1)]
        trip = pltpu.make_async_remote_copy(
            src_ref=sent.at[d], dst_ref=landed_halo.at[d], send_sem=hs.at[d], recv_sem=hr.at[d],
            device_id={"vtx": v_right if d == 0 else v_left}, device_id_type=MESH,
        )
        trip.start()
        halo_trips.append(trip)

    def wide(ref):
        return jnp.concatenate([ref[...].reshape(1, NNZ), jnp.zeros((1, ENT - NNZ), I32)], axis=1)

    rows, cols = wide(rows_v), wide(cols_v)
    active = iota((1, ENT), 1) < count_ref[0]
    where_col = jnp.where(cols < HALO, cols + NB + 1, jnp.where(cols < HALO + NB, cols - HALO, cols + 1))
    slot_place, places = order_slots(jnp.where(active, cols, 1000))
    places_out[...] = jnp.broadcast_to(places, (8, BS))
    place_trips = []
    for k, peer in ((0, v_right), (1, v_left)):
        trip = pltpu.make_async_remote_copy(
            src_ref=places_out, dst_ref=places_in.at[k], send_sem=ls.at[2 + k], recv_sem=lr.at[2 + k],
            device_id={"vtx": peer}, device_id_type=MESH,
        )
        trip.start()
        place_trips.append(trip)
    place, at_place, entry_place = order_groups(jnp.where(active, rows, 1000))
    table = pair_schedule(entry_place, where_col, active) + pair_schedule(slot_place, entry_place, active)
    table += [jnp.zeros((1, ENT), I32), jnp.clip(place, 0, NB - 1), jnp.clip(at_place, 0, NB - 1)]
    for k, row in enumerate(table):
        plan_v[k : k + 1] = row
    for k in range(len(table), 16):
        plan_v[k : k + 1] = jnp.zeros((1, ENT), I32)
    local = pltpu.make_async_copy(plan_v, plan, sm_sem)
    local.start()
    local.wait()

    def block_at(q):
        return plan[10, q]

    def side_by_side(blocks):
        return jnp.concatenate(blocks, axis=1)

    for p in range(PIECES):
        own = side_by_side([ext[block_at(p * PB + k)] for k in range(PB)])
        pre = jnp.dot(wst[...], own, preferred_element_type=F32)
        for k in range(PB):
            part[p * PB + k] = pre[:, k * BS : (k + 1) * BS]
    for trip in place_trips:
        trip.wait()
    from_right = inverse(lists_in[1, 0:1], places_in[1, 0:1], 0)
    from_left = inverse(lists_in[0, 0:1], places_in[0, 0:1], HALO)
    plan_v[8:9] = jnp.concatenate([from_right, from_left, jnp.zeros((1, BS), I32)], axis=1)
    local = pltpu.make_async_copy(plan_v.at[pl.ds(8, 8)], plan.at[pl.ds(8, 8)], sm_sem)
    local.start()
    for d in range(2):
        arrived[d, HALO] = jnp.zeros((FC, BS), BF16)
    local.wait()
    for load in val_loads + cot_loads:
        load.wait()
    for trip in halo_trips:
        trip.wait()
    for d in range(2):
        for j in range(HALO):
            ext[NB + 1 + HALO * d + j] = landed_halo[d, j]

    way = {p: 1 - 2 * (p % 2) for p in range(PIECES)}
    peer_of = {1: right, -1: left}

    def chunk(w, back_by):
        return lax.rem(me - w * back_by + 2 * NF, NF)

    def reduce_hop(p, s, w):
        return pltpu.make_async_remote_copy(
            src_ref=staged.at[s, p], dst_ref=landed.at[s, p],
            send_sem=send_sem.at[s, p], recv_sem=recv_sem.at[s, p],
            device_id={"feat": peer_of[w]}, device_id_type=MESH,
        )

    def gather_hop(p, s, w):
        owner = chunk(w, s)
        return pltpu.make_async_remote_copy(
            src_ref=slopes.at[p, owner], dst_ref=slopes.at[p, owner],
            send_sem=send_sem.at[3 + s, p], recv_sem=recv_sem.at[3 + s, p],
            device_id={"feat": peer_of[w]}, device_id_type=MESH,
        )

    def chunk_rows(c):
        return pl.ds(pl.multiple_of(c * HC, HC), HC)

    def forward_product(t):
        a = side_by_side([vals[plan[0, 2 * t]], vals[plan[0, 2 * t + 1]]])
        x = side_by_side([ext[plan[1, 2 * t]], ext[plan[1, 2 * t + 1]]])
        return lax.dot_general(x, a, (((1,), (1,)), ((), ())), preferred_element_type=F32)

    def reduce_on(p, s, w):
        reduce_hop(p, s - 1, w).wait_recv()
        for k in range(PB):
            more = part[p * PB + k, chunk_rows(chunk(w, 1 + s))]
            staged[s, p, k] = (landed[s - 1, p, k].astype(F32) + more).astype(BF16)
        reduce_hop(p, s, w).start()

    def forward_pieces(i, acc):
        for w in (1, -1):
            p = 2 * i + (0 if w == 1 else 1)
            for u in range(PIECE_PAIRS):
                t = p * PIECE_PAIRS + u
                acc = acc * plan[2, 2 * t].astype(F32) + forward_product(t)
                sums[t] = acc
            for k in range(PB):
                q = p * PB + k
                scale = rdeg[block_at(q)][0:1]
                mean[q] = (sums[plan[3, q]] * scale).astype(BF16)
            pre = jnp.dot(wnt[...], side_by_side([mean[p * PB + k] for k in range(PB)]), preferred_element_type=F32)
            for k in range(PB):
                q = p * PB + k
                part[q] = part[q] + pre[:, k * BS : (k + 1) * BS]
                staged[0, p, k] = part[q, chunk_rows(chunk(w, 1))].astype(BF16)
            reduce_hop(p, 0, w).start()
        return acc

    acc = forward_pieces(0, jnp.zeros((FC, BS), F32))

    def forward_step(i, acc):
        acc = forward_pieces(i, acc)
        for w in (1, -1):
            reduce_on(2 * i - 2 + (0 if w == 1 else 1), 1, w)
        return acc

    lax.fori_loop(1, PIECES // 2, forward_step, acc)
    for p in (PIECES - 2, PIECES - 1):
        reduce_on(p, 1, way[p])
    for p in range(PIECES):
        reduce_on(p, 2, way[p])
    for p in range(PIECES):
        reduce_hop(p, 2, way[p]).wait_recv()
        for k in range(PB):
            q = p * PB + k
            pre = landed[2, p, k].astype(F32) + part[q, chunk_rows(me)] + bias
            squash = 1.0 / (1.0 + jnp.exp(-pre))
            hid[q] = (pre * squash).astype(BF16)
            slope = cot[block_at(q)].astype(F32) * squash * (1.0 + pre * (1.0 - squash))
            slopes[p, me, k] = slope.astype(BF16)
        gather_hop(p, 0, way[p]).start()
    for s in range(1, 3):
        for p in range(PIECES):
            gather_hop(p, s - 1, way[p]).wait_recv()
            gather_hop(p, s, way[p]).start()
    total[...] = jnp.zeros_like(total)
    lanes = (((1,), (1,)), ((), ()))

    def slopes_of(p):
        return side_by_side([slopes[p, :, k].reshape(HID, BS) for k in range(PB)])

    for p in range(PIECES):
        gather_hop(p, 2, way[p]).wait_recv()
        full = slopes_of(p)
        far = jnp.dot(wn_ref[...], full, preferred_element_type=F32)
        for k in range(PB):
            q = p * PB + k
            back[q] = (far[:, k * BS : (k + 1) * BS] * rdeg[block_at(q)][0:1]).astype(BF16)
        own = side_by_side([ext[block_at(p * PB + k)] for k in range(PB)])
        near = side_by_side([mean[p * PB + k] for k in range(PB)])
        total[0] += lax.dot_general(own, full, lanes, preferred_element_type=F32)
        total[1] += lax.dot_general(near, full, lanes, preferred_element_type=F32)
    for k in range(2):
        for c in range(2):
            at = (2 * k + c) * FC
            grads[at : at + FC] = total[k, :, c * BS : (c + 1) * BS].astype(BF16)

    def exchange(peer_at, count, src_of, dst, mine, send, recv):
        trips = []
        for k in range(1, count + 1):
            other, device = peer_at(k)
            trips.append(pltpu.make_async_remote_copy(
                src_ref=src_of(other), dst_ref=dst.at[mine], send_sem=send.at[k - 1], recv_sem=recv.at[k - 1],
                device_id=device, device_id_type=MESH,
            ))
        for trip in trips:
            trip.start()
        return trips

    def rows_a(k):
        return pl.ds(pl.multiple_of(k * SL_A, 32), SL_A)

    a_trips = exchange(g_peer, 7, lambda k: grads.at[rows_a(k)], land_a, g, as_, ar)

    def backward_pair(t, acc):
        a = jnp.concatenate([vals[plan[4, 2 * t]], vals[plan[4, 2 * t + 1]]], axis=0)
        b = side_by_side([back[plan[5, 2 * t]], back[plan[5, 2 * t + 1]]])
        acc = acc * plan[6, 2 * t].astype(F32) + jnp.dot(b, a, preferred_element_type=F32)
        sums[t] = acc
        return acc

    def back_hop(q, d):
        return pltpu.make_async_remote_copy(
            src_ref=sent.at[d, pl.ds(4 * q, 4)], dst_ref=arrived.at[d, pl.ds(4 * q, 4)],
            send_sem=bs.at[d, q], recv_sem=br.at[d, q],
            device_id={"vtx": v_right if d else v_left}, device_id_type=MESH,
        )

    def backward_quarter(q, acc):
        for u in range(QUARTER):
            acc = backward_pair(q * QUARTER + u, acc)
        for d in range(2):
            for j in range(4):
                sent[d, 4 * q + j] = sums[plan[7, 8 * q + 4 * d + j]].astype(BF16)
            back_hop(q, d).start()
        return acc

    acc = lax.fori_loop(0, 2, backward_quarter, jnp.zeros((FC, BS), F32))
    for trip in a_trips:
        trip.wait()
    land_a[g] = grads[rows_a(g)]
    sum_a[x] = jnp.sum(land_a[...].astype(F32), axis=0).astype(BF16)
    x_trips = exchange(x_peer, 3, lambda k: sum_a.at[x], sum_a, x, zs, zr)
    acc = lax.fori_loop(2, 4, backward_quarter, acc)
    for u in range(REST):
        acc = backward_pair(4 * QUARTER + u, acc)
    for trip in x_trips:
        trip.wait()
    whole[...] = (jnp.sum(sum_a[...].astype(F32), axis=0) * float(NV * ROWS) ** -0.5).astype(BF16)
    d_trips = exchange(g_peer, 7, lambda k: whole, grads_hbm, g, ds, dr)
    outs = [pltpu.make_async_copy(whole, grads_hbm.at[g], out_sem.at[6])]
    outs[-1].start()
    for b in range(NB):
        hidden[:, b * BS : (b + 1) * BS] = hid[plan[9, b]]
    outs.append(pltpu.make_async_copy(hidden, hidden_hbm, out_sem.at[1]))
    outs[-1].start()
    for p in range(PIECES):
        near = jnp.dot(ws_ref[...], slopes_of(p), preferred_element_type=F32)
        for k in range(PB):
            part[p * PB + k, :FC] = near[:, k * BS : (k + 1) * BS]
    for b in range(NB):
        base[b] = part[plan[9, b], :FC] + sums[plan[7, 2 * HALO + b]]
    for s in range(3):
        for p in range(PIECES):
            reduce_hop(p, s, way[p]).wait_send()
            gather_hop(p, s, way[p]).wait_send()
    for q in range(4):
        for d in range(2):
            back_hop(q, d).wait()
    for c in range(4):
        for b in range(8 * c, 8 * c + 8):
            extra = arrived[0, plan[8, b]].astype(F32) + arrived[1, plan[8, BS + b]].astype(F32)
            features[:, b * BS : (b + 1) * BS] = (base[b] + extra).astype(BF16)
        at = pl.ds(8 * c * BS, 8 * BS)
        outs.append(pltpu.make_async_copy(features.at[:, at], features_hbm.at[:, at], out_sem.at[2 + c]))
        outs[-1].start()
    for out in outs:
        out.wait()
    for trip in d_trips:
        trip.wait()


def layer_call(rows, cols, count, lists, feat, cot, degree, ws, wn, bias, vals):
    dma = pltpu.SemaphoreType.DMA
    V = pltpu.VMEM
    return pl.pallas_call(
        layer_kernel,
        out_shape=(
            jax.ShapeDtypeStruct((HC, ROWS), BF16),
            jax.ShapeDtypeStruct((FC, ROWS), BF16),
            jax.ShapeDtypeStruct((8, SL_A, BS), BF16),
        ),
        in_specs=[anyspace(), anyspace(), smem()] + [anyspace()] * 4 + [vmem()] * 2 + [anyspace()] * 2,
        out_specs=(anyspace(),) * 3,
        scratch_shapes=[
            V((NNZ,), I32),
            V((NNZ,), I32),
            V((2 * HALO,), I32),
            V((HC,), F32),
            V((NB, BS), I32),
            V((NB, 8, BS), F32),
            V((8, BS), I32),
            V((2, 8, BS), I32),
            pltpu.SMEM((2, 8, BS), I32),
            V((8, BS), I32),
            V((2, 8, BS), I32),
            V((16, ENT), I32),
            pltpu.SMEM((16, ENT), I32),
            V((EXT + 1, FC, BS), BF16),
            V((2, HALO, FC, BS), BF16),
            V((NB, HC, BS), BF16),
            V((NNZ + 1, BS, BS), BF16),
            V((PAIRS_B + 1, FC, BS), F32),
            V((2, HALO, FC, BS), BF16),
            V((NB, FC, BS), BF16),
            V((HID, FC), BF16),
            V((HID, FC), BF16),
            V((NB, HID, BS), F32),
            V((3, PIECES, PB, HC, BS), BF16),
            V((3, PIECES, PB, HC, BS), BF16),
            V((PIECES, NF, PB, HC, BS), BF16),
            V((NB, HC, BS), BF16),
            V((NB, FC, BS), BF16),
            V((NB, FC, BS), F32),
            V((HC, ROWS), BF16),
            V((2, HALO + 1, FC, BS), BF16),
            V((FC, ROWS), BF16),
            V((2, FC, HID), F32),
            V((4 * FC, BS), BF16),
            V((8, SL_A, BS), BF16),
            V((4, SL_A, BS), BF16),
            V((SL_A, BS), BF16),
            dma((5,)), dma((NB,)), dma((NB,)), dma((8,)), dma, dma((4,)), dma((4,)), dma((2,)), dma((2,)),
            dma((6, PIECES)), dma((6, PIECES)), dma((2, 4)), dma((2, 4)),
            dma((7,)), dma((7,)), dma((3,)), dma((3,)), dma((7,)), dma((7,)), dma((7,)),
        ],
        compiler_params=pltpu.CompilerParams(collective_id=0, has_side_effects=True, vmem_limit_bytes=60 * MB),
        name="layer",
    )(rows, cols, count, lists, feat, cot, degree, ws, wn, bias, vals)


def results_kernel(
    features_in, hidden_in, grads_hbm, hidden_out, features_out, self_hbm, neigh_hbm,
    features, hidden, grads, weights, in_sems, out_sems,
):
    share = FC // 4
    routes = [(hidden_in, hidden, hidden_out)]
    for c in range(4):
        at = pl.ds(c * share, share)
        routes.append((features_in.at[at], features.at[at], features_out.at[at]))
    grads_load = pltpu.make_async_copy(grads_hbm, grads, in_sems.at[5])
    grads_load.start()
    loads = [pltpu.make_async_copy(src, via, in_sems.at[k]) for k, (src, via, dst) in enumerate(routes)]
    outs = [pltpu.make_async_copy(via, dst, out_sems.at[k]) for k, (src, via, dst) in enumerate(routes)]
    for load in loads:
        load.start()
    grads_load.wait()
    every = grads[...].reshape(4 * FC, BS).astype(F32)
    for k, ref in ((0, self_hbm), (1, neigh_hbm)):
        for c in range(2):
            at = (2 * k + c) * FC
            weights[k, :, c * BS : (c + 1) * BS] = every[at : at + FC]
        outs.append(pltpu.make_async_copy(weights.at[k], ref, out_sems.at[5 + k]))
        outs[-1].start()
    for k in range(5):
        loads[k].wait()
        outs[k].start()
    for out in outs:
        out.wait()


def results_call(features, hidden, grads):
    V = pltpu.VMEM
    return pl.pallas_call(
        results_kernel,
        out_shape=(
            jax.ShapeDtypeStruct((HC, ROWS), BF16),
            jax.ShapeDtypeStruct((FC, ROWS), BF16),
            jax.ShapeDtypeStruct((FC, HID), F32),
            jax.ShapeDtypeStruct((FC, HID), F32),
        ),
        in_specs=[anyspace()] * 3,
        out_specs=(anyspace(),) * 4,
        scratch_shapes=[
            V((FC, ROWS), BF16),
            V((HC, ROWS), BF16),
            V((8, SL_A, BS), BF16),
            V((2, FC, HID), F32),
            pltpu.SemaphoreType.DMA((6,)),
            pltpu.SemaphoreType.DMA((7,)),
        ],
        compiler_params=pltpu.CompilerParams(vmem_limit_bytes=60 * MB),
        name="results",
    )(features, hidden, grads)


def on_device(
    features, w_self, w_neigh, bias_terms, block_vals, block_rows, block_cols, block_count, recv_lists, degree, cotangent
):
    hidden, grad_features, grads = layer_call(
        block_rows, block_cols, block_count, recv_lists, features.T, cotangent.T, degree.reshape(NB, BS),
        w_self, w_neigh, bias_terms, block_vals,
    )
    hidden, grad_features, grad_self, grad_neigh = results_call(grad_features, hidden, grads)
    return hidden.T, grad_features.T, grad_self, grad_neigh


def solution(mesh):
    placed = (
        P("vtx", "feat"), P("feat", None), P("feat", None), P("feat"), P("vtx", None, None), P("vtx"), P("vtx"), P("vtx"),
        P("vtx"), P("vtx"), P("vtx", "feat"),
    )
    return jax.shard_map(
        on_device,
        mesh=mesh,
        in_specs=placed,
        out_specs=(P("vtx", "feat"), P("vtx", "feat"), P("feat", None), P("feat", None)),
        check_vma=False,
    )
```
